32 devices in a mesh: dp: 2 (over core), row: 4 (over y, x), col: 4 (over z).
Axes of the slice: x: 2, y: 2, z: 4, core: 2. Of those that a mesh axis runs over, the one named last changes fastest.
Arguments:
- layer_in: bfloat16 [768, 4096], P(None, ('dp', 'row', 'col')), may hold values from -6 to 6
- lengths: int32 [2], P('dp'), may hold values from 512 to 2048, as said below
- w_attn: bfloat16 [768, 3, 768], P('col', None, 'row'), may hold values from -0.21875 to 0.21875
- b_attn: bfloat16 [2, 768], P(None, 'row'), may hold values from -3 to 3
- w_mixer: bfloat16 [768, 768], P('col', 'row'), may hold values from -6 to 6
- b_mixer: bfloat16 [768], P('col'), may hold values from -3 to 3
- gain_one: bfloat16 [768], P('col'), may hold values from 0.5 to 1.5
- shift_one: bfloat16 [768], P('col'), may hold values from -3 to 3
- w_expand: bfloat16 [768, 3072], P('col', 'row'), may hold values from -0.21875 to 0.21875
- b_expand: bfloat16 [3072], P('row'), may hold values from -3 to 3
- w_reduce: bfloat16 [768, 3072], P('col', 'row'), may hold values from -0.109375 to 0.109375
- b_reduce: bfloat16 [768], P('col'), may hold values from -3 to 3
- gain_two: bfloat16 [768], P('col'), may hold values from 0.5 to 1.5
- shift_two: bfloat16 [768], P('col'), may hold values from -3 to 3
- out_grad: bfloat16 [768, 4096], P(None, ('dp', 'row', 'col')), may hold values from -6 to 6
Outputs:
- layer_out: bfloat16 [768, 4096], P(None, ('dp', 'row', 'col'))
- grad_input: float32 [768, 4096], P(None, ('dp', 'row', 'col'))
- grad_attn: float32 [768, 3, 768], P('col', None, 'row')
- grad_attnbias: float32 [2, 768], P(None, 'row')
- grad_mixer: float32 [768, 768], P('col', 'row')
- grad_mixerbias: float32 [768], P('col')
- grad_gainone: float32 [768], P('col')
- grad_shiftone: float32 [768], P('col')
- grad_expand: float32 [768, 3072], P('col', 'row')
- grad_expandbias: float32 [3072], P('row')
- grad_reduce: float32 [768, 3072], P('col', 'row')
- grad_reducebias: float32 [768], P('col')
- grad_gaintwo: float32 [768], P('col')
- grad_shifttwo: float32 [768], P('col')
The draws below stay inside these ranges and needn't reach their ends.
Inputs may be any that keep to these rules, and one draw needn't show every extreme that they name: lengths[s] slots of sequence s are valid, the rest are padding; some sequence fills all 2048 slots.
All inputs are finite; a program needn't handle non-finite values.
Results may differ from the reference program's by a relative error of at most 0.018.
Values may be sent and summed in bfloat16 or wider, within the bound.
A program may use at most 448 MiB of HBM per device.

```python
import jax
import jax.numpy as jnp
from jax import lax

D = 768
H = 12
FF = 3072
HD = 64
SEQ = 2048
SEQS = 2
TOKENS = 4096


def draw_lengths(key, part):
    picks = jax.random.randint(key, (SEQS,), SEQ // 4, SEQ + 1)
    full_at = jax.random.randint(jax.random.fold_in(key, 7), (), 0, SEQS)
    return jnp.where(jnp.arange(SEQS) == full_at, SEQ, picks).astype(jnp.int32)


def level_of(key, shape, cuts, low, top_value):
    level = 1.0
    for axis_at, blocks in cuts:
        heights = jax.random.uniform(jax.random.fold_in(jax.random.fold_in(key, 6), axis_at), (blocks,), jnp.float32, low / len(cuts), top_value / len(cuts))
        level = level * jnp.repeat(jnp.exp(heights), shape[axis_at] // blocks).reshape((-1,) + (1,) * (len(shape) - 1 - axis_at))
    return level


def scatter_about(key, shape, scale, most, pieces=(), held_as=jnp.bfloat16):
    entries = scale * jax.random.normal(key, shape, jnp.float32)
    if pieces:
        entries = entries * level_of(key, shape, pieces, -0.22, 0.18)
    return jnp.clip(entries, -most, most).astype(held_as)


def setup_inputs(seed: int = 0) -> dict:
    keys = jax.random.split(jax.random.key(seed), 16)
    layer_in = scatter_about(keys[0], (D, TOKENS), 1.0, 6.0, ((1, 32),))
    lengths = draw_lengths(jax.random.fold_in(keys[15], 71), 0)
    w_attn = scatter_about(keys[2], (D, 3, D), D ** -0.5, 0.21875, ((0, 4), (2, 4)))
    b_attn = scatter_about(keys[3], (2, D), 0.5, 3.0, ((1, 4),))
    w_mixer = scatter_about(keys[4], (D, D), ((4 * D) ** -0.5 * SEQ ** 0.5), 6.0, ((0, 4), (1, 4)))
    b_mixer = scatter_about(keys[5], (D,), 0.3, 3.0, ((0, 4),))
    gain_one = jnp.clip(1.0 + 0.1 * jax.random.normal(keys[6], (D,), jnp.float32), 0.5, 1.5).astype(jnp.bfloat16)
    shift_one = scatter_about(keys[7], (D,), 0.3, 3.0, ((0, 4),))
    w_expand = scatter_about(keys[8], (D, FF), D ** -0.5, 0.21875, ((0, 4), (1, 4)))
    b_expand = scatter_about(keys[9], (FF,), 0.3, 3.0, ((0, 4),))
    w_reduce = scatter_about(keys[10], (D, FF), FF ** -0.5, 0.109375, ((0, 4), (1, 4)))
    b_reduce = scatter_about(keys[11], (D,), 0.3, 3.0, ((0, 4),))
    gain_two = jnp.clip(1.0 + 0.1 * jax.random.normal(keys[12], (D,), jnp.float32), 0.5, 1.5).astype(jnp.bfloat16)
    shift_two = scatter_about(keys[13], (D,), 0.3, 3.0, ((0, 4),))
    out_grad = scatter_about(keys[14], (D, TOKENS), 1.0, 6.0, ((1, 32),))
    return dict(layer_in=layer_in, lengths=lengths, w_attn=w_attn, b_attn=b_attn, w_mixer=w_mixer, b_mixer=b_mixer, gain_one=gain_one, shift_one=shift_one, w_expand=w_expand, b_expand=b_expand, w_reduce=w_reduce, b_reduce=b_reduce, gain_two=gain_two, shift_two=shift_two, out_grad=out_grad)


EPSILON = 1e-12
NEGATIVE = -1000000000.0
HIGH = lax.Precision.HIGHEST

@jax.custom_vjp
def low(v):
    return lax.optimization_barrier(v.astype(jnp.bfloat16)).astype(jnp.float32)

@jax.custom_vjp
def low_back(v):
    return v

def low_keep(v):
    return (low(v), None)

def low_pass(kept, grad):
    return (grad,)

def back_keep(v):
    return (v, None)

def back_low(kept, grad):
    return (low(grad),)
low.defvjp(low_keep, low_pass)
low_back.defvjp(back_keep, back_low)

def matmul(left_in, right_in):
    return jnp.dot(left_in, right_in, precision=HIGH, preferred_element_type=jnp.float32)

def normalize(values, gain_vec, shift_vec):
    row_mean = lax.optimization_barrier(jnp.mean(values, -1, keepdims=True))
    centered = values - row_mean
    row_var = lax.optimization_barrier(jnp.mean(centered * centered, -1, keepdims=True))
    return centered * lax.rsqrt(row_var + EPSILON) * gain_vec + shift_vec

def attend_block(query_block, keys_seq, values_seq, key_valid):
    raw_scores = jnp.einsum('qhd,khd->hqk', query_block, keys_seq, precision=HIGH) * HD ** (-0.5)
    scores = jnp.where(key_valid[None, None, :], low_back(raw_scores), NEGATIVE)
    top_score = lax.optimization_barrier(jnp.max(scores, 2, keepdims=True))
    exp_scores = jnp.exp(scores - top_score)
    weights = low(exp_scores / lax.optimization_barrier(jnp.sum(exp_scores, 2, keepdims=True)))
    return jnp.einsum('hqk,khd->qhd', weights, values_seq, precision=HIGH)

def attend_sequence(block_items):
    queries, keys_seq, values_seq, length = block_items
    key_valid = jnp.arange(SEQ) < length
    block_rows = min(512, SEQ)
    grouped = queries.reshape(SEQ // block_rows, block_rows, H, HD)

    def block_fn(query_block):
        return attend_block(query_block, keys_seq, values_seq, key_valid)
    return lax.map(jax.checkpoint(block_fn), grouped).reshape(SEQ, H * HD)

def to_heads(array_in):
    return array_in.reshape(SEQS, SEQ, H, HD)

def forward(params, lengths):
    layer_in_t, w_attn, b_attn, w_mixer, b_mixer, gain_one, shift_one, w_expand, b_expand, w_reduce, b_reduce, gain_two, shift_two = params
    layer_in = layer_in_t.T
    projected = matmul(layer_in, w_attn.reshape(D, 3 * D)).reshape(TOKENS, 3, D)
    queries = low_back(low(projected[:, 0] + b_attn[0]))
    keys_in = low_back(low(projected[:, 1]))
    values_in = low_back(low(projected[:, 2] + b_attn[1]))
    context = lax.map(attend_sequence, (to_heads(queries), to_heads(keys_in), to_heads(values_in), lengths))
    context = low_back(low(context.reshape(TOKENS, D)))
    mixed = low_back(matmul(context, w_mixer.T) + b_mixer)
    hidden = normalize(layer_in + mixed, gain_one, shift_one)
    inner = low_back(matmul(low(hidden), w_expand) + b_expand)
    active = low_back(low(jax.nn.gelu(inner, approximate=False)))
    reduced = low_back(matmul(active, w_reduce.T) + b_reduce)
    output = normalize(hidden + reduced, gain_two, shift_two)
    valid = (jnp.arange(SEQ)[None, :] < lengths[:, None]).reshape(TOKENS, 1).astype(jnp.float32)
    return (output * valid).T

def reference(layer_in, lengths, w_attn, b_attn, w_mixer, b_mixer, gain_one, shift_one, w_expand, b_expand, w_reduce, b_reduce, gain_two, shift_two, out_grad):
    params = tuple((item.astype(jnp.float32) for item in (layer_in, w_attn, b_attn, w_mixer, b_mixer, gain_one, shift_one, w_expand, b_expand, w_reduce, b_reduce, gain_two, shift_two)))

    def forward_fn(*inputs):
        return forward(inputs, lengths)
    output, pull_back = jax.vjp(forward_fn, *params)
    gradients = pull_back(out_grad.astype(jnp.float32))
    return (output.astype(jnp.bfloat16), gradients[0], gradients[1], gradients[2], gradients[3], gradients[4], gradients[5], gradients[6], gradients[7], gradients[8], gradients[9], gradients[10], gradients[11], gradients[12])
```

```python
import functools
from types import SimpleNamespace

import jax
import jax.numpy as jnp
from jax import lax
from jax.experimental import pallas as pl
from jax.experimental.pallas import tpu as pltpu
from jax.sharding import PartitionSpec as P

D = 768
H = 12
EPSILON = 1e-12
NEGATIVE = -1000000000.0
MESH = pl.DeviceIdType.MESH
F32 = jnp.float32
BF16 = jnp.bfloat16


def dot_nn(left_in, right_in):
    return lax.dot_general(
        left_in, right_in, (((1,), (0,)), ((), ())), preferred_element_type=F32
    )


def dot_nt(left_in, right_in):
    return lax.dot_general(
        left_in, right_in, (((1,), (1,)), ((), ())), preferred_element_type=F32
    )


def turned(values):
    return values.astype(F32).T


def normalize(values):
    row_mean = jnp.mean(values, 1, keepdims=True)
    centered = values - row_mean
    row_var = jnp.mean(centered * centered, 1, keepdims=True)
    row_scale = lax.rsqrt(row_var + EPSILON)
    return centered * row_scale, row_scale


def normalize_back(upstream, normed, row_scale, gain_vec):
    scaled = upstream * gain_vec
    mean_plain = jnp.mean(scaled, 1, keepdims=True)
    mean_cross = jnp.mean(scaled * normed, 1, keepdims=True)
    return row_scale * (scaled - mean_plain - normed * mean_cross)


def column_sum(values):
    return jnp.sum(values, 0, keepdims=True)


class Slots:
    def __init__(self):
        self.base = {}
        self.total = 0

    def add(self, name, count):
        self.base[name] = self.total
        self.total += count


def slots_of(R, C):
    slots = Slots()
    for name in ("x", "mix", "hid", "red", "gr", "gh", "gm", "dx", "gv_row"):
        slots.add(name, R)
    for name in ("vec", "gv_col", "ab_col", "kv_right", "kv_left", "dkv_right", "dkv_left"):
        slots.add(name, C)
    for name in ("w1", "w2", "w3"):
        slots.add(name, C)
        slots.add(name + "_dp", C)
        slots.add("d" + name, C)
        slots.add("d" + name + "_dp", 1)
        slots.add("d" + name + "_out", 1)
    for name in ("gv_dp", "ab_dp"):
        slots.add(name, 1)
    return slots


def layer_kernel(dims, names, *refs):
    e = SimpleNamespace(**dict(zip(names, refs)))
    R, C, T, S, F, U, RB = dims.R, dims.C, dims.T, dims.S, dims.F, dims.U, dims.RB
    NH, HS, N1 = dims.NH, dims.HS, dims.N1
    slots = slots_of(R, C)
    me_d = lax.axis_index("dp")
    me_r = lax.axis_index("row")
    me_c = lax.axis_index("col")

    def to_row(step):
        return {"row": lax.rem(me_r + step, R)}

    def to_col(step):
        return {"col": lax.rem(me_c + step, C)}

    partner = {"dp": 1 - me_d}

    def copy(src, dst, family, at, where):
        number = slots.base[family] + at
        return pltpu.make_async_remote_copy(
            src_ref=src,
            dst_ref=dst,
            send_sem=e.send_sems.at[number],
            recv_sem=e.recv_sems.at[number],
            device_id=where,
            device_id_type=MESH,
        )

    barrier = pltpu.get_barrier_semaphore()
    pl.semaphore_signal(barrier, inc=1, device_id=partner, device_id_type=MESH)
    for i in range(1, R):
        pl.semaphore_signal(barrier, inc=1, device_id=to_row(i), device_id_type=MESH)
    for i in range(1, C):
        pl.semaphore_signal(barrier, inc=1, device_id=to_col(i), device_id_type=MESH)
    e.xg[me_r] = turned(e.x_t[...]).astype(BF16)
    pl.semaphore_wait(barrier, 1 + (R - 1) + (C - 1))

    def w_slot(ref, c):
        if dims.flat:
            return ref.at[pl.ds(pl.multiple_of(c * RB, RB), RB)]
        return ref.at[c]

    def half_of(width, d):
        return pl.ds(pl.multiple_of(d * (width // 2), width // 2), width // 2)

    def weight_copy(name, own, full, width, i):
        mine = half_of(width, me_d)
        return copy(own.at[:, mine], w_slot(full, me_c).at[:, mine], name, i, to_col(i))

    def weight_pass(name, full, width, i):
        mine = half_of(width, me_d)
        there = w_slot(full, lax.rem(me_c - i + C, C)).at[:, mine]
        return copy(there, there, name + "_dp", i, partner)

    def weight_start(name, own, full, width):
        for i in range(1, C):
            weight_copy(name, own, full, width, i).start()
        w_slot(full, me_c)[...] = own[...]

    def weight_share(name, own, full, width):
        for i in range(1, C):
            weight_copy(name, own, full, width, i).wait_recv()
            weight_pass(name, full, width, i).start()

    def weight_end(name, own, full, flat, width):
        for i in range(1, C):
            weight_pass(name, full, width, i).wait_recv()
        if not dims.flat:
            flat[...] = full[...].astype(F32).reshape(C * RB, width).astype(BF16)

    def weight_close(name, own, full, width):
        for i in range(1, C):
            weight_copy(name, own, full, width, i).wait_send()
            weight_pass(name, full, width, i).wait_send()

    w1 = ("w1", e.w1, e.w1g, N1)
    w2 = ("w2", e.w2, e.w2g, U)
    w3 = ("w3", e.w3, e.w3g, U)
    w1f = e.w1g if dims.flat else e.w1f
    w2f = e.w2g if dims.flat else e.w2f
    w3f = e.w3g if dims.flat else e.w3f

    def x_copy(i):
        return copy(e.xg.at[me_r], e.xg.at[me_r], "x", i, to_row(i))

    def vec_copy(i):
        return copy(e.vec, e.vecr.at[i], "vec", i, to_col(i))

    for i in range(1, R):
        x_copy(i).start()
    weight_start(*w1)
    for i in range(1, C):
        vec_copy(i).start()
    length = e.length[0]

    weight_share(*w1)
    weight_end("w1", e.w1, e.w1g, w1f, N1)

    def project(i):
        rb = lax.rem(me_r - i + R, R)
        if i:
            x_copy(i).wait_recv()
        tokens = pl.ds(pl.multiple_of(rb * T, T), T)
        block = e.xg[rb]
        proj = dot_nn(block, w1f[:, : 3 * F])
        q = (proj[:, :F] + e.b_attn[0:1, :]).astype(BF16).astype(F32) * (HS ** (-0.5))
        k = proj[:, F : 2 * F]
        v = proj[:, 2 * F :] + e.b_attn[1:2, :]
        e.kv[me_c, pl.ds(0, F), tokens] = k.T.astype(BF16)
        e.kv[me_c, pl.ds(F, F), tokens] = v.T.astype(BF16)
        e.q_t[:, tokens] = q.T.astype(BF16)
        for h in range(NH):
            e.q_h[h, tokens, :] = q[:, h * HS : (h + 1) * HS].astype(BF16)
        e.x_rows_t[:, tokens] = turned(block).astype(BF16)

    for i in range(R):
        project(i)

    right = {"col": lax.rem(me_c + 1, C)}
    left = {"col": lax.rem(me_c + C - 1, C)}

    def kv_right(b):
        return copy(e.kv.at[b], e.kv.at[b], "kv_right", b, right)

    def kv_left(b):
        return copy(e.kv.at[b], e.kv.at[b], "kv_left", b, left)

    def key_valid(b):
        lane = lax.broadcasted_iota(jnp.int32, (1, S), 1)
        return (lane // T * (T * C) + b * T + lane % T) < length

    TQ = dims.TQ
    e.top[...] = jnp.full(e.top.shape, -3e38, F32)
    e.total[...] = jnp.zeros(e.total.shape, F32)
    e.acc[...] = jnp.zeros(e.acc.shape, F32)

    def attend(b):
        valid = key_valid(b)

        def tile(t, carry):
            rows = pl.ds(pl.multiple_of(t * TQ, TQ), TQ)
            for h in range(NH):
                keys = e.kv[b, h * HS : (h + 1) * HS, :]
                values = e.kv[b, F + h * HS : F + (h + 1) * HS, :]
                scores = dot_nn(e.q_h[h, rows, :], keys)
                scores = jnp.where(valid, scores, NEGATIVE)
                old = e.top[h, rows, :]
                new = jnp.maximum(old, jnp.max(scores, 1, keepdims=True))
                shrink = jnp.exp(old - new)
                probs = jnp.exp(scores - new)
                e.top[h, rows, :] = new
                e.total[h, rows, :] = shrink * e.total[h, rows, :] + jnp.sum(
                    probs, 1, keepdims=True
                )
                e.acc[h, rows, :] = shrink * e.acc[h, rows, :] + dot_nt(
                    probs.astype(BF16), values
                )
            return carry

        lax.fori_loop(0, S // TQ, tile, 0)

    @pl.when(me_c < C - 1)
    def _():
        kv_right(me_c).start()

    @pl.when(me_c > 0)
    def _():
        kv_left(me_c).start()

    attend(me_c)

    def kv_step(s, carry):
        from_left = me_c - s
        from_right = me_c + s

        @pl.when(from_left >= 0)
        def _():
            kv_right(from_left).wait_recv()

            @pl.when(me_c < C - 1)
            def _():
                kv_right(from_left).start()

        @pl.when(from_right < C)
        def _():
            kv_left(from_right).wait_recv()

            @pl.when(me_c > 0)
            def _():
                kv_left(from_right).start()

        @pl.when(from_left >= 0)
        def _():
            attend(from_left)

        @pl.when(from_right < C)
        def _():
            attend(from_right)

        return carry

    lax.fori_loop(1, C, kv_step, 0)

    def kv_close(b, carry):
        @pl.when((b <= me_c) & (me_c < C - 1))
        def _():
            kv_right(b).wait_send()

        @pl.when((b >= me_c) & (me_c > 0))
        def _():
            kv_left(b).wait_send()

        return carry

    lax.fori_loop(0, C, kv_close, 0)
    weight_start(*w2)
    weight_start(*w3)

    for h in range(NH):
        inverse = 1.0 / e.total[h]
        e.total[h] = inverse
        context = e.acc[h] * inverse
        e.acc[h] = context
        e.ctx[:, h * HS : (h + 1) * HS] = context.astype(BF16)

    vec = e.vec[...]
    for i in range(1, C):
        vec_copy(i).wait_recv()
        vec = vec + e.vecr[i]
    e.vecs[...] = vec

    def vector(at):
        return e.vecs[at : at + 1, :]

    def blk_rows(rb):
        return pl.ds(pl.multiple_of(rb * T, T), T)

    def sum_copy(family, i, where):
        return copy(e.stage.at[i], e.landing.at[slots.base[family] // R, i], family, i, where)

    for i in list(range(1, R)) + [0]:
        rb = lax.rem(me_r + i, R)
        part = dot_nt(e.ctx[blk_rows(rb), :], w1f[:, 3 * F :])
        if i:
            e.stage[0, i] = part.astype(BF16)
            copy(e.stage.at[0, i], e.landing.at[0, i], "mix", i, to_row(i)).start()
        else:
            e.own[...] = part

    def collect(number, family):
        total = e.own[...]
        for i in range(1, R):
            copy(e.stage.at[number, i], e.landing.at[number, i], family, i, to_row(i)).wait_recv()
            total = total + e.landing[number, i].astype(F32)
        return total

    first_sum = turned(e.x_t[...]) + collect(0, "mix") + vector(0)
    normed, scale = normalize(first_sum)
    hidden = normed * vector(1) + vector(2)
    e.n1[...] = normed
    e.r1[...] = scale
    e.hidden[...] = hidden
    e.hid_g[me_r] = hidden.astype(BF16)

    def share(ref, family, i):
        return copy(ref.at[me_r], ref.at[me_r], family, i, to_row(i))

    for i in range(1, R):
        share(e.hid_g, "hid", i).start()
    weight_share(*w2)
    weight_end("w2", e.w2, e.w2g, w2f, U)

    def spread(number, family, part, i, rb):
        if i:
            e.stage[number, i] = part.astype(BF16)
            copy(
                e.stage.at[number, i], e.landing.at[number, i], family, i, to_row(R - i)
            ).start()
        else:
            e.own[...] = part

    for i in range(R):
        rb = lax.rem(me_r - i + R, R)
        if i:
            share(e.hid_g, "hid", i).wait_recv()
        inner = dot_nn(e.hid_g[rb], w2f[...]) + e.b_expand[...]
        cdf = 0.5 * (1.0 + lax.erf(inner * (0.5**0.5)))
        active = (inner * cdf).astype(BF16)
        slope = cdf + inner * (jnp.exp(-0.5 * inner * inner) * 0.3989422804014327)
        e.active[blk_rows(rb), :] = active
        e.slope[blk_rows(rb), :] = slope
        if i == 0:
            weight_share(*w3)
            weight_end("w3", e.w3, e.w3g, w3f, U)
        spread(1, "red", dot_nt(e.active[blk_rows(rb), :], w3f[...]), i, rb)
    for i in range(R):
        rb = lax.rem(me_r - i + R, R)
        e.hid_t[:, blk_rows(rb)] = turned(e.hid_g[rb]).astype(BF16)

    second_sum = e.hidden[...] + collect(1, "red") + vector(3)
    normed, scale = normalize(second_sum)
    slot = lax.broadcasted_iota(jnp.int32, (T, 1), 0) + (me_r * (T * C) + me_c * T)
    row_valid = (slot < length).astype(F32)
    upstream = turned(e.out_grad[...]) * row_valid
    g_second = normalize_back(upstream, normed, scale, vector(4))
    g_reduced = g_second.astype(BF16)
    e.gr_g[me_r] = g_reduced
    for i in range(1, R):
        share(e.gr_g, "gr", i).start()
    e.layer_out[...] = ((normed * vector(4) + vector(5)) * row_valid).T.astype(BF16)
    e.g_second[...] = g_second
    e.gv[4:5, :] = column_sum(upstream * normed)
    e.gv[5:6, :] = column_sum(upstream)
    e.gv[3:4, :] = column_sum(g_reduced.astype(F32))
    e.gv[7:8, :] = jnp.zeros((1, D), F32)

    unit_sum = jnp.zeros((1, U), F32)
    for i in range(R):
        rb = lax.rem(me_r - i + R, R)
        if i:
            share(e.gr_g, "gr", i).wait_recv()
        g_active = dot_nn(e.gr_g[rb], w3f[...]).astype(BF16).astype(F32)
        g_inner = (g_active * e.slope[blk_rows(rb), :]).astype(BF16)
        e.g_inner[blk_rows(rb), :] = g_inner
        unit_sum = unit_sum + column_sum(g_inner.astype(F32))
        spread(2, "gh", dot_nt(e.g_inner[blk_rows(rb), :], w2f[...]), i, rb)
    e.gu[0:1, :] = unit_sum
    for i in range(R):
        rb = lax.rem(me_r - i + R, R)
        e.gr_t[:, blk_rows(rb)] = turned(e.gr_g[rb]).astype(BF16)

    TR = dims.TR

    def other_copy(name, k):
        return copy(e.dw_out.at[k], e.dw_in.at[k], name + "_dp", 0, partner)

    def weight_product(k, lhs_ref, rhs_of, transposed):
        product = dot_nt if transposed else dot_nn

        def tile(t, carry):
            rows = pl.ds(pl.multiple_of(t * TR, TR), TR)
            lhs = lhs_ref[rows, :]
            e.dw_out[k, rows, :] = product(lhs, rhs_of(1 - me_d)).astype(BF16)
            return carry

        def own_tile(t, carry):
            rows = pl.ds(pl.multiple_of(t * TR, TR), TR)
            lhs = lhs_ref[rows, :]
            e.dw_own[rows, :] = product(lhs, rhs_of(me_d))
            return carry

        return tile, own_tile

    def d_copy(name, k, i):
        return copy(e.dw_stage.at[k, lax.rem(me_c + i, C)], e.dw_land.at[k, i], name, i, to_col(i))

    def weight_grad(name, k, lhs_ref, rhs_of, transposed):
        tile, own_tile = weight_product(k, lhs_ref, rhs_of, transposed)
        lax.fori_loop(0, D // TR, tile, 0)
        other_copy(name, k).start()
        lax.fori_loop(0, D // TR, own_tile, 0)
        other_copy(name, k).wait_recv()

    def weight_send(name, k):
        if dims.flat:
            for c in range(C):
                rows = slice(c * RB, (c + 1) * RB)
                total = e.dw_own[rows, :] + e.dw_in[k, rows, :].astype(F32)
                e.dw_stage[k, c] = total.astype(BF16)
        else:
            total = e.dw_own[...] + e.dw_in[k].astype(F32)
            e.dw_stage[k] = total.reshape(C, RB, N1 // 2).astype(BF16)
        for i in range(1, C):
            d_copy(name, k, i).start()

    def result_copy(name, k):
        mine = half_of(N1, me_d)
        return copy(e.dw.at[k, :, mine], e.dw.at[k, :, mine], name + "_out", 0, partner)

    def weight_collect(name, k):
        total = e.dw_stage[k, me_c].astype(F32)
        for i in range(1, C):
            d_copy(name, k, i).wait_recv()
            total = total + e.dw_land[k, i].astype(F32)
        e.dw[k, :, half_of(N1, me_d)] = total
        result_copy(name, k).start()

    weight_grad(
        "dw3", 2, e.gr_t, lambda d: e.active[:, half_of(U, d)], False
    )
    weight_send("dw3", 2)
    weight_grad(
        "dw2", 1, e.hid_t, lambda d: e.g_inner[:, half_of(U, d)], False
    )
    weight_send("dw2", 1)

    g_hidden = collect(2, "gh") + e.g_second[...]
    normed = e.n1[...]
    g_first = normalize_back(g_hidden, normed, e.r1[...], vector(1))
    g_mixed = g_first.astype(BF16)
    for i in range(1, R):
        share(e.hid_g, "hid", i).wait_send()
    e.hid_g[me_r] = g_mixed
    for i in range(1, R):
        share(e.hid_g, "gm", i).start()
    e.g_first[...] = g_first
    e.gv[1:2, :] = column_sum(g_hidden * normed)
    e.gv[2:3, :] = column_sum(g_hidden)
    e.gv[0:1, :] = column_sum(g_mixed.astype(F32))
    e.gv[6:7, :] = jnp.zeros((1, D), F32)

    def gv_dp():
        return copy(e.gall.at[0], e.gall.at[1], "gv_dp", 0, partner)

    e.gall[0, 0:8, :D] = e.gv[...]
    e.gall[0, 8:16, :U] = jnp.broadcast_to(e.gu[0:1, :], (8, U))
    gv_dp().start()

    for i in range(R):
        rb = lax.rem(me_r - i + R, R)
        if i:
            share(e.hid_g, "gm", i).wait_recv()
        rows = blk_rows(rb)
        g_context = dot_nn(e.hid_g[rb], w1f[:, 3 * F :]).astype(BF16).astype(F32)
        e.gc_t[:, rows] = g_context.T.astype(BF16)
        for h in range(NH):
            part = g_context[:, h * HS : (h + 1) * HS]
            e.gc_h[h, rows, :] = part.astype(BF16)
            e.inner_sum[h, rows, :] = jnp.sum(part * e.acc[h, rows, :], 1, keepdims=True)
        e.gr_t[:, rows] = turned(e.hid_g[rb]).astype(BF16)

    gv_dp().wait_recv()
    e.gall[2] = e.gall[0] + e.gall[1]

    def gv_col(i):
        return copy(e.gall.at[2], e.gcol.at[i], "gv_col", i, to_col(i))

    for i in range(1, C):
        gv_col(i).start()

    e.dq[...] = jnp.zeros(e.dq.shape, F32)

    def attend_back(b):
        valid = key_valid(b)
        for h in range(NH):
            krows = slice(h * HS, (h + 1) * HS)
            vrows = slice(F + h * HS, F + (h + 1) * HS)

            def tile(t, carry):
                d_keys, d_values = carry
                rows = pl.ds(pl.multiple_of(t * TQ, TQ), TQ)
                keys = e.kv[b, krows, :]
                values = e.kv[b, vrows, :]
                scores = dot_nn(e.q_h[h, rows, :], keys)
                scores = jnp.where(valid, scores, NEGATIVE)
                probs = jnp.exp(scores - e.top[h, rows, :]) * e.total[h, rows, :]
                g_weights = dot_nn(e.gc_h[h, rows, :], values)
                g_scores = (probs * (g_weights - e.inner_sum[h, rows, :])).astype(BF16)
                e.dq[h, rows, :] += dot_nt(g_scores, keys)
                d_keys = d_keys + dot_nn(e.q_t[krows, rows], g_scores)
                d_values = d_values + dot_nn(e.gc_t[krows, rows], probs.astype(BF16))
                return d_keys, d_values

            zero = jnp.zeros((HS, S), F32)
            d_keys, d_values = lax.fori_loop(0, S // TQ, tile, (zero, zero))
            e.dkv[krows, :] = d_keys
            e.dkv[vrows, :] = d_values

    NB = dims.NB

    def dkv_right(b):
        return copy(
            e.kv.at[b], e.dkv_in.at[0, lax.rem(C - 1 - b, NB)], "dkv_right", b, right
        )

    def dkv_left(b):
        return copy(e.kv.at[b], e.dkv_in.at[1, lax.rem(b, NB)], "dkv_left", b, left)

    def dkv_send(way, b):
        order = C - 1 - b if way == 0 else b
        if C - 1 > NB:

            @pl.when(order >= NB)
            def _():
                pl.semaphore_wait(e.credits.at[way], 1)

        (dkv_right if way == 0 else dkv_left)(b).start()

    def dkv_take(way, b):
        order = C - 1 - b if way == 0 else b
        (dkv_right if way == 0 else dkv_left)(b).wait_recv()
        e.dkv[...] += e.dkv_in[way, lax.rem(order, NB)].astype(F32)
        if C - 1 > NB:
            sends = C - me_c if way == 0 else me_c + 1

            @pl.when(order + NB < sends)
            def _():
                pl.semaphore_signal(
                    e.credits.at[way],
                    inc=1,
                    device_id=left if way == 0 else right,
                    device_id_type=MESH,
                )

    def dkv_step(s, carry):
        far_right = C - 1 - s
        far_left = s

        @pl.when(far_right > me_c)
        def _():
            attend_back(far_right)

            @pl.when(me_c > 0)
            def _():
                dkv_take(0, far_right)

            e.kv[far_right] = e.dkv[...].astype(BF16)
            dkv_send(0, far_right)

        @pl.when(far_left < me_c)
        def _():
            attend_back(far_left)

            @pl.when(me_c < C - 1)
            def _():
                dkv_take(1, far_left)

            e.kv[far_left] = e.dkv[...].astype(BF16)
            dkv_send(1, far_left)

        return carry

    lax.fori_loop(0, C - 1, dkv_step, 0)
    attend_back(me_c)

    for h in range(NH):
        e.dqkv[h * HS : (h + 1) * HS, :] = (e.dq[h] * (HS ** (-0.5))).T.astype(BF16)

    for i in range(1, C):
        gv_col(i).wait_recv()
    gsum = e.gall[2]
    for i in range(1, C):
        gsum = gsum + e.gcol[i]
    e.gsum[...] = gsum

    def gv_row(i):
        return copy(e.gsum.at[pl.ds(0, 8)], e.grow.at[i], "gv_row", i, to_row(i))

    for i in range(1, R):
        gv_row(i).start()

    @pl.when(me_c > 0)
    def _():
        dkv_take(0, me_c)

    @pl.when(me_c < C - 1)
    def _():
        dkv_take(1, me_c)

    e.dqkv[F : 3 * F, :] = e.dkv[...].astype(BF16)

    for i in list(range(1, R)) + [0]:
        rb = lax.rem(me_r + i, R)
        part = dot_nn(w1f[:, : 3 * F], e.dqkv[:, blk_rows(rb)])
        if i:
            e.dx_stage[i] = part.astype(BF16)
            copy(e.dx_stage.at[i], e.dx_land.at[i], "dx", i, to_row(i)).start()
        else:
            e.dx_own[...] = part

    def packed_tile(t, carry):
        rows = pl.ds(pl.multiple_of(t * TR, TR), TR)
        e.dw1[rows, : 3 * F] = dot_nt(e.x_rows_t[rows, :], e.dqkv[...])
        e.dw1[rows, 3 * F :] = dot_nn(e.gr_t[rows, :], e.ctx[...])
        return carry

    lax.fori_loop(0, D // TR, packed_tile, 0)
    e.dw_out[0] = e.dw1[:, half_of(N1, 1 - me_d)].astype(BF16)
    other_copy("dw1", 0).start()
    sums = dot_nt(jnp.ones((8, S), BF16), e.dqkv[...])
    e.ab[0] = sums

    def ab_dp():
        return copy(e.ab.at[0], e.ab.at[1], "ab_dp", 0, partner)

    def ab_col(i):
        return copy(e.ab.at[2], e.abcol.at[i], "ab_col", i, to_col(i))

    ab_dp().start()
    e.dw_own[...] = e.dw1[:, half_of(N1, me_d)]
    other_copy("dw1", 0).wait_recv()
    weight_send("dw1", 0)
    ab_dp().wait_recv()
    e.ab[2] = e.ab[0] + e.ab[1]
    for i in range(1, C):
        ab_col(i).start()

    weight_collect("dw3", 2)
    weight_collect("dw2", 1)

    total = e.dx_own[...] + e.g_first[...].T
    for i in range(1, R):
        copy(e.dx_stage.at[i], e.dx_land.at[i], "dx", i, to_row(i)).wait_recv()
        total = total + e.dx_land[i].astype(F32)
    e.grad_input[...] = total

    vsum = e.gsum[0:8, :D]
    for i in range(1, R):
        gv_row(i).wait_recv()
        vsum = vsum + e.grow[i][:, :D]
    e.gvec[...] = vsum
    e.gunit[...] = e.gsum[8:16, :U]
    asum = e.ab[2]
    for i in range(1, C):
        ab_col(i).wait_recv()
        asum = asum + e.abcol[i]
    e.gab[...] = asum
    weight_collect("dw1", 0)
    for name, k in (("dw3", 2), ("dw2", 1), ("dw1", 0)):
        result_copy(name, k).wait_recv()

    weight_close(*w1)
    weight_close(*w2)
    weight_close(*w3)
    for i in range(1, R):
        x_copy(i).wait_send()
        copy(e.stage.at[0, i], e.landing.at[0, i], "mix", i, to_row(i)).wait_send()
        copy(e.stage.at[1, i], e.landing.at[1, i], "red", i, to_row(i)).wait_send()
        share(e.gr_g, "gr", i).wait_send()
        copy(e.stage.at[2, i], e.landing.at[2, i], "gh", i, to_row(i)).wait_send()
        share(e.hid_g, "gm", i).wait_send()
        copy(e.dx_stage.at[i], e.dx_land.at[i], "dx", i, to_row(i)).wait_send()
        gv_row(i).wait_send()
    gv_dp().wait_send()
    ab_dp().wait_send()
    for i in range(1, C):
        vec_copy(i).wait_send()
        gv_col(i).wait_send()
        ab_col(i).wait_send()
    for name, k in (("dw3", 2), ("dw2", 1), ("dw1", 0)):
        other_copy(name, k).wait_send()
        for i in range(1, C):
            d_copy(name, k, i).wait_send()
        result_copy(name, k).wait_send()

    def dkv_close(s, carry):
        @pl.when(C - 1 - s > me_c)
        def _():
            dkv_right(C - 1 - s).wait_send()

        @pl.when(s < me_c)
        def _():
            dkv_left(s).wait_send()

        return carry

    lax.fori_loop(0, C - 1, dkv_close, 0)


def run_layer(x_t, length, w1, w2, w3, vec, b_attn, b_expand, out_grad):
    R = lax.axis_size("row")
    C = lax.axis_size("col")
    T = x_t.shape[1]
    S = T * R
    F = b_attn.shape[1]
    U = w2.shape[1]
    RB = w1.shape[0]
    HS = D // H
    dims = SimpleNamespace(
        R=R, C=C, T=T, S=S, F=F, U=U, RB=RB, HS=HS, NH=F // HS, N1=4 * F,
        flat=RB % 16 == 0, TQ=min(256, S), TR=256, NB=min(C, 4),
    )
    N1 = dims.N1
    NH = dims.NH
    slots = slots_of(R, C)
    wide = max(D, U)
    w_shape = (lambda n: (C * RB, n)) if dims.flat else (lambda n: (C, RB, n))
    inputs = dict(
        x_t=x_t, length=length, w1=w1, w2=w2, w3=w3, vec=vec, b_attn=b_attn,
        b_expand=b_expand, out_grad=out_grad,
    )
    outputs = dict(
        layer_out=((D, T), BF16),
        grad_input=((D, T), F32),
        dw=((3, RB, N1), F32),
        gvec=((8, D), F32),
        gunit=((8, U), F32),
        gab=((8, 3 * F), F32),
    )
    scratch = dict(
        xg=((R, T, D), BF16),
        w1g=(w_shape(N1), BF16),
        w2g=(w_shape(U), BF16),
        w3g=(w_shape(U), BF16),
        vecr=((C, 8, D), F32),
        vecs=((8, D), F32),
        kv=((C, 2 * F, S), BF16),
        q_t=((F, S), BF16),
        q_h=((NH, S, HS), BF16),
        x_rows_t=((D, S), BF16),
        top=((NH, S, 1), F32),
        total=((NH, S, 1), F32),
        acc=((NH, S, HS), F32),
        ctx=((S, F), BF16),
        stage=((3, R, T, D), BF16),
        landing=((3, R, T, D), BF16),
        own=((T, D), F32),
        n1=((T, D), F32),
        r1=((T, 1), F32),
        hidden=((T, D), F32),
        hid_g=((R, T, D), BF16),
        active=((S, U), BF16),
        slope=((S, U), F32),
        hid_t=((D, S), BF16),
        g_second=((T, D), F32),
        gr_g=((R, T, D), BF16),
        gr_t=((D, S), BF16),
        g_inner=((S, U), BF16),
        gv=((8, D), F32),
        gu=((8, U), F32),
        gall=((3, 16, wide), F32),
        gcol=((C, 16, wide), F32),
        gsum=((16, wide), F32),
        grow=((R, 8, wide), F32),
        dw_out=((3, D, N1 // 2), BF16),
        dw_in=((3, D, N1 // 2), BF16),
        dw_own=((D, N1 // 2), F32),
        dw_stage=((3, C, RB, N1 // 2), BF16),
        dw_land=((3, C, RB, N1 // 2), BF16),
        dw1=((D, N1), F32),
        g_first=((T, D), F32),
        gc_t=((F, S), BF16),
        gc_h=((NH, S, HS), BF16),
        inner_sum=((NH, S, 1), F32),
        dq=((NH, S, HS), F32),
        dkv=((2 * F, S), F32),
        dkv_in=((2, dims.NB, 2 * F, S), BF16),
        dqkv=((3 * F, S), BF16),
        dx_stage=((R, D, T), BF16),
        dx_land=((R, D, T), BF16),
        dx_own=((D, T), F32),
        ab=((3, 8, 3 * F), F32),
        abcol=((C, 8, 3 * F), F32),
    )
    if not dims.flat:
        scratch.update(
            w1f=((C * RB, N1), BF16), w2f=((C * RB, U), BF16), w3f=((C * RB, U), BF16)
        )
    names = list(inputs) + list(outputs) + list(scratch) + ["send_sems", "recv_sems", "credits"]
    vmem = pl.BlockSpec(memory_space=pltpu.VMEM)
    in_specs = [
        pl.BlockSpec(memory_space=pltpu.SMEM) if name == "length" else vmem for name in inputs
    ]
    results = pl.pallas_call(
        functools.partial(layer_kernel, dims, names),
        out_shape=[jax.ShapeDtypeStruct(s, t) for s, t in outputs.values()],
        in_specs=in_specs,
        out_specs=[vmem] * len(outputs),
        scratch_shapes=[pltpu.VMEM(s, t) for s, t in scratch.values()]
        + [pltpu.SemaphoreType.DMA((slots.total,)), pltpu.SemaphoreType.DMA((slots.total,))]
        + [pltpu.SemaphoreType.REGULAR((2,))],
        compiler_params=pltpu.CompilerParams(
            collective_id=0, has_side_effects=True, vmem_limit_bytes=63 * 2**20
        ),
        name="layer",
    )(*inputs.values())
    return dict(zip(outputs, results))


def on_device(
    layer_in,
    lengths,
    w_attn,
    b_attn,
    w_mixer,
    b_mixer,
    gain_one,
    shift_one,
    w_expand,
    b_expand,
    w_reduce,
    b_reduce,
    gain_two,
    shift_two,
    out_grad,
):
    col_index = lax.axis_index("col")
    rows = w_mixer.shape[0]
    feats = w_mixer.shape[1]
    w1 = jnp.concatenate([w_attn.reshape(rows, 3 * feats), w_mixer], 1)
    own = jnp.stack([b_mixer, gain_one, shift_one, b_reduce, gain_two, shift_two]).astype(F32)
    vec = lax.dynamic_update_slice(jnp.zeros((8, D), F32), own, (0, col_index * rows))
    out = run_layer(
        layer_in,
        lengths,
        w1,
        w_expand,
        w_reduce,
        vec,
        b_attn.astype(F32),
        b_expand.astype(F32)[None],
        out_grad,
    )
    gvec = lax.dynamic_slice(out["gvec"], (0, col_index * rows), (8, rows))
    dw1 = out["dw"][0]
    gab = out["gab"]
    return (
        out["layer_out"],
        out["grad_input"],
        dw1[:, : 3 * feats].reshape(rows, 3, feats),
        jnp.stack([gab[0, :feats], gab[0, 2 * feats :]]),
        dw1[:, 3 * feats :],
        gvec[0],
        gvec[1],
        gvec[2],
        out["dw"][1],
        out["gunit"][0],
        out["dw"][2],
        gvec[3],
        gvec[4],
        gvec[5],
    )


def solution(mesh):
    return jax.shard_map(
        on_device,
        mesh=mesh,
        in_specs=(
            P(None, ("dp", "row", "col")),
            P("dp"),
            P("col", None, "row"),
            P(None, "row"),
            P("col", "row"),
            P("col"),
            P("col"),
            P("col"),
            P("col", "row"),
            P("row"),
            P("col", "row"),
            P("col"),
            P("col"),
            P("col"),
            P(None, ("dp", "row", "col")),
        ),
        out_specs=(
            P(None, ("dp", "row", "col")),
            P(None, ("dp", "row", "col")),
            P("col", None, "row"),
            P(None, "row"),
            P("col", "row"),
            P("col"),
            P("col"),
            P("col"),
            P("col", "row"),
            P("row"),
            P("col", "row"),
            P("col"),
            P("col"),
            P("col"),
        ),
        check_vma=False,
    )
```

```python
import functools
from types import SimpleNamespace

import jax
import jax.numpy as jnp
from jax import lax
from jax.experimental import pallas as pl
from jax.experimental.pallas import tpu as pltpu
from jax.sharding import PartitionSpec as P

D = 768
H = 12
EPSILON = 1e-12
NEGATIVE = -1000000000.0
MESH = pl.DeviceIdType.MESH
F32 = jnp.float32
BF16 = jnp.bfloat16


def dot_nn(left_in, right_in):
    return lax.dot_general(
        left_in, right_in, (((1,), (0,)), ((), ())), preferred_element_type=F32
    )


def dot_nt(left_in, right_in):
    return lax.dot_general(
        left_in, right_in, (((1,), (1,)), ((), ())), preferred_element_type=F32
    )


def turned(values):
    return values.astype(F32).T


def normalize(values):
    row_mean = jnp.mean(values, 1, keepdims=True)
    centered = values - row_mean
    row_var = jnp.mean(centered * centered, 1, keepdims=True)
    row_scale = lax.rsqrt(row_var + EPSILON)
    return centered * row_scale, row_scale


def normalize_back(upstream, normed, row_scale, gain_vec):
    scaled = upstream * gain_vec
    mean_plain = jnp.mean(scaled, 1, keepdims=True)
    mean_cross = jnp.mean(scaled * normed, 1, keepdims=True)
    return row_scale * (scaled - mean_plain - normed * mean_cross)


def column_sum(values):
    return jnp.sum(values, 0, keepdims=True)


class Slots:
    def __init__(self):
        self.base = {}
        self.total = 0

    def add(self, name, count):
        self.base[name] = self.total
        self.total += count


def slots_of(R, C):
    slots = Slots()
    for name in ("x", "mix", "hid", "red", "gr", "gh", "gm", "dx", "gv_row"):
        slots.add(name, R)
    for name in ("vec", "gv_col", "ab_col", "kv_right", "kv_left", "dkv_right", "dkv_left"):
        slots.add(name, C)
    for name in ("wkv", "wqm", "w2", "w3"):
        slots.add(name, C)
        slots.add(name + "_dp", C)
        slots.add("d" + name, C)
        slots.add("d" + name + "_dp", 1)
        slots.add("d" + name + "_out", 1)
    for name in ("gv_dp", "ab_dp"):
        slots.add(name, 1)
    return slots


def layer_kernel(dims, names, *refs):
    e = SimpleNamespace(**dict(zip(names, refs)))
    R, C, T, S, F, U, RB = dims.R, dims.C, dims.T, dims.S, dims.F, dims.U, dims.RB
    NH, HS, HB = dims.NH, dims.HS, dims.HB
    slots = slots_of(R, C)
    me_d = lax.axis_index("dp")
    me_r = lax.axis_index("row")
    me_c = lax.axis_index("col")

    def to_row(step):
        return {"row": lax.rem(me_r + step, R)}

    def to_col(step):
        return {"col": lax.rem(me_c + step, C)}

    partner = {"dp": 1 - me_d}

    def copy(src, dst, family, at, where):
        number = slots.base[family] + at
        return pltpu.make_async_remote_copy(
            src_ref=src,
            dst_ref=dst,
            send_sem=e.send_sems.at[number],
            recv_sem=e.recv_sems.at[number],
            device_id=where,
            device_id_type=MESH,
        )

    barrier = pltpu.get_barrier_semaphore()
    pl.semaphore_signal(barrier, inc=1, device_id=partner, device_id_type=MESH)
    for i in range(1, R):
        pl.semaphore_signal(barrier, inc=1, device_id=to_row(i), device_id_type=MESH)
    for i in range(1, C):
        pl.semaphore_signal(barrier, inc=1, device_id=to_col(i), device_id_type=MESH)
    e.xg[me_r] = turned(e.x_t[...]).astype(BF16)
    e.wkv[:, :F] = e.w_attn[1]
    e.wkv[:, F:] = e.w_attn[2]
    e.wqm[:, :F] = e.w_attn[0]
    e.wqm[:, F:] = e.w_mixer[...]
    e.vecr[me_c] = e.small[0:8, :]
    pl.semaphore_wait(barrier, 1 + (R - 1) + (C - 1))

    def w_rows(ref, c, d):
        if not dims.flat:
            return ref.at[c]
        return ref.at[pl.ds(pl.multiple_of(c * RB + d * HB, HB), HB)]

    def weight_copy(name, i):
        own = getattr(e, name)
        if dims.flat:
            own = own.at[pl.ds(pl.multiple_of(me_d * HB, HB), HB)]
        return copy(own, w_rows(getattr(e, name + "_g"), me_c, me_d), name, i, to_col(i))

    def weight_pass(name, i):
        there = w_rows(getattr(e, name + "_g"), lax.rem(me_c - i + C, C), me_d)
        return copy(there, there, name + "_dp", i, partner)

    def weight_start(name, which=None):
        for i in range(1, C):
            if which is None:
                weight_copy(name, i).start()
            else:
                to = lax.rem(me_c + i, C)
                inner = (to > 0) & (to < C - 1)
                pl.when(inner if which == "inner" else jnp.logical_not(inner))(
                    weight_copy(name, i).start
                )

    def weight_own(name):
        full = getattr(e, name + "_g")
        if dims.flat:
            full[pl.ds(pl.multiple_of(me_c * RB, RB), RB), :] = getattr(e, name)[...]
        else:
            full[me_c] = getattr(e, name)[...]

    def weight_share(name):
        for i in range(1, C):
            weight_copy(name, i).wait_recv()
            if dims.flat:
                weight_pass(name, i).start()

    def weight_end(name):
        if dims.flat:
            for i in range(1, C):
                weight_pass(name, i).wait_recv()
        else:
            full = getattr(e, name + "_g")
            flat = full[...].astype(F32).reshape(C * RB, full.shape[2])
            getattr(e, name + "_f")[...] = flat.astype(BF16)

    def weight_close(name):
        for i in range(1, C):
            weight_copy(name, i).wait_send()
            if dims.flat:
                weight_pass(name, i).wait_send()

    wkv, wqm, w2f, w3f = [
        getattr(e, name + ("_g" if dims.flat else "_f")) for name in ("wkv", "wqm", "w2", "w3")
    ]

    def x_copy(i):
        return copy(e.xg.at[me_r], e.xg.at[me_r], "x", i, to_row(i))

    def vec_copy(i):
        return copy(e.vecr.at[me_c], e.vecr.at[me_c], "vec", i, to_col(i))

    for i in range(1, R):
        x_copy(i).start()
    weight_start("wkv")
    length = e.length[0]
    for name in ("wkv", "wqm", "w2", "w3"):
        weight_own(name)

    weight_share("wkv")
    weight_start("wqm")
    for i in range(1, C):
        vec_copy(i).start()
    weight_end("wkv")

    for i in range(R):
        rb = lax.rem(me_r - i + R, R)
        if i:
            x_copy(i).wait_recv()
        tokens = pl.ds(pl.multiple_of(rb * T, T), T)
        both = dot_nn(e.xg[rb], wkv[...])
        values = both[:, F:] + e.small[7:8, :]
        e.kv[me_c, pl.ds(0, F), tokens] = both[:, :F].T.astype(BF16)
        e.kv[me_c, pl.ds(F, F), tokens] = values.T.astype(BF16)

    def make_queries():
        weight_share("wqm")
        weight_end("wqm")
        e.mix[...] = wqm[:, F:]
        for i in range(R):
            tokens = pl.ds(i * T, T)
            block = e.xg[i]
            q = dot_nn(block, wqm[:, :F]) + e.small[6:7, :]
            q = q.astype(BF16).astype(F32) * (HS ** (-0.5))
            e.q_t[:, tokens] = q.T.astype(BF16)
            for h in range(NH):
                e.q_h[h, tokens, :] = q[:, h * HS : (h + 1) * HS].astype(BF16)
            e.x_rows_t[:, tokens] = turned(block).astype(BF16)

    right = {"col": lax.rem(me_c + 1, C)}
    left = {"col": lax.rem(me_c + C - 1, C)}

    def kv_right(b):
        return copy(e.kv.at[b], e.kv.at[b], "kv_right", b, right)

    def kv_left(b):
        return copy(e.kv.at[b], e.kv.at[b], "kv_left", b, left)

    def key_valid(b):
        lane = lax.broadcasted_iota(jnp.int32, (1, S), 1)
        return (lane // T * (T * C) + b * T + lane % T) < length

    TQ = dims.TQ
    e.top[...] = jnp.full(e.top.shape, -3e38, F32)
    e.total[...] = jnp.zeros(e.total.shape, F32)
    e.acc[...] = jnp.zeros(e.acc.shape, F32)

    def attend(b):
        valid = key_valid(b)

        def tile(t, carry):
            rows = pl.ds(pl.multiple_of(t * TQ, TQ), TQ)
            for h in range(NH):
                keys = e.kv[b, h * HS : (h + 1) * HS, :]
                values = e.kv[b, F + h * HS : F + (h + 1) * HS, :]
                scores = dot_nn(e.q_h[h, rows, :], keys)
                scores = jnp.where(valid, scores, NEGATIVE)
                old = e.top[h, rows, :]
                new = jnp.maximum(old, jnp.max(scores, 1, keepdims=True))
                shrink = jnp.exp(old - new)
                probs = jnp.exp(scores - new)
                e.top[h, rows, :] = new
                e.total[h, rows, :] = shrink * e.total[h, rows, :] + jnp.sum(
                    probs, 1, keepdims=True
                )
                e.acc[h, rows, :] = shrink * e.acc[h, rows, :] + dot_nt(
                    probs.astype(BF16), values
                )
            return carry

        lax.fori_loop(0, S // TQ, tile, 0)

    @pl.when(me_c < C - 1)
    def _():
        kv_right(me_c).start()

    @pl.when(me_c > 0)
    def _():
        kv_left(me_c).start()

    make_queries()
    attend(me_c)

    def kv_step(s, carry):
        from_left = me_c - s
        from_right = me_c + s

        @pl.when(from_left >= 0)
        def _():
            kv_right(from_left).wait_recv()

            @pl.when(me_c < C - 1)
            def _():
                kv_right(from_left).start()

        @pl.when(from_right < C)
        def _():
            kv_left(from_right).wait_recv()

            @pl.when(me_c > 0)
            def _():
                kv_left(from_right).start()

        @pl.when(s == min(2, C - 1))
        def _():
            weight_start("w2", "inner")
            weight_start("w3", "inner")

        @pl.when(from_left >= 0)
        def _():
            attend(from_left)

        @pl.when(from_right < C)
        def _():
            attend(from_right)

        return carry

    lax.fori_loop(1, C, kv_step, 0)

    def kv_close(b, carry):
        @pl.when((b <= me_c) & (me_c < C - 1))
        def _():
            kv_right(b).wait_send()

        @pl.when((b >= me_c) & (me_c > 0))
        def _():
            kv_left(b).wait_send()

        return carry

    lax.fori_loop(0, C, kv_close, 0)
    weight_start("w2", "outer")
    weight_start("w3", "outer")

    for h in range(NH):
        inverse = 1.0 / e.total[h]
        e.total[h] = inverse
        context = e.acc[h] * inverse
        e.acc[h] = context
        e.ctx[:, h * HS : (h + 1) * HS] = context.astype(BF16)

    for i in range(1, C):
        vec_copy(i).wait_recv()
    for c in range(C):
        e.vecs[:, c * RB : (c + 1) * RB] = e.vecr[c][:, :RB]
    for k in range(U // F):
        e.bias[:, k * F : (k + 1) * F] = e.small[8 + k : 9 + k, :]

    def vector(at):
        return e.vecs[at : at + 1, :]

    def blk_rows(rb):
        return pl.ds(pl.multiple_of(rb * T, T), T)

    for i in list(range(1, R)) + [0]:
        rb = lax.rem(me_r + i, R)
        part = dot_nt(e.ctx[blk_rows(rb), :], e.mix[...])
        if i:
            e.stage[0, i] = part.astype(BF16)
            copy(e.stage.at[0, i], e.landing.at[0, i], "mix", i, to_row(i)).start()
        else:
            e.own[...] = part

    def collect(number, family):
        total = e.own[...]
        for i in range(1, R):
            copy(e.stage.at[number, i], e.landing.at[number, i], family, i, to_row(i)).wait_recv()
            total = total + e.landing[number, i].astype(F32)
        return total

    first_sum = turned(e.x_t[...]) + collect(0, "mix") + vector(0)
    normed, scale = normalize(first_sum)
    hidden = normed * vector(1) + vector(2)
    e.n1[...] = normed
    e.r1[...] = scale
    e.hidden[...] = hidden
    e.hid_g[me_r] = hidden.astype(BF16)

    def share(ref, family, i):
        return copy(ref.at[me_r], ref.at[me_r], family, i, to_row(i))

    for i in range(1, R):
        share(e.hid_g, "hid", i).start()
    weight_share("w2")
    weight_end("w2")

    def spread(number, family, part, i, rb):
        if i:
            e.stage[number, i] = part.astype(BF16)
            copy(
                e.stage.at[number, i], e.landing.at[number, i], family, i, to_row(R - i)
            ).start()
        else:
            e.own[...] = part

    for i in range(R):
        rb = lax.rem(me_r - i + R, R)
        if i:
            share(e.hid_g, "hid", i).wait_recv()
        inner = dot_nn(e.hid_g[rb], w2f[...]) + e.bias[...]
        cdf = 0.5 * (1.0 + lax.erf(inner * (0.5**0.5)))
        active = (inner * cdf).astype(BF16)
        slope = cdf + inner * (jnp.exp(-0.5 * inner * inner) * 0.3989422804014327)
        e.active[blk_rows(rb), :] = active
        e.slope[blk_rows(rb), :] = slope
        if i == 0:
            weight_share("w3")
            weight_end("w3")
        spread(1, "red", dot_nt(e.active[blk_rows(rb), :], w3f[...]), i, rb)
    for i in range(R):
        rb = lax.rem(me_r - i + R, R)
        e.hid_t[:, blk_rows(rb)] = turned(e.hid_g[rb]).astype(BF16)

    second_sum = e.hidden[...] + collect(1, "red") + vector(3)
    normed, scale = normalize(second_sum)
    slot = lax.broadcasted_iota(jnp.int32, (T, 1), 0) + (me_r * (T * C) + me_c * T)
    row_valid = (slot < length).astype(F32)
    upstream = turned(e.out_grad[...]) * row_valid
    g_second = normalize_back(upstream, normed, scale, vector(4))
    g_reduced = g_second.astype(BF16)
    e.gr_g[me_r] = g_reduced
    for i in range(1, R):
        share(e.gr_g, "gr", i).start()
    e.layer_out[...] = ((normed * vector(4) + vector(5)) * row_valid).T.astype(BF16)
    e.g_second[...] = g_second
    e.gv[4:5, :] = column_sum(upstream * normed)
    e.gv[5:6, :] = column_sum(upstream)
    e.gv[3:4, :] = column_sum(g_reduced.astype(F32))
    e.gv[7:8, :] = jnp.zeros((1, D), F32)

    unit_sum = jnp.zeros((1, U), F32)
    for i in range(R):
        rb = lax.rem(me_r - i + R, R)
        if i:
            share(e.gr_g, "gr", i).wait_recv()
        g_active = dot_nn(e.gr_g[rb], w3f[...]).astype(BF16).astype(F32)
        g_inner = (g_active * e.slope[blk_rows(rb), :]).astype(BF16)
        e.g_inner[blk_rows(rb), :] = g_inner
        unit_sum = unit_sum + column_sum(g_inner.astype(F32))
        spread(2, "gh", dot_nt(e.g_inner[blk_rows(rb), :], w2f[...]), i, rb)
    e.gu[0:1, :] = unit_sum
    for i in range(R):
        rb = lax.rem(me_r - i + R, R)
        e.gr_t[:, blk_rows(rb)] = turned(e.gr_g[rb]).astype(BF16)

    TR = dims.TR

    def half_rows(c, d):
        if not dims.flat:
            return pl.ds(c * RB, RB)
        return pl.ds(pl.multiple_of(c * RB + d * HB, HB), HB)

    def other_copy(name):
        return copy(getattr(e, name + "_out"), getattr(e, name + "_in"), name + "_dp", 0, partner)

    def d_copy(name, i):
        stage = getattr(e, name + "_in").at[lax.rem(me_c + i, C)]
        return copy(stage, getattr(e, name + "_land").at[i], name, i, to_col(i))

    def row_tiles(fill):
        def tile(t, carry):
            fill(pl.ds(pl.multiple_of(t * TR, TR), TR))
            return carry

        lax.fori_loop(0, D // TR, tile, 0)

    def weight_swap(name, source):
        def block(c, carry):
            getattr(e, name + "_out")[c] = source[half_rows(c, 1 - me_d), :].astype(BF16)
            return carry

        lax.fori_loop(0, C, block, 0)
        other_copy(name).start()

    def weight_send(name, source):
        other_copy(name).wait_recv()

        def block(c, carry):
            total = source[half_rows(c, me_d), :] + getattr(e, name + "_in")[c].astype(F32)
            getattr(e, name + "_in")[c] = total.astype(BF16)
            return carry

        lax.fori_loop(0, C, block, 0)
        for i in range(1, C):
            d_copy(name, i).start()

    def result_part(name):
        full = getattr(e, name + "_sum")
        return full.at[pl.ds(pl.multiple_of(me_d * HB, HB), HB)] if dims.flat else full

    def result_copy(name):
        return copy(result_part(name), result_part(name), name + "_out", 0, partner)

    def weight_collect(name):
        total = getattr(e, name + "_in")[me_c].astype(F32)
        for i in range(1, C):
            d_copy(name, i).wait_recv()
            total = total + getattr(e, name + "_land")[i].astype(F32)
        result_part(name)[...] = total
        if dims.flat:
            result_copy(name).start()

    def fill_reduce(rows):
        e.dw_f[rows, :] = dot_nn(e.gr_t[rows, :], e.active[...])

    def fill_expand(rows):
        e.dw_f[rows, :] = dot_nn(e.hid_t[rows, :], e.g_inner[...])

    row_tiles(fill_reduce)
    weight_swap("dw3", e.dw_f)
    weight_send("dw3", e.dw_f)
    row_tiles(fill_expand)
    weight_swap("dw2", e.dw_f)
    weight_send("dw2", e.dw_f)

    g_hidden = collect(2, "gh") + e.g_second[...]
    normed = e.n1[...]
    g_first = normalize_back(g_hidden, normed, e.r1[...], vector(1))
    g_mixed = g_first.astype(BF16)
    for i in range(1, R):
        share(e.hid_g, "hid", i).wait_send()
    e.hid_g[me_r] = g_mixed
    for i in range(1, R):
        share(e.hid_g, "gm", i).start()
    e.g_first[...] = g_first
    e.gv[1:2, :] = column_sum(g_hidden * normed)
    e.gv[2:3, :] = column_sum(g_hidden)
    e.gv[0:1, :] = column_sum(g_mixed.astype(F32))
    e.gv[6:7, :] = jnp.zeros((1, D), F32)

    def gv_dp():
        return copy(e.gall.at[0], e.gall.at[1], "gv_dp", 0, partner)

    e.gall[0, 0:8, :D] = e.gv[...]
    e.gall[0, 8:16, :U] = jnp.broadcast_to(e.gu[0:1, :], (8, U))
    gv_dp().start()

    for i in range(R):
        rb = lax.rem(me_r - i + R, R)
        if i:
            share(e.hid_g, "gm", i).wait_recv()
        rows = blk_rows(rb)
        g_context = dot_nn(e.hid_g[rb], e.mix[...]).astype(BF16).astype(F32)
        e.gc_t[:, rows] = g_context.T.astype(BF16)
        for h in range(NH):
            part = g_context[:, h * HS : (h + 1) * HS]
            e.gc_h[h, rows, :] = part.astype(BF16)
            e.inner_sum[h, rows, :] = jnp.sum(part * e.acc[h, rows, :], 1, keepdims=True)
        e.gr_t[:, rows] = turned(e.hid_g[rb]).astype(BF16)

    gv_dp().wait_recv()
    e.gall[2] = e.gall[0] + e.gall[1]

    def gv_col(i):
        return copy(e.gall.at[2], e.gcol.at[i], "gv_col", i, to_col(i))

    for i in range(1, C):
        gv_col(i).start()

    e.dq[...] = jnp.zeros(e.dq.shape, F32)

    def attend_back(b):
        valid = key_valid(b)
        for h in range(NH):
            krows = slice(h * HS, (h + 1) * HS)
            vrows = slice(F + h * HS, F + (h + 1) * HS)

            def tile(t, carry):
                d_keys, d_values = carry
                rows = pl.ds(pl.multiple_of(t * TQ, TQ), TQ)
                keys = e.kv[b, krows, :]
                values = e.kv[b, vrows, :]
                scores = dot_nn(e.q_h[h, rows, :], keys)
                scores = jnp.where(valid, scores, NEGATIVE)
                probs = jnp.exp(scores - e.top[h, rows, :]) * e.total[h, rows, :]
                g_weights = dot_nn(e.gc_h[h, rows, :], values)
                g_scores = (probs * (g_weights - e.inner_sum[h, rows, :])).astype(BF16)
                e.dq[h, rows, :] += dot_nt(g_scores, keys)
                d_keys = d_keys + dot_nn(e.q_t[krows, rows], g_scores)
                d_values = d_values + dot_nn(e.gc_t[krows, rows], probs.astype(BF16))
                return d_keys, d_values

            zero = jnp.zeros((HS, S), F32)
            d_keys, d_values = lax.fori_loop(0, S // TQ, tile, (zero, zero))
            e.dkv[krows, :] = d_keys
            e.dkv[vrows, :] = d_values

    NB = dims.NB

    def dkv_right(b):
        return copy(
            e.kv.at[b], e.dkv_in.at[0, lax.rem(C - 1 - b, NB)], "dkv_right", b, right
        )

    def dkv_left(b):
        return copy(e.kv.at[b], e.dkv_in.at[1, lax.rem(b, NB)], "dkv_left", b, left)

    def dkv_send(way, b):
        order = C - 1 - b if way == 0 else b
        if C - 1 > NB:

            @pl.when(order >= NB)
            def _():
                pl.semaphore_wait(e.credits.at[way], 1)

        (dkv_right if way == 0 else dkv_left)(b).start()

    def dkv_take(way, b):
        order = C - 1 - b if way == 0 else b
        (dkv_right if way == 0 else dkv_left)(b).wait_recv()
        e.dkv[...] += e.dkv_in[way, lax.rem(order, NB)].astype(F32)
        if C - 1 > NB:
            sends = C - me_c if way == 0 else me_c + 1

            @pl.when(order + NB < sends)
            def _():
                pl.semaphore_signal(
                    e.credits.at[way],
                    inc=1,
                    device_id=left if way == 0 else right,
                    device_id_type=MESH,
                )

    def dkv_step(s, carry):
        far_right = C - 1 - s
        far_left = s

        @pl.when(far_right > me_c)
        def _():
            attend_back(far_right)

            @pl.when(me_c > 0)
            def _():
                dkv_take(0, far_right)

            e.kv[far_right] = e.dkv[...].astype(BF16)
            dkv_send(0, far_right)

        @pl.when(far_left < me_c)
        def _():
            attend_back(far_left)

            @pl.when(me_c < C - 1)
            def _():
                dkv_take(1, far_left)

            e.kv[far_left] = e.dkv[...].astype(BF16)
            dkv_send(1, far_left)

        return carry

    lax.fori_loop(0, C - 1, dkv_step, 0)
    attend_back(me_c)

    for h in range(NH):
        e.dqkv[h * HS : (h + 1) * HS, :] = (e.dq[h] * (HS ** (-0.5))).T.astype(BF16)

    def fill_query(rows):
        e.dw_s[rows, :F] = dot_nt(e.x_rows_t[rows, :], e.dqkv[:F, :])
        e.dw_s[rows, F:] = dot_nn(e.gr_t[rows, :], e.ctx[...])

    row_tiles(fill_query)
    weight_swap("dwqm", e.dw_s)
    weight_send("dwqm", e.dw_s)
    weight_collect("dw3")
    weight_collect("dw2")

    for i in range(1, C):
        gv_col(i).wait_recv()
    gsum = e.gall[2]
    for i in range(1, C):
        gsum = gsum + e.gcol[i]
    e.gsum[...] = gsum

    def gv_row(i):
        return copy(e.gsum.at[pl.ds(0, 8)], e.grow.at[i], "gv_row", i, to_row(i))

    for i in range(1, R):
        gv_row(i).start()

    @pl.when(me_c > 0)
    def _():
        dkv_take(0, me_c)

    @pl.when(me_c < C - 1)
    def _():
        dkv_take(1, me_c)

    e.dqkv[F : 3 * F, :] = e.dkv[...].astype(BF16)

    for i in list(range(1, R)) + [0]:
        rb = lax.rem(me_r + i, R)
        part = dot_nn(wqm[:, :F], e.dqkv[:F, blk_rows(rb)]) + dot_nn(
            wkv[...], e.dqkv[F:, blk_rows(rb)]
        )
        if i:
            e.dx_stage[i] = part.astype(BF16)
            copy(e.dx_stage.at[i], e.dx_land.at[i], "dx", i, to_row(i)).start()
        else:
            e.dx_own[...] = part

    def fill_keys(rows):
        e.dw_s[rows, :] = dot_nt(e.x_rows_t[rows, :], e.dqkv[F:, :])

    row_tiles(fill_keys)
    weight_swap("dwkv", e.dw_s)
    e.ab[0] = dot_nt(jnp.ones((8, S), BF16), e.dqkv[...])

    def ab_dp():
        return copy(e.ab.at[0], e.ab.at[1], "ab_dp", 0, partner)

    def ab_col(i):
        return copy(e.ab.at[2], e.abcol.at[i], "ab_col", i, to_col(i))

    ab_dp().start()
    weight_send("dwkv", e.dw_s)
    ab_dp().wait_recv()
    e.ab[2] = e.ab[0] + e.ab[1]
    for i in range(1, C):
        ab_col(i).start()

    weight_collect("dwqm")

    total = e.dx_own[...] + e.g_first[...].T
    for i in range(1, R):
        copy(e.dx_stage.at[i], e.dx_land.at[i], "dx", i, to_row(i)).wait_recv()
        total = total + e.dx_land[i].astype(F32)
    e.grad_input[...] = total

    vsum = e.gsum[0:8, :D]
    for i in range(1, R):
        gv_row(i).wait_recv()
        vsum = vsum + e.grow[i][:, :D]
    mine = vsum[:, :RB]
    for c in range(1, C):
        mine = jnp.where(me_c == c, vsum[:, c * RB : (c + 1) * RB], mine)
    e.g_vec[...] = mine
    e.g_unit[...] = e.gsum[8:9, :U]
    asum = e.ab[2]
    for i in range(1, C):
        ab_col(i).wait_recv()
        asum = asum + e.abcol[i]
    e.g_ab[0:1, :] = asum[0:1, :F]
    e.g_ab[1:2, :] = asum[0:1, 2 * F :]
    weight_collect("dwkv")
    if dims.flat:
        for name in ("dw3", "dw2", "dwqm", "dwkv"):
            result_copy(name).wait_recv()
    e.g_attn[0] = e.dwqm_sum[:, :F]
    e.g_mix[...] = e.dwqm_sum[:, F:]
    e.g_attn[1] = e.dwkv_sum[:, :F]
    e.g_attn[2] = e.dwkv_sum[:, F:]

    for name in ("wkv", "wqm", "w2", "w3"):
        weight_close(name)
    for i in range(1, R):
        x_copy(i).wait_send()
        copy(e.stage.at[0, i], e.landing.at[0, i], "mix", i, to_row(i)).wait_send()
        copy(e.stage.at[1, i], e.landing.at[1, i], "red", i, to_row(i)).wait_send()
        share(e.gr_g, "gr", i).wait_send()
        copy(e.stage.at[2, i], e.landing.at[2, i], "gh", i, to_row(i)).wait_send()
        share(e.hid_g, "gm", i).wait_send()
        copy(e.dx_stage.at[i], e.dx_land.at[i], "dx", i, to_row(i)).wait_send()
        gv_row(i).wait_send()
    gv_dp().wait_send()
    ab_dp().wait_send()
    for i in range(1, C):
        vec_copy(i).wait_send()
        gv_col(i).wait_send()
        ab_col(i).wait_send()
    for name in ("dw3", "dw2", "dwqm", "dwkv"):
        other_copy(name).wait_send()
        for i in range(1, C):
            d_copy(name, i).wait_send()
        if dims.flat:
            result_copy(name).wait_send()

    def dkv_close(s, carry):
        @pl.when(C - 1 - s > me_c)
        def _():
            dkv_right(C - 1 - s).wait_send()

        @pl.when(s < me_c)
        def _():
            dkv_left(s).wait_send()

        return carry

    lax.fori_loop(0, C - 1, dkv_close, 0)


def run_layer(x_t, length, w_attn, w_mixer, w2, w3, small, out_grad):
    R = lax.axis_size("row")
    C = lax.axis_size("col")
    T = x_t.shape[1]
    S = T * R
    F = w_mixer.shape[1]
    U = w2.shape[1]
    RB = w_mixer.shape[0]
    flat = RB % 32 == 0
    HS = D // H
    dims = SimpleNamespace(
        R=R, C=C, T=T, S=S, F=F, U=U, RB=RB, HS=HS, NH=F // HS,
        flat=flat, HB=RB // 2 if flat else RB, TQ=min(256, S), TR=256, NB=min(C - 1, 3),
    )
    HB = dims.HB
    NH = dims.NH
    slots = slots_of(R, C)
    wide = max(D, U)
    w_shape = (lambda n: (C * RB, n)) if dims.flat else (lambda n: (C, RB, n))
    inputs = dict(
        x_t=x_t, length=length, w_attn=w_attn, w_mixer=w_mixer, w2=w2, w3=w3, small=small,
        out_grad=out_grad,
    )
    outputs = dict(
        layer_out=((D, T), BF16),
        grad_input=((D, T), F32),
        g_attn=((3, RB, F), F32),
        g_mix=((RB, F), F32),
        dw2_sum=((RB, U), F32),
        dw3_sum=((RB, U), F32),
        g_vec=((8, RB), F32),
        g_unit=((1, U), F32),
        g_ab=((2, F), F32),
    )
    scratch = dict(
        xg=((R, T, D), BF16),
        wkv=((RB, 2 * F), BF16),
        wqm=((RB, 2 * F), BF16),
        wkv_g=(w_shape(2 * F), BF16),
        wqm_g=(w_shape(2 * F), BF16),
        w2_g=(w_shape(U), BF16),
        w3_g=(w_shape(U), BF16),
        mix=((D, F), BF16),
        vecr=((C, 8, F), F32),
        vecs=((8, D), F32),
        bias=((1, U), F32),
        kv=((C, 2 * F, S), BF16),
        q_t=((F, S), BF16),
        q_h=((NH, S, HS), BF16),
        x_rows_t=((D, S), BF16),
        top=((NH, S, 1), F32),
        total=((NH, S, 1), F32),
        acc=((NH, S, HS), F32),
        ctx=((S, F), BF16),
        stage=((3, R, T, D), BF16),
        landing=((3, R, T, D), BF16),
        own=((T, D), F32),
        n1=((T, D), F32),
        r1=((T, 1), F32),
        hidden=((T, D), F32),
        hid_g=((R, T, D), BF16),
        active=((S, U), BF16),
        slope=((S, U), F32),
        hid_t=((D, S), BF16),
        g_second=((T, D), F32),
        gr_g=((R, T, D), BF16),
        gr_t=((D, S), BF16),
        g_inner=((S, U), BF16),
        gv=((8, D), F32),
        gu=((8, U), F32),
        gall=((3, 16, wide), F32),
        gcol=((C, 16, wide), F32),
        gsum=((16, wide), F32),
        grow=((R, 8, wide), F32),
        dw_f=((D, U), F32),
        dw_s=((D, 2 * F), F32),
        dwqm_sum=((RB, 2 * F), F32),
        dwkv_sum=((RB, 2 * F), F32),
        g_first=((T, D), F32),
        gc_t=((F, S), BF16),
        gc_h=((NH, S, HS), BF16),
        inner_sum=((NH, S, 1), F32),
        dq=((NH, S, HS), F32),
        dkv=((2 * F, S), F32),
        dkv_in=((2, dims.NB, 2 * F, S), BF16),
        dqkv=((3 * F, S), BF16),
        dx_stage=((R, D, T), BF16),
        dx_land=((R, D, T), BF16),
        dx_own=((D, T), F32),
        ab=((3, 8, 3 * F), F32),
        abcol=((C, 8, 3 * F), F32),
    )
    for name, width in (("wkv", 2 * F), ("wqm", 2 * F), ("w2", U), ("w3", U)):
        for part in ("out", "in", "land"):
            scratch["d" + name + "_" + part] = ((C, HB, width), BF16)
        if not dims.flat:
            scratch[name + "_f"] = ((C * RB, width), BF16)
    names = list(inputs) + list(outputs) + list(scratch) + ["send_sems", "recv_sems", "credits"]
    vmem = pl.BlockSpec(memory_space=pltpu.VMEM)
    in_specs = [
        pl.BlockSpec(memory_space=pltpu.SMEM) if name == "length" else vmem for name in inputs
    ]
    results = pl.pallas_call(
        functools.partial(layer_kernel, dims, names),
        out_shape=[jax.ShapeDtypeStruct(s, t) for s, t in outputs.values()],
        in_specs=in_specs,
        out_specs=[vmem] * len(outputs),
        scratch_shapes=[pltpu.VMEM(s, t) for s, t in scratch.values()]
        + [pltpu.SemaphoreType.DMA((slots.total,)), pltpu.SemaphoreType.DMA((slots.total,))]
        + [pltpu.SemaphoreType.REGULAR((2,))],
        compiler_params=pltpu.CompilerParams(
            collective_id=0, has_side_effects=True, vmem_limit_bytes=63 * 2**20
        ),
        name="layer",
    )(*inputs.values())
    return dict(zip(outputs, results))


def on_device(
    layer_in,
    lengths,
    w_attn,
    b_attn,
    w_mixer,
    b_mixer,
    gain_one,
    shift_one,
    w_expand,
    b_expand,
    w_reduce,
    b_reduce,
    gain_two,
    shift_two,
    out_grad,
):
    rows = w_mixer.shape[0]
    feats = w_mixer.shape[1]
    units = w_expand.shape[1]
    own = jnp.stack([b_mixer, gain_one, shift_one, b_reduce, gain_two, shift_two])
    small = jnp.concatenate(
        [
            jnp.pad(own, ((0, 0), (0, feats - rows))),
            b_attn,
            b_expand.reshape(units // feats, feats),
        ]
    ).astype(F32)
    out = run_layer(
        layer_in,
        lengths,
        jnp.transpose(w_attn, (1, 0, 2)),
        w_mixer,
        w_expand,
        w_reduce,
        small,
        out_grad,
    )
    g_vec = out["g_vec"]
    return (
        out["layer_out"],
        out["grad_input"],
        jnp.transpose(out["g_attn"], (1, 0, 2)),
        out["g_ab"],
        out["g_mix"],
        g_vec[0],
        g_vec[1],
        g_vec[2],
        out["dw2_sum"],
        out["g_unit"][0],
        out["dw3_sum"],
        g_vec[3],
        g_vec[4],
        g_vec[5],
    )


def solution(mesh):
    return jax.shard_map(
        on_device,
        mesh=mesh,
        in_specs=(
            P(None, ("dp", "row", "col")),
            P("dp"),
            P("col", None, "row"),
            P(None, "row"),
            P("col", "row"),
            P("col"),
            P("col"),
            P("col"),
            P("col", "row"),
            P("row"),
            P("col", "row"),
            P("col"),
            P("col"),
            P("col"),
            P(None, ("dp", "row", "col")),
        ),
        out_specs=(
            P(None, ("dp", "row", "col")),
            P(None, ("dp", "row", "col")),
            P("col", None, "row"),
            P(None, "row"),
            P("col", "row"),
            P("col"),
            P("col"),
            P("col"),
            P("col", "row"),
            P("row"),
            P("col", "row"),
            P("col"),
            P("col"),
            P("col"),
        ),
        check_vma=False,
    )
```

```python
import functools
from types import SimpleNamespace

import jax
import jax.numpy as jnp
from jax import lax
from jax.experimental import pallas as pl
from jax.experimental.pallas import tpu as pltpu
from jax.sharding import PartitionSpec as P

D = 768
H = 12
EPSILON = 1e-12
NEGATIVE = -1000000000.0
MESH = pl.DeviceIdType.MESH
F32 = jnp.float32
BF16 = jnp.bfloat16


def dot_nn(left_in, right_in):
    return lax.dot_general(
        left_in, right_in, (((1,), (0,)), ((), ())), preferred_element_type=F32
    )


def dot_nt(left_in, right_in):
    return lax.dot_general(
        left_in, right_in, (((1,), (1,)), ((), ())), preferred_element_type=F32
    )


def turned(values):
    return values.astype(F32).T


def normalize(values):
    row_mean = jnp.mean(values, 1, keepdims=True)
    centered = values - row_mean
    row_var = jnp.mean(centered * centered, 1, keepdims=True)
    row_scale = lax.rsqrt(row_var + EPSILON)
    return centered * row_scale, row_scale


def normalize_back(upstream, normed, row_scale, gain_vec):
    scaled = upstream * gain_vec
    mean_plain = jnp.mean(scaled, 1, keepdims=True)
    mean_cross = jnp.mean(scaled * normed, 1, keepdims=True)
    return row_scale * (scaled - mean_plain - normed * mean_cross)


def column_sum(values):
    return jnp.sum(values, 0, keepdims=True)


class Slots:
    def __init__(self):
        self.base = {}
        self.total = 0

    def add(self, name, count):
        self.base[name] = self.total
        self.total += count


def slots_of(R, C):
    slots = Slots()
    for name in ("x", "mix", "hid", "red", "gr", "gh", "gm", "dx", "gv_row"):
        slots.add(name, R)
    for name in ("vec", "gv_col", "ab_col", "kv_right", "kv_left", "dkv_right", "dkv_left"):
        slots.add(name, C)
    for name in ("wkv", "wqm", "w2", "w3"):
        slots.add(name, C)
        slots.add(name + "_dp", C)
        slots.add("d" + name, C)
        slots.add("d" + name + "_dp", 1)
        slots.add("d" + name + "_out", 1)
    for name in ("gv_dp", "ab_dp"):
        slots.add(name, 1)
    return slots


def layer_kernel(dims, names, *refs):
    e = SimpleNamespace(**dict(zip(names, refs)))
    R, C, T, S, F, U, RB = dims.R, dims.C, dims.T, dims.S, dims.F, dims.U, dims.RB
    NH, HS, HB = dims.NH, dims.HS, dims.HB
    slots = slots_of(R, C)
    me_d = lax.axis_index("dp")
    me_r = lax.axis_index("row")
    me_c = lax.axis_index("col")

    def to_row(step):
        return {"row": lax.rem(me_r + step, R)}

    def to_col(step):
        return {"col": lax.rem(me_c + step, C)}

    partner = {"dp": 1 - me_d}

    def copy(src, dst, family, at, where):
        number = slots.base[family] + at
        return pltpu.make_async_remote_copy(
            src_ref=src,
            dst_ref=dst,
            send_sem=e.send_sems.at[number],
            recv_sem=e.recv_sems.at[number],
            device_id=where,
            device_id_type=MESH,
        )

    barrier = pltpu.get_barrier_semaphore()
    pl.semaphore_signal(barrier, inc=1, device_id=partner, device_id_type=MESH)
    for i in range(1, R):
        pl.semaphore_signal(barrier, inc=1, device_id=to_row(i), device_id_type=MESH)
    for i in range(1, C):
        pl.semaphore_signal(barrier, inc=1, device_id=to_col(i), device_id_type=MESH)
    e.xg[me_r] = turned(e.x_t[...]).astype(BF16)
    e.wkv[:, :F] = e.w_attn[1]
    e.wkv[:, F:] = e.w_attn[2]
    e.wqm[:, :F] = e.w_attn[0]
    e.wqm[:, F:] = e.w_mixer[...]
    e.vecr[me_c] = e.small[0:8, :]
    pl.semaphore_wait(barrier, 1 + (R - 1) + (C - 1))

    def w_rows(ref, c, d):
        if not dims.flat:
            return ref.at[c]
        return ref.at[pl.ds(pl.multiple_of(c * RB + d * HB, HB), HB)]

    def weight_copy(name, i):
        own = getattr(e, name)
        if dims.flat:
            own = own.at[pl.ds(pl.multiple_of(me_d * HB, HB), HB)]
        return copy(own, w_rows(getattr(e, name + "_g"), me_c, me_d), name, i, to_col(i))

    def weight_pass(name, i):
        there = w_rows(getattr(e, name + "_g"), lax.rem(me_c - i + C, C), me_d)
        return copy(there, there, name + "_dp", i, partner)

    def weight_start(name, which=None):
        for i in range(1, C):
            if which is None:
                weight_copy(name, i).start()
            else:
                to = lax.rem(me_c + i, C)
                inner = (to > 0) & (to < C - 1)
                pl.when(inner if which == "inner" else jnp.logical_not(inner))(
                    weight_copy(name, i).start
                )

    def weight_own(name):
        full = getattr(e, name + "_g")
        if dims.flat:
            full[pl.ds(pl.multiple_of(me_c * RB, RB), RB), :] = getattr(e, name)[...]
        else:
            full[me_c] = getattr(e, name)[...]

    def weight_share(name):
        for i in range(1, C):
            weight_copy(name, i).wait_recv()
            if dims.flat:
                weight_pass(name, i).start()

    def weight_end(name):
        if dims.flat:
            for i in range(1, C):
                weight_pass(name, i).wait_recv()
        else:
            full = getattr(e, name + "_g")
            flat = full[...].astype(F32).reshape(C * RB, full.shape[2])
            getattr(e, name + "_f")[...] = flat.astype(BF16)

    def weight_close(name):
        for i in range(1, C):
            weight_copy(name, i).wait_send()
            if dims.flat:
                weight_pass(name, i).wait_send()

    wkv, wqm, w2f, w3f = [
        getattr(e, name + ("_g" if dims.flat else "_f")) for name in ("wkv", "wqm", "w2", "w3")
    ]

    def x_copy(i):
        return copy(e.xg.at[me_r], e.xg.at[me_r], "x", i, to_row(i))

    def vec_copy(i):
        return copy(e.vecr.at[me_c], e.vecr.at[me_c], "vec", i, to_col(i))

    for i in range(1, R):
        x_copy(i).start()
    weight_start("wkv")
    length = e.length[0]
    for name in ("wkv", "wqm", "w2", "w3"):
        weight_own(name)

    weight_share("wkv")
    weight_start("wqm")
    for i in range(1, C):
        vec_copy(i).start()
    weight_end("wkv")

    for i in range(R):
        rb = lax.rem(me_r - i + R, R)
        if i:
            x_copy(i).wait_recv()
        tokens = pl.ds(pl.multiple_of(rb * T, T), T)
        both = dot_nn(e.xg[rb], wkv[...])
        values = both[:, F:] + e.small[7:8, :]
        e.kv[me_c, pl.ds(0, F), tokens] = both[:, :F].T.astype(BF16)
        e.kv[me_c, pl.ds(F, F), tokens] = values.T.astype(BF16)

    def make_queries():
        weight_share("wqm")
        weight_end("wqm")
        e.mix[...] = wqm[:, F:]
        for i in range(R):
            tokens = pl.ds(i * T, T)
            block = e.xg[i]
            q = dot_nn(block, wqm[:, :F]) + e.small[6:7, :]
            q = q.astype(BF16).astype(F32) * (HS ** (-0.5))
            e.q_t[:, tokens] = q.T.astype(BF16)
            for h in range(NH):
                e.q_h[h, tokens, :] = q[:, h * HS : (h + 1) * HS].astype(BF16)
            e.x_rows_t[:, tokens] = turned(block).astype(BF16)

    right = {"col": lax.rem(me_c + 1, C)}
    left = {"col": lax.rem(me_c + C - 1, C)}

    def kv_right(b):
        return copy(e.kv.at[b], e.kv.at[b], "kv_right", b, right)

    def kv_left(b):
        return copy(e.kv.at[b], e.kv.at[b], "kv_left", b, left)

    def key_valid(b):
        lane = lax.broadcasted_iota(jnp.int32, (1, S), 1)
        return (lane // T * (T * C) + b * T + lane % T) < length

    TQ = dims.TQ
    e.top[...] = jnp.full(e.top.shape, -3e38, F32)
    e.total[...] = jnp.zeros(e.total.shape, F32)
    e.acc[...] = jnp.zeros(e.acc.shape, F32)

    def attend(b):
        valid = key_valid(b)

        def tile(t, carry):
            rows = pl.ds(pl.multiple_of(t * TQ, TQ), TQ)
            for h in range(NH):
                keys = e.kv[b, h * HS : (h + 1) * HS, :]
                values = e.kv[b, F + h * HS : F + (h + 1) * HS, :]
                scores = dot_nn(e.q_h[h, rows, :], keys)
                scores = jnp.where(valid, scores, NEGATIVE)
                old = e.top[h, rows, :]
                new = jnp.maximum(old, jnp.max(scores, 1, keepdims=True))
                shrink = jnp.exp(old - new)
                probs = jnp.exp(scores - new)
                e.top[h, rows, :] = new
                e.total[h, rows, :] = shrink * e.total[h, rows, :] + jnp.sum(
                    probs, 1, keepdims=True
                )
                e.acc[h, rows, :] = shrink * e.acc[h, rows, :] + dot_nt(
                    probs.astype(BF16), values
                )
            return carry

        lax.fori_loop(0, S // TQ, tile, 0)

    @pl.when(me_c < C - 1)
    def _():
        kv_right(me_c).start()

    @pl.when(me_c > 0)
    def _():
        kv_left(me_c).start()

    make_queries()
    attend(me_c)

    def kv_step(s, carry):
        from_left = me_c - s
        from_right = me_c + s

        @pl.when(from_left >= 0)
        def _():
            kv_right(from_left).wait_recv()

            @pl.when(me_c < C - 1)
            def _():
                kv_right(from_left).start()

        @pl.when(from_right < C)
        def _():
            kv_left(from_right).wait_recv()

            @pl.when(me_c > 0)
            def _():
                kv_left(from_right).start()

        @pl.when(s == min(2, C - 1))
        def _():
            weight_start("w2", "inner")
            weight_start("w3", "inner")

        @pl.when(from_left >= 0)
        def _():
            attend(from_left)

        @pl.when(from_right < C)
        def _():
            attend(from_right)

        return carry

    lax.fori_loop(1, C, kv_step, 0)

    def kv_close(b, carry):
        @pl.when((b <= me_c) & (me_c < C - 1))
        def _():
            kv_right(b).wait_send()

        @pl.when((b >= me_c) & (me_c > 0))
        def _():
            kv_left(b).wait_send()

        return carry

    lax.fori_loop(0, C, kv_close, 0)
    weight_start("w2", "outer")
    weight_start("w3", "outer")

    for h in range(NH):
        inverse = 1.0 / e.total[h]
        e.total[h] = inverse
        context = e.acc[h] * inverse
        e.acc[h] = context
        e.ctx[:, h * HS : (h + 1) * HS] = context.astype(BF16)

    for i in range(1, C):
        vec_copy(i).wait_recv()
    for c in range(C):
        e.vecs[:, c * RB : (c + 1) * RB] = e.vecr[c][:, :RB]
    for k in range(U // F):
        e.bias[:, k * F : (k + 1) * F] = e.small[8 + k : 9 + k, :]

    def vector(at):
        return e.vecs[at : at + 1, :]

    def blk_rows(rb):
        return pl.ds(pl.multiple_of(rb * T, T), T)

    for i in list(range(1, R)) + [0]:
        rb = lax.rem(me_r + i, R)
        part = dot_nt(e.ctx[blk_rows(rb), :], e.mix[...])
        if i:
            e.stage[0, i - 1] = part.astype(BF16)
            copy(e.stage.at[0, i - 1], e.landing.at[0, i - 1], "mix", i, to_row(i)).start()
        else:
            e.own[...] = part

    def collect(number, family):
        total = e.own[...]
        for i in range(1, R):
            copy(e.stage.at[number, i - 1], e.landing.at[number, i - 1], family, i, to_row(i)).wait_recv()
            total = total + e.landing[number, i - 1].astype(F32)
        return total

    first_sum = turned(e.x_t[...]) + collect(0, "mix") + vector(0)
    normed, scale = normalize(first_sum)
    hidden = normed * vector(1) + vector(2)
    e.n1[...] = normed
    e.r1[...] = scale
    e.hidden[...] = hidden
    e.hid_g[me_r] = hidden.astype(BF16)

    def share(ref, family, i):
        return copy(ref.at[me_r], ref.at[me_r], family, i, to_row(i))

    for i in range(1, R):
        share(e.hid_g, "hid", i).start()
    weight_share("w2")
    weight_end("w2")

    def spread(number, family, part, i, rb):
        if i:
            e.stage[number, i - 1] = part.astype(BF16)
            copy(
                e.stage.at[number, i - 1], e.landing.at[number, i - 1], family, i, to_row(R - i)
            ).start()
        else:
            e.own[...] = part

    for i in range(R):
        rb = lax.rem(me_r - i + R, R)
        if i:
            share(e.hid_g, "hid", i).wait_recv()
        inner = dot_nn(e.hid_g[rb], w2f[...]) + e.bias[...]
        cdf = 0.5 * (1.0 + lax.erf(inner * (0.5**0.5)))
        active = (inner * cdf).astype(BF16)
        slope = cdf + inner * (jnp.exp(-0.5 * inner * inner) * 0.3989422804014327)
        e.active[blk_rows(rb), :] = active
        e.slope[blk_rows(rb), :] = slope
        if i == 0:
            weight_share("w3")
            weight_end("w3")
        spread(1, "red", dot_nt(e.active[blk_rows(rb), :], w3f[...]), i, rb)
    for i in range(R):
        rb = lax.rem(me_r - i + R, R)
        e.hid_t[:, blk_rows(rb)] = turned(e.hid_g[rb]).astype(BF16)

    second_sum = e.hidden[...] + collect(1, "red") + vector(3)
    normed, scale = normalize(second_sum)
    slot = lax.broadcasted_iota(jnp.int32, (T, 1), 0) + (me_r * (T * C) + me_c * T)
    row_valid = (slot < length).astype(F32)
    upstream = turned(e.out_grad[...]) * row_valid
    g_second = normalize_back(upstream, normed, scale, vector(4))
    g_reduced = g_second.astype(BF16)
    e.gr_g[me_r] = g_reduced
    for i in range(1, R):
        share(e.gr_g, "gr", i).start()
    e.layer_out[...] = ((normed * vector(4) + vector(5)) * row_valid).T.astype(BF16)
    e.g_second[...] = g_second
    e.gv[4:5, :] = column_sum(upstream * normed)
    e.gv[5:6, :] = column_sum(upstream)
    e.gv[3:4, :] = column_sum(g_reduced.astype(F32))
    e.gv[7:8, :] = jnp.zeros((1, D), F32)

    unit_sum = jnp.zeros((1, U), F32)
    for i in range(R):
        rb = lax.rem(me_r - i + R, R)
        if i:
            share(e.gr_g, "gr", i).wait_recv()
        g_active = dot_nn(e.gr_g[rb], w3f[...]).astype(BF16).astype(F32)
        g_inner = (g_active * e.slope[blk_rows(rb), :]).astype(BF16)
        e.g_inner[blk_rows(rb), :] = g_inner
        unit_sum = unit_sum + column_sum(g_inner.astype(F32))
        spread(2, "gh", dot_nt(e.g_inner[blk_rows(rb), :], w2f[...]), i, rb)
    e.gu[0:1, :] = unit_sum
    for i in range(R):
        rb = lax.rem(me_r - i + R, R)
        e.gr_t[:, blk_rows(rb)] = turned(e.gr_g[rb]).astype(BF16)

    TR = dims.TR

    def half_rows(c, d):
        if not dims.flat:
            return pl.ds(c * RB, RB)
        return pl.ds(pl.multiple_of(c * RB + d * HB, HB), HB)

    def other_copy(name):
        return copy(getattr(e, name + "_out"), getattr(e, name + "_in"), name + "_dp", 0, partner)

    def d_copy(name, i):
        stage = getattr(e, name + "_in").at[lax.rem(me_c + i, C)]
        return copy(stage, getattr(e, name + "_land").at[i], name, i, to_col(i))

    def row_tiles(fill):
        def tile(t, carry):
            fill(pl.ds(pl.multiple_of(t * TR, TR), TR))
            return carry

        lax.fori_loop(0, D // TR, tile, 0)

    def weight_swap(name, source):
        def block(c, carry):
            getattr(e, name + "_out")[c] = source[half_rows(c, 1 - me_d), :].astype(BF16)
            return carry

        lax.fori_loop(0, C, block, 0)
        other_copy(name).start()

    def weight_send(name, source):
        other_copy(name).wait_recv()

        def block(c, carry):
            total = source[half_rows(c, me_d), :] + getattr(e, name + "_in")[c].astype(F32)
            getattr(e, name + "_in")[c] = total.astype(BF16)
            return carry

        lax.fori_loop(0, C, block, 0)
        for i in range(1, C):
            d_copy(name, i).start()

    def result_part(name):
        full = getattr(e, name + "_sum")
        return full.at[pl.ds(pl.multiple_of(me_d * HB, HB), HB)] if dims.flat else full

    def result_copy(name):
        return copy(result_part(name), result_part(name), name + "_out", 0, partner)

    def weight_collect(name):
        total = getattr(e, name + "_in")[me_c].astype(F32)
        for i in range(1, C):
            d_copy(name, i).wait_recv()
            total = total + getattr(e, name + "_land")[i].astype(F32)
        result_part(name)[...] = total
        if dims.flat:
            result_copy(name).start()

    def fill_reduce(rows):
        e.dw_f[rows, :] = dot_nn(e.gr_t[rows, :], e.active[...])

    def fill_expand(rows):
        e.dw_f[rows, :] = dot_nn(e.hid_t[rows, :], e.g_inner[...])

    row_tiles(fill_reduce)
    weight_swap("dw3", e.dw_f)
    weight_send("dw3", e.dw_f)
    row_tiles(fill_expand)
    weight_swap("dw2", e.dw_f)
    weight_send("dw2", e.dw_f)

    g_hidden = collect(2, "gh") + e.g_second[...]
    normed = e.n1[...]
    g_first = normalize_back(g_hidden, normed, e.r1[...], vector(1))
    g_mixed = g_first.astype(BF16)
    for i in range(1, R):
        share(e.hid_g, "hid", i).wait_send()
    e.hid_g[me_r] = g_mixed
    for i in range(1, R):
        share(e.hid_g, "gm", i).start()
    e.g_first[...] = g_first
    e.gv[1:2, :] = column_sum(g_hidden * normed)
    e.gv[2:3, :] = column_sum(g_hidden)
    e.gv[0:1, :] = column_sum(g_mixed.astype(F32))
    e.gv[6:7, :] = jnp.zeros((1, D), F32)

    def gv_dp():
        return copy(e.gall.at[0], e.gall.at[1], "gv_dp", 0, partner)

    e.gall[0, 0:8, :D] = e.gv[...]
    e.gall[0, 8:16, :U] = jnp.broadcast_to(e.gu[0:1, :], (8, U))
    gv_dp().start()

    for i in range(R):
        rb = lax.rem(me_r - i + R, R)
        if i:
            share(e.hid_g, "gm", i).wait_recv()
        rows = blk_rows(rb)
        g_context = dot_nn(e.hid_g[rb], e.mix[...]).astype(BF16).astype(F32)
        e.gc_t[:, rows] = g_context.T.astype(BF16)
        for h in range(NH):
            part = g_context[:, h * HS : (h + 1) * HS]
            e.gc_h[h, rows, :] = part.astype(BF16)
            e.inner_sum[h, rows, :] = jnp.sum(part * e.acc[h, rows, :], 1, keepdims=True)
        e.gr_t[:, rows] = turned(e.hid_g[rb]).astype(BF16)

    gv_dp().wait_recv()
    e.gall[2] = e.gall[0] + e.gall[1]

    def gv_col(i):
        return copy(e.gall.at[2], e.gcol.at[i], "gv_col", i, to_col(i))

    for i in range(1, C):
        gv_col(i).start()

    e.dq[...] = jnp.zeros(e.dq.shape, F32)

    def attend_back(b, to):
        valid = key_valid(b)
        for h in range(NH):
            krows = slice(h * HS, (h + 1) * HS)
            vrows = slice(F + h * HS, F + (h + 1) * HS)

            def tile(t, carry):
                d_keys, d_values = carry
                rows = pl.ds(pl.multiple_of(t * TQ, TQ), TQ)
                keys = e.kv[b, krows, :]
                values = e.kv[b, vrows, :]
                scores = dot_nn(e.q_h[h, rows, :], keys)
                scores = jnp.where(valid, scores, NEGATIVE)
                probs = jnp.exp(scores - e.top[h, rows, :]) * e.total[h, rows, :]
                g_weights = dot_nn(e.gc_h[h, rows, :], values)
                g_scores = (probs * (g_weights - e.inner_sum[h, rows, :])).astype(BF16)
                e.dq[h, rows, :] += dot_nt(g_scores, keys)
                d_keys = d_keys + dot_nn(e.q_t[krows, rows], g_scores)
                d_values = d_values + dot_nn(e.gc_t[krows, rows], probs.astype(BF16))
                return d_keys, d_values

            zero = jnp.zeros((HS, S), F32)
            d_keys, d_values = lax.fori_loop(0, S // TQ, tile, (zero, zero))
            e.dkv[to, krows, :] = d_keys
            e.dkv[to, vrows, :] = d_values

    NB = dims.NB

    def dkv_right(b):
        return copy(
            e.kv.at[b], e.dkv_in.at[0, lax.rem(C - 1 - b, NB)], "dkv_right", b, right
        )

    def dkv_left(b):
        return copy(e.kv.at[b], e.dkv_in.at[1, lax.rem(b, NB)], "dkv_left", b, left)

    def dkv_send(way, b):
        order = C - 1 - b if way == 0 else b
        if C - 1 > NB:

            @pl.when(order >= NB)
            def _():
                pl.semaphore_wait(e.credits.at[way], 1)

        if way == 0:

            @pl.when(b < C - 1)
            def _():
                dkv_right(b + 1).wait_send()

            dkv_right(b).start()
        else:

            @pl.when(b > 0)
            def _():
                dkv_left(b - 1).wait_send()

            dkv_left(b).start()

    def dkv_take(way, b, to):
        order = C - 1 - b if way == 0 else b
        (dkv_right if way == 0 else dkv_left)(b).wait_recv()
        e.dkv[to] += e.dkv_in[way, lax.rem(order, NB)].astype(F32)
        if C - 1 > NB:
            sends = C - me_c if way == 0 else me_c + 1

            @pl.when(order + NB < sends)
            def _():
                pl.semaphore_signal(
                    e.credits.at[way],
                    inc=1,
                    device_id=left if way == 0 else right,
                    device_id_type=MESH,
                )

    inner_device = (me_c > 0) & (me_c < C - 1)

    @pl.when(inner_device)
    def _():
        attend_back(me_c, 2)

    def dkv_step(s, carry):
        from_left = C - 1 + me_c - s
        from_right = s - (C - 1 - me_c)

        @pl.when(s >= me_c)
        def _():
            attend_back(from_left, 0)

        @pl.when(from_right >= 0)
        def _():
            attend_back(from_right, 1)

        @pl.when(s >= me_c)
        def _():
            @pl.when(me_c > 0)
            def _():
                dkv_take(0, from_left, 0)

            e.kv[from_left] = e.dkv[0].astype(BF16)
            dkv_send(0, from_left)

        @pl.when(from_right >= 0)
        def _():
            @pl.when(me_c < C - 1)
            def _():
                dkv_take(1, from_right, 1)

            e.kv[from_right] = e.dkv[1].astype(BF16)
            dkv_send(1, from_right)

        return carry

    lax.fori_loop(0, C - 1, dkv_step, 0)

    @pl.when(jnp.logical_not(inner_device))
    def _():
        attend_back(me_c, 2)

    for h in range(NH):
        e.dqkv[h * HS : (h + 1) * HS, :] = (e.dq[h] * (HS ** (-0.5))).T.astype(BF16)

    def fill_query(rows):
        e.dw_s[rows, :F] = dot_nt(e.x_rows_t[rows, :], e.dqkv[:F, :])
        e.dw_s[rows, F:] = dot_nn(e.gr_t[rows, :], e.ctx[...])

    row_tiles(fill_query)
    weight_swap("dwqm", e.dw_s)
    weight_send("dwqm", e.dw_s)
    weight_collect("dw3")
    weight_collect("dw2")

    for i in range(1, C):
        gv_col(i).wait_recv()
    gsum = e.gall[2]
    for i in range(1, C):
        gsum = gsum + e.gcol[i]
    e.gsum[...] = gsum

    def gv_row(i):
        return copy(e.gsum.at[pl.ds(0, 8)], e.grow.at[i], "gv_row", i, to_row(i))

    for i in range(1, R):
        gv_row(i).start()

    @pl.when(me_c > 0)
    def _():
        dkv_take(0, me_c, 2)

    @pl.when(me_c < C - 1)
    def _():
        dkv_take(1, me_c, 2)

    e.dqkv[F : 3 * F, :] = e.dkv[2].astype(BF16)

    for i in list(range(1, R)) + [0]:
        rb = lax.rem(me_r + i, R)
        part = dot_nn(wqm[:, :F], e.dqkv[:F, blk_rows(rb)]) + dot_nn(
            wkv[...], e.dqkv[F:, blk_rows(rb)]
        )
        if i:
            e.dx_stage[i - 1] = part.astype(BF16)
            copy(e.dx_stage.at[i - 1], e.dx_land.at[i - 1], "dx", i, to_row(i)).start()
        else:
            e.dx_own[...] = part

    def fill_keys(rows):
        e.dw_s[rows, :] = dot_nt(e.x_rows_t[rows, :], e.dqkv[F:, :])

    row_tiles(fill_keys)
    weight_swap("dwkv", e.dw_s)
    e.ab[0] = dot_nt(jnp.ones((8, S), BF16), e.dqkv[...])

    def ab_dp():
        return copy(e.ab.at[0], e.ab.at[1], "ab_dp", 0, partner)

    def ab_col(i):
        return copy(e.ab.at[2], e.abcol.at[i], "ab_col", i, to_col(i))

    ab_dp().start()
    weight_send("dwkv", e.dw_s)
    ab_dp().wait_recv()
    e.ab[2] = e.ab[0] + e.ab[1]
    for i in range(1, C):
        ab_col(i).start()

    weight_collect("dwqm")

    total = e.dx_own[...] + e.g_first[...].T
    for i in range(1, R):
        copy(e.dx_stage.at[i - 1], e.dx_land.at[i - 1], "dx", i, to_row(i)).wait_recv()
        total = total + e.dx_land[i - 1].astype(F32)
    e.grad_input[...] = total

    vsum = e.gsum[0:8, :D]
    for i in range(1, R):
        gv_row(i).wait_recv()
        vsum = vsum + e.grow[i][:, :D]
    mine = vsum[:, :RB]
    for c in range(1, C):
        mine = jnp.where(me_c == c, vsum[:, c * RB : (c + 1) * RB], mine)
    e.g_vec[...] = mine
    e.g_unit[...] = e.gsum[8:9, :U]
    asum = e.ab[2]
    for i in range(1, C):
        ab_col(i).wait_recv()
        asum = asum + e.abcol[i]
    e.g_ab[0:1, :] = asum[0:1, :F]
    e.g_ab[1:2, :] = asum[0:1, 2 * F :]
    weight_collect("dwkv")
    if dims.flat:
        for name in ("dw3", "dw2", "dwqm", "dwkv"):
            result_copy(name).wait_recv()
    e.g_attn[0] = e.dwqm_sum[:, :F]
    e.g_mix[...] = e.dwqm_sum[:, F:]
    e.g_attn[1] = e.dwkv_sum[:, :F]
    e.g_attn[2] = e.dwkv_sum[:, F:]

    for name in ("wkv", "wqm", "w2", "w3"):
        weight_close(name)
    for i in range(1, R):
        x_copy(i).wait_send()
        copy(e.stage.at[0, i - 1], e.landing.at[0, i - 1], "mix", i, to_row(i)).wait_send()
        copy(e.stage.at[1, i - 1], e.landing.at[1, i - 1], "red", i, to_row(i)).wait_send()
        share(e.gr_g, "gr", i).wait_send()
        copy(e.stage.at[2, i - 1], e.landing.at[2, i - 1], "gh", i, to_row(i)).wait_send()
        share(e.hid_g, "gm", i).wait_send()
        copy(e.dx_stage.at[i - 1], e.dx_land.at[i - 1], "dx", i, to_row(i)).wait_send()
        gv_row(i).wait_send()
    gv_dp().wait_send()
    ab_dp().wait_send()
    for i in range(1, C):
        vec_copy(i).wait_send()
        gv_col(i).wait_send()
        ab_col(i).wait_send()
    for name in ("dw3", "dw2", "dwqm", "dwkv"):
        other_copy(name).wait_send()
        for i in range(1, C):
            d_copy(name, i).wait_send()
        if dims.flat:
            result_copy(name).wait_send()

    @pl.when(me_c < C - 1)
    def _():
        dkv_right(me_c + 1).wait_send()

    @pl.when(me_c > 0)
    def _():
        dkv_left(me_c - 1).wait_send()


def run_layer(x_t, length, w_attn, w_mixer, w2, w3, small, out_grad):
    R = lax.axis_size("row")
    C = lax.axis_size("col")
    T = x_t.shape[1]
    S = T * R
    F = w_mixer.shape[1]
    U = w2.shape[1]
    RB = w_mixer.shape[0]
    flat = RB % 32 == 0
    HS = D // H
    dims = SimpleNamespace(
        R=R, C=C, T=T, S=S, F=F, U=U, RB=RB, HS=HS, NH=F // HS,
        flat=flat, HB=RB // 2 if flat else RB, TQ=min(256, S), TR=256, NB=min(C - 1, 3),
    )
    HB = dims.HB
    NH = dims.NH
    slots = slots_of(R, C)
    wide = max(D, U)
    w_shape = (lambda n: (C * RB, n)) if dims.flat else (lambda n: (C, RB, n))
    inputs = dict(
        x_t=x_t, length=length, w_attn=w_attn, w_mixer=w_mixer, w2=w2, w3=w3, small=small,
        out_grad=out_grad,
    )
    outputs = dict(
        layer_out=((D, T), BF16),
        grad_input=((D, T), F32),
        g_attn=((3, RB, F), F32),
        g_mix=((RB, F), F32),
        dw2_sum=((RB, U), F32),
        dw3_sum=((RB, U), F32),
        g_vec=((8, RB), F32),
        g_unit=((1, U), F32),
        g_ab=((2, F), F32),
    )
    scratch = dict(
        xg=((R, T, D), BF16),
        wkv=((RB, 2 * F), BF16),
        wqm=((RB, 2 * F), BF16),
        wkv_g=(w_shape(2 * F), BF16),
        wqm_g=(w_shape(2 * F), BF16),
        w2_g=(w_shape(U), BF16),
        w3_g=(w_shape(U), BF16),
        mix=((D, F), BF16),
        vecr=((C, 8, F), F32),
        vecs=((8, D), F32),
        bias=((1, U), F32),
        kv=((C, 2 * F, S), BF16),
        q_t=((F, S), BF16),
        q_h=((NH, S, HS), BF16),
        x_rows_t=((D, S), BF16),
        top=((NH, S, 1), F32),
        total=((NH, S, 1), F32),
        acc=((NH, S, HS), F32),
        ctx=((S, F), BF16),
        stage=((3, R - 1, T, D), BF16),
        landing=((3, R - 1, T, D), BF16),
        own=((T, D), F32),
        n1=((T, D), F32),
        r1=((T, 1), F32),
        hidden=((T, D), F32),
        hid_g=((R, T, D), BF16),
        active=((S, U), BF16),
        slope=((S, U), F32),
        hid_t=((D, S), BF16),
        g_second=((T, D), F32),
        gr_g=((R, T, D), BF16),
        gr_t=((D, S), BF16),
        g_inner=((S, U), BF16),
        gv=((8, D), F32),
        gu=((8, U), F32),
        gall=((3, 16, wide), F32),
        gcol=((C, 16, wide), F32),
        gsum=((16, wide), F32),
        grow=((R, 8, wide), F32),
        dw_f=((D, U), F32),
        dw_s=((D, 2 * F), F32),
        dwqm_sum=((RB, 2 * F), F32),
        dwkv_sum=((RB, 2 * F), F32),
        g_first=((T, D), F32),
        gc_t=((F, S), BF16),
        gc_h=((NH, S, HS), BF16),
        inner_sum=((NH, S, 1), F32),
        dq=((NH, S, HS), F32),
        dkv=((3, 2 * F, S), F32),
        dkv_in=((2, dims.NB, 2 * F, S), BF16),
        dqkv=((3 * F, S), BF16),
        dx_stage=((R - 1, D, T), BF16),
        dx_land=((R - 1, D, T), BF16),
        dx_own=((D, T), F32),
        ab=((3, 8, 3 * F), F32),
        abcol=((C, 8, 3 * F), F32),
    )
    for name, width in (("wkv", 2 * F), ("wqm", 2 * F), ("w2", U), ("w3", U)):
        for part in ("out", "in", "land"):
            scratch["d" + name + "_" + part] = ((C, HB, width), BF16)
        if not dims.flat:
            scratch[name + "_f"] = ((C * RB, width), BF16)
    names = list(inputs) + list(outputs) + list(scratch) + ["send_sems", "recv_sems", "credits"]
    vmem = pl.BlockSpec(memory_space=pltpu.VMEM)
    in_specs = [
        pl.BlockSpec(memory_space=pltpu.SMEM) if name == "length" else vmem for name in inputs
    ]
    results = pl.pallas_call(
        functools.partial(layer_kernel, dims, names),
        out_shape=[jax.ShapeDtypeStruct(s, t) for s, t in outputs.values()],
        in_specs=in_specs,
        out_specs=[vmem] * len(outputs),
        scratch_shapes=[pltpu.VMEM(s, t) for s, t in scratch.values()]
        + [pltpu.SemaphoreType.DMA((slots.total,)), pltpu.SemaphoreType.DMA((slots.total,))]
        + [pltpu.SemaphoreType.REGULAR((2,))],
        compiler_params=pltpu.CompilerParams(
            collective_id=0, has_side_effects=True, vmem_limit_bytes=63 * 2**20
        ),
        name="layer",
    )(*inputs.values())
    return dict(zip(outputs, results))


def on_device(
    layer_in,
    lengths,
    w_attn,
    b_attn,
    w_mixer,
    b_mixer,
    gain_one,
    shift_one,
    w_expand,
    b_expand,
    w_reduce,
    b_reduce,
    gain_two,
    shift_two,
    out_grad,
):
    rows = w_mixer.shape[0]
    feats = w_mixer.shape[1]
    units = w_expand.shape[1]
    own = jnp.stack([b_mixer, gain_one, shift_one, b_reduce, gain_two, shift_two])
    small = jnp.concatenate(
        [
            jnp.pad(own, ((0, 0), (0, feats - rows))),
            b_attn,
            b_expand.reshape(units // feats, feats),
        ]
    ).astype(F32)
    out = run_layer(
        layer_in,
        lengths,
        jnp.transpose(w_attn, (1, 0, 2)),
        w_mixer,
        w_expand,
        w_reduce,
        small,
        out_grad,
    )
    g_vec = out["g_vec"]
    return (
        out["layer_out"],
        out["grad_input"],
        jnp.transpose(out["g_attn"], (1, 0, 2)),
        out["g_ab"],
        out["g_mix"],
        g_vec[0],
        g_vec[1],
        g_vec[2],
        out["dw2_sum"],
        out["g_unit"][0],
        out["dw3_sum"],
        g_vec[3],
        g_vec[4],
        g_vec[5],
    )


def solution(mesh):
    return jax.shard_map(
        on_device,
        mesh=mesh,
        in_specs=(
            P(None, ("dp", "row", "col")),
            P("dp"),
            P("col", None, "row"),
            P(None, "row"),
            P("col", "row"),
            P("col"),
            P("col"),
            P("col"),
            P("col", "row"),
            P("row"),
            P("col", "row"),
            P("col"),
            P("col"),
            P("col"),
            P(None, ("dp", "row", "col")),
        ),
        out_specs=(
            P(None, ("dp", "row", "col")),
            P(None, ("dp", "row", "col")),
            P("col", None, "row"),
            P(None, "row"),
            P("col", "row"),
            P("col"),
            P("col"),
            P("col"),
            P("col", "row"),
            P("row"),
            P("col", "row"),
            P("col"),
            P("col"),
            P("col"),
        ),
        check_vma=False,
    )
```

```python
import functools
from types import SimpleNamespace

import jax
import jax.numpy as jnp
from jax import lax
from jax.experimental import pallas as pl
from jax.experimental.pallas import tpu as pltpu
from jax.sharding import PartitionSpec as P

D = 768
H = 12
EPSILON = 1e-12
NEGATIVE = -1000000000.0
MESH = pl.DeviceIdType.MESH
F32 = jnp.float32
BF16 = jnp.bfloat16


def dot_nn(left_in, right_in):
    return lax.dot_general(
        left_in, right_in, (((1,), (0,)), ((), ())), preferred_element_type=F32
    )


def dot_nt(left_in, right_in):
    return lax.dot_general(
        left_in, right_in, (((1,), (1,)), ((), ())), preferred_element_type=F32
    )


def turned(values):
    return values.astype(F32).T


def normalize(values):
    row_mean = jnp.mean(values, 1, keepdims=True)
    centered = values - row_mean
    row_var = jnp.mean(centered * centered, 1, keepdims=True)
    row_scale = lax.rsqrt(row_var + EPSILON)
    return centered * row_scale, row_scale


def normalize_back(upstream, normed, row_scale, gain_vec):
    scaled = upstream * gain_vec
    mean_plain = jnp.mean(scaled, 1, keepdims=True)
    mean_cross = jnp.mean(scaled * normed, 1, keepdims=True)
    return row_scale * (scaled - mean_plain - normed * mean_cross)


def column_sum(values):
    return jnp.sum(values, 0, keepdims=True)


class Slots:
    def __init__(self):
        self.base = {}
        self.total = 0

    def add(self, name, count):
        self.base[name] = self.total
        self.total += count


def slots_of(R, C):
    slots = Slots()
    for name in ("x", "mix", "hid", "red", "gr", "gh", "gm", "dx", "gv_row"):
        slots.add(name, R)
    for name in ("vec", "gv_col", "ab_col", "kv_right", "kv_left", "dkv_right", "dkv_left"):
        slots.add(name, C)
    for name in ("wkv", "wqm", "w2", "w3"):
        slots.add(name, C)
        slots.add(name + "_dp", C)
        slots.add("d" + name, C)
        slots.add("d" + name + "_dp", 1)
        slots.add("d" + name + "_out", 1)
    for name in ("gv_dp", "ab_dp"):
        slots.add(name, 1)
    return slots


def layer_kernel(dims, names, *refs):
    e = SimpleNamespace(**dict(zip(names, refs)))
    R, C, T, S, F, U, RB = dims.R, dims.C, dims.T, dims.S, dims.F, dims.U, dims.RB
    NH, HS, HB = dims.NH, dims.HS, dims.HB
    slots = slots_of(R, C)
    me_d = lax.axis_index("dp")
    me_r = lax.axis_index("row")
    me_c = lax.axis_index("col")

    def to_row(step):
        return {"row": lax.rem(me_r + step, R)}

    def to_col(step):
        return {"col": lax.rem(me_c + step, C)}

    partner = {"dp": 1 - me_d}

    def copy(src, dst, family, at, where):
        number = slots.base[family] + at
        return pltpu.make_async_remote_copy(
            src_ref=src,
            dst_ref=dst,
            send_sem=e.send_sems.at[number],
            recv_sem=e.recv_sems.at[number],
            device_id=where,
            device_id_type=MESH,
        )

    barrier = pltpu.get_barrier_semaphore()
    pl.semaphore_signal(barrier, inc=1, device_id=partner, device_id_type=MESH)
    for i in range(1, R):
        pl.semaphore_signal(barrier, inc=1, device_id=to_row(i), device_id_type=MESH)
    for i in range(1, C):
        pl.semaphore_signal(barrier, inc=1, device_id=to_col(i), device_id_type=MESH)
    e.xg[me_r] = turned(e.x_t[...]).astype(BF16)
    e.wkv[:, :F] = e.w_attn[1]
    e.wkv[:, F:] = e.w_attn[2]
    e.wqm[:, :F] = e.w_attn[0]
    e.wqm[:, F:] = e.w_mixer[...]
    vectors = (e.b_mixer, e.gain_one, e.shift_one, e.b_reduce, e.gain_two, e.shift_two)
    for k, ref in enumerate(vectors):
        e.vecr[me_c, k : k + 1, :RB] = ref[...].astype(F32).reshape(1, RB)
    e.bias[...] = e.b_expand[...].astype(F32).reshape(1, U)
    pl.semaphore_wait(barrier, 1 + (R - 1) + (C - 1))

    def w_rows(ref, c, d):
        if not dims.flat:
            return ref.at[c]
        return ref.at[pl.ds(pl.multiple_of(c * RB + d * HB, HB), HB)]

    def weight_copy(name, i):
        own = getattr(e, name)
        if dims.flat:
            own = own.at[pl.ds(pl.multiple_of(me_d * HB, HB), HB)]
        return copy(own, w_rows(getattr(e, name + "_g"), me_c, me_d), name, i, to_col(i))

    def weight_pass(name, i):
        there = w_rows(getattr(e, name + "_g"), lax.rem(me_c - i + C, C), me_d)
        return copy(there, there, name + "_dp", i, partner)

    def weight_start(name, which=None):
        for i in range(1, C):
            if which is None:
                weight_copy(name, i).start()
            else:
                to = lax.rem(me_c + i, C)
                inner = (to > 0) & (to < C - 1)
                pl.when(inner if which == "inner" else jnp.logical_not(inner))(
                    weight_copy(name, i).start
                )

    def weight_own(name):
        full = getattr(e, name + "_g")
        if dims.flat:
            full[pl.ds(pl.multiple_of(me_c * RB, RB), RB), :] = getattr(e, name)[...]
        else:
            full[me_c] = getattr(e, name)[...]

    def weight_share(name):
        for i in range(1, C):
            weight_copy(name, i).wait_recv()
            if dims.flat:
                weight_pass(name, i).start()

    def weight_end(name):
        if dims.flat:
            for i in range(1, C):
                weight_pass(name, i).wait_recv()
        else:
            full = getattr(e, name + "_g")
            flat = full[...].astype(F32).reshape(C * RB, full.shape[2])
            getattr(e, name + "_f")[...] = flat.astype(BF16)

    def weight_close(name):
        for i in range(1, C):
            weight_copy(name, i).wait_send()
            if dims.flat:
                weight_pass(name, i).wait_send()

    wkv, wqm, w2f, w3f = [
        getattr(e, name + ("_g" if dims.flat else "_f")) for name in ("wkv", "wqm", "w2", "w3")
    ]

    def x_copy(i):
        return copy(e.xg.at[me_r], e.xg.at[me_r], "x", i, to_row(i))

    def vec_copy(i):
        return copy(e.vecr.at[me_c], e.vecr.at[me_c], "vec", i, to_col(i))

    for i in range(1, R):
        x_copy(i).start()
    weight_start("wkv")
    length = e.length[0]
    for name in ("wkv", "wqm", "w2", "w3"):
        weight_own(name)

    weight_share("wkv")
    weight_start("wqm")
    for i in range(1, C):
        vec_copy(i).start()
    weight_end("wkv")

    for i in range(R):
        rb = lax.rem(me_r - i + R, R)
        if i:
            x_copy(i).wait_recv()
        tokens = pl.ds(pl.multiple_of(rb * T, T), T)
        both = dot_nn(e.xg[rb], wkv[...])
        values = both[:, F:] + e.b_attn[1:2, :].astype(F32)
        e.kv[me_c, pl.ds(0, F), tokens] = both[:, :F].T.astype(BF16)
        e.kv[me_c, pl.ds(F, F), tokens] = values.T.astype(BF16)

    def make_queries():
        weight_share("wqm")
        weight_end("wqm")
        e.mix[...] = wqm[:, F:]
        for i in range(R):
            tokens = pl.ds(i * T, T)
            block = e.xg[i]
            q = dot_nn(block, wqm[:, :F]) + e.b_attn[0:1, :].astype(F32)
            q = q.astype(BF16).astype(F32) * (HS ** (-0.5))
            e.q_t[:, tokens] = q.T.astype(BF16)
            for h in range(NH):
                e.q_h[h, tokens, :] = q[:, h * HS : (h + 1) * HS].astype(BF16)
            e.x_rows_t[:, tokens] = turned(block).astype(BF16)

    right = {"col": lax.rem(me_c + 1, C)}
    left = {"col": lax.rem(me_c + C - 1, C)}

    def kv_right(b):
        return copy(e.kv.at[b], e.kv.at[b], "kv_right", b, right)

    def kv_left(b):
        return copy(e.kv.at[b], e.kv.at[b], "kv_left", b, left)

    def key_valid(b):
        lane = lax.broadcasted_iota(jnp.int32, (1, S), 1)
        return (lane // T * (T * C) + b * T + lane % T) < length

    TQ = dims.TQ
    e.top[...] = jnp.full(e.top.shape, -3e38, F32)
    e.total[...] = jnp.zeros(e.total.shape, F32)
    e.acc[...] = jnp.zeros(e.acc.shape, F32)

    def attend(b):
        valid = key_valid(b)

        def tile(t, carry):
            rows = pl.ds(pl.multiple_of(t * TQ, TQ), TQ)
            for h in range(NH):
                keys = e.kv[b, h * HS : (h + 1) * HS, :]
                values = e.kv[b, F + h * HS : F + (h + 1) * HS, :]
                scores = dot_nn(e.q_h[h, rows, :], keys)
                scores = jnp.where(valid, scores, NEGATIVE)
                old = e.top[h, rows, :]
                new = jnp.maximum(old, jnp.max(scores, 1, keepdims=True))
                shrink = jnp.exp(old - new)
                probs = jnp.exp(scores - new)
                e.top[h, rows, :] = new
                e.total[h, rows, :] = shrink * e.total[h, rows, :] + jnp.sum(
                    probs, 1, keepdims=True
                )
                e.acc[h, rows, :] = shrink * e.acc[h, rows, :] + dot_nt(
                    probs.astype(BF16), values
                )
            return carry

        lax.fori_loop(0, S // TQ, tile, 0)

    @pl.when(me_c < C - 1)
    def _():
        kv_right(me_c).start()

    @pl.when(me_c > 0)
    def _():
        kv_left(me_c).start()

    make_queries()
    attend(me_c)

    def kv_step(s, carry):
        from_left = me_c - s
        from_right = me_c + s

        @pl.when(from_left >= 0)
        def _():
            kv_right(from_left).wait_recv()

            @pl.when(me_c < C - 1)
            def _():
                kv_right(from_left).start()

        @pl.when(from_right < C)
        def _():
            kv_left(from_right).wait_recv()

            @pl.when(me_c > 0)
            def _():
                kv_left(from_right).start()

        @pl.when(s == min(2, C - 1))
        def _():
            weight_start("w2", "inner")
            weight_start("w3", "inner")

        @pl.when(from_left >= 0)
        def _():
            attend(from_left)

        @pl.when(from_right < C)
        def _():
            attend(from_right)

        return carry

    lax.fori_loop(1, C, kv_step, 0)

    def kv_close(b, carry):
        @pl.when((b <= me_c) & (me_c < C - 1))
        def _():
            kv_right(b).wait_send()

        @pl.when((b >= me_c) & (me_c > 0))
        def _():
            kv_left(b).wait_send()

        return carry

    lax.fori_loop(0, C, kv_close, 0)
    weight_start("w2", "outer")
    weight_start("w3", "outer")

    for h in range(NH):
        inverse = 1.0 / e.total[h]
        e.total[h] = inverse
        context = e.acc[h] * inverse
        e.acc[h] = context
        e.ctx[:, h * HS : (h + 1) * HS] = context.astype(BF16)

    for i in range(1, C):
        vec_copy(i).wait_recv()
    for c in range(C):
        e.vecs[:, c * RB : (c + 1) * RB] = e.vecr[c][:, :RB]

    def vector(at):
        return e.vecs[at : at + 1, :]

    def blk_rows(rb):
        return pl.ds(pl.multiple_of(rb * T, T), T)

    for i in list(range(1, R)) + [0]:
        rb = lax.rem(me_r + i, R)
        part = dot_nt(e.ctx[blk_rows(rb), :], e.mix[...])
        if i:
            e.stage[0, i - 1] = part.astype(BF16)
            copy(e.stage.at[0, i - 1], e.landing.at[0, i - 1], "mix", i, to_row(i)).start()
        else:
            e.own[...] = part

    def collect(number, family):
        total = e.own[...]
        for i in range(1, R):
            copy(e.stage.at[number, i - 1], e.landing.at[number, i - 1], family, i, to_row(i)).wait_recv()
            total = total + e.landing[number, i - 1].astype(F32)
        return total

    first_sum = turned(e.x_t[...]) + collect(0, "mix") + vector(0)
    normed, scale = normalize(first_sum)
    hidden = normed * vector(1) + vector(2)
    e.n1[...] = normed
    e.r1[...] = scale
    e.hidden[...] = hidden
    e.hid_g[me_r] = hidden.astype(BF16)

    def share(ref, family, i):
        return copy(ref.at[me_r], ref.at[me_r], family, i, to_row(i))

    for i in range(1, R):
        share(e.hid_g, "hid", i).start()
    weight_share("w2")
    weight_end("w2")

    def spread(number, family, part, i, rb):
        if i:
            e.stage[number, i - 1] = part.astype(BF16)
            copy(
                e.stage.at[number, i - 1], e.landing.at[number, i - 1], family, i, to_row(R - i)
            ).start()
        else:
            e.own[...] = part

    for i in range(R):
        rb = lax.rem(me_r - i + R, R)
        if i:
            share(e.hid_g, "hid", i).wait_recv()
        inner = dot_nn(e.hid_g[rb], w2f[...]) + e.bias[...]
        cdf = 0.5 * (1.0 + lax.erf(inner * (0.5**0.5)))
        active = (inner * cdf).astype(BF16)
        slope = cdf + inner * (jnp.exp(-0.5 * inner * inner) * 0.3989422804014327)
        e.active[blk_rows(rb), :] = active
        e.slope[blk_rows(rb), :] = slope
        if i == 0:
            weight_share("w3")
            weight_end("w3")
        spread(1, "red", dot_nt(e.active[blk_rows(rb), :], w3f[...]), i, rb)
    for i in range(R):
        rb = lax.rem(me_r - i + R, R)
        e.hid_t[:, blk_rows(rb)] = turned(e.hid_g[rb]).astype(BF16)

    second_sum = e.hidden[...] + collect(1, "red") + vector(3)
    normed, scale = normalize(second_sum)
    slot = lax.broadcasted_iota(jnp.int32, (T, 1), 0) + (me_r * (T * C) + me_c * T)
    row_valid = (slot < length).astype(F32)
    upstream = turned(e.out_grad[...]) * row_valid
    g_second = normalize_back(upstream, normed, scale, vector(4))
    g_reduced = g_second.astype(BF16)
    e.gr_g[me_r] = g_reduced
    for i in range(1, R):
        share(e.gr_g, "gr", i).start()
    e.layer_out[...] = ((normed * vector(4) + vector(5)) * row_valid).T.astype(BF16)
    e.g_second[...] = g_second
    e.gv[4:5, :] = column_sum(upstream * normed)
    e.gv[5:6, :] = column_sum(upstream)
    e.gv[3:4, :] = column_sum(g_reduced.astype(F32))
    e.gv[7:8, :] = jnp.zeros((1, D), F32)

    unit_sum = jnp.zeros((1, U), F32)
    for i in range(R):
        rb = lax.rem(me_r - i + R, R)
        if i:
            share(e.gr_g, "gr", i).wait_recv()
        g_active = dot_nn(e.gr_g[rb], w3f[...]).astype(BF16).astype(F32)
        g_inner = (g_active * e.slope[blk_rows(rb), :]).astype(BF16)
        e.g_inner[blk_rows(rb), :] = g_inner
        unit_sum = unit_sum + column_sum(g_inner.astype(F32))
        spread(2, "gh", dot_nt(e.g_inner[blk_rows(rb), :], w2f[...]), i, rb)
    e.gu[0:1, :] = unit_sum
    for i in range(R):
        rb = lax.rem(me_r - i + R, R)
        e.gr_t[:, blk_rows(rb)] = turned(e.gr_g[rb]).astype(BF16)

    TR = dims.TR

    def half_rows(c, d):
        if not dims.flat:
            return pl.ds(c * RB, RB)
        return pl.ds(pl.multiple_of(c * RB + d * HB, HB), HB)

    def other_copy(name):
        return copy(getattr(e, name + "_out"), getattr(e, name + "_in"), name + "_dp", 0, partner)

    def d_copy(name, i):
        stage = getattr(e, name + "_in").at[lax.rem(me_c + i, C)]
        return copy(stage, getattr(e, name + "_land").at[i], name, i, to_col(i))

    def row_tiles(fill):
        def tile(t, carry):
            fill(pl.ds(pl.multiple_of(t * TR, TR), TR))
            return carry

        lax.fori_loop(0, D // TR, tile, 0)

    def weight_swap(name, source):
        def block(c, carry):
            getattr(e, name + "_out")[c] = source[half_rows(c, 1 - me_d), :].astype(BF16)
            return carry

        lax.fori_loop(0, C, block, 0)
        other_copy(name).start()

    def weight_send(name, source):
        other_copy(name).wait_recv()

        def block(c, carry):
            total = source[half_rows(c, me_d), :] + getattr(e, name + "_in")[c].astype(F32)
            getattr(e, name + "_in")[c] = total.astype(BF16)
            return carry

        lax.fori_loop(0, C, block, 0)
        for i in range(1, C):
            d_copy(name, i).start()

    def result_part(name):
        full = getattr(e, name + "_sum")
        return full.at[pl.ds(pl.multiple_of(me_d * HB, HB), HB)] if dims.flat else full

    def result_copy(name):
        return copy(result_part(name), result_part(name), name + "_out", 0, partner)

    def weight_collect(name):
        total = getattr(e, name + "_in")[me_c].astype(F32)
        for i in range(1, C):
            d_copy(name, i).wait_recv()
            total = total + getattr(e, name + "_land")[i].astype(F32)
        result_part(name)[...] = total
        if dims.flat:
            result_copy(name).start()

    def fill_reduce(rows):
        e.dw_f[rows, :] = dot_nn(e.gr_t[rows, :], e.active[...])

    def fill_expand(rows):
        e.dw_f[rows, :] = dot_nn(e.hid_t[rows, :], e.g_inner[...])

    row_tiles(fill_reduce)
    weight_swap("dw3", e.dw_f)
    weight_send("dw3", e.dw_f)
    row_tiles(fill_expand)
    weight_swap("dw2", e.dw_f)
    weight_send("dw2", e.dw_f)

    g_hidden = collect(2, "gh") + e.g_second[...]
    normed = e.n1[...]
    g_first = normalize_back(g_hidden, normed, e.r1[...], vector(1))
    g_mixed = g_first.astype(BF16)
    for i in range(1, R):
        share(e.hid_g, "hid", i).wait_send()
    e.hid_g[me_r] = g_mixed
    for i in range(1, R):
        share(e.hid_g, "gm", i).start()
    e.g_first[...] = g_first
    e.gv[1:2, :] = column_sum(g_hidden * normed)
    e.gv[2:3, :] = column_sum(g_hidden)
    e.gv[0:1, :] = column_sum(g_mixed.astype(F32))
    e.gv[6:7, :] = jnp.zeros((1, D), F32)

    def gv_dp():
        return copy(e.gall.at[0], e.gall.at[1], "gv_dp", 0, partner)

    e.gall[0, 0:8, :D] = e.gv[...]
    e.gall[0, 8:16, :U] = jnp.broadcast_to(e.gu[0:1, :], (8, U))
    gv_dp().start()

    for i in range(R):
        rb = lax.rem(me_r - i + R, R)
        if i:
            share(e.hid_g, "gm", i).wait_recv()
        rows = blk_rows(rb)
        g_context = dot_nn(e.hid_g[rb], e.mix[...]).astype(BF16).astype(F32)
        e.gc_t[:, rows] = g_context.T.astype(BF16)
        for h in range(NH):
            part = g_context[:, h * HS : (h + 1) * HS]
            e.gc_h[h, rows, :] = part.astype(BF16)
            e.inner_sum[h, rows, :] = jnp.sum(part * e.acc[h, rows, :], 1, keepdims=True)
        e.gr_t[:, rows] = turned(e.hid_g[rb]).astype(BF16)

    gv_dp().wait_recv()
    e.gall[2] = e.gall[0] + e.gall[1]

    def gv_col(i):
        return copy(e.gall.at[2], e.gcol.at[i], "gv_col", i, to_col(i))

    for i in range(1, C):
        gv_col(i).start()

    e.dq[...] = jnp.zeros(e.dq.shape, F32)

    def attend_back(b, to):
        valid = key_valid(b)
        for h in range(NH):
            krows = slice(h * HS, (h + 1) * HS)
            vrows = slice(F + h * HS, F + (h + 1) * HS)

            def tile(t, carry):
                d_keys, d_values = carry
                rows = pl.ds(pl.multiple_of(t * TQ, TQ), TQ)
                keys = e.kv[b, krows, :]
                values = e.kv[b, vrows, :]
                scores = dot_nn(e.q_h[h, rows, :], keys)
                scores = jnp.where(valid, scores, NEGATIVE)
                probs = jnp.exp(scores - e.top[h, rows, :]) * e.total[h, rows, :]
                g_weights = dot_nn(e.gc_h[h, rows, :], values)
                g_scores = (probs * (g_weights - e.inner_sum[h, rows, :])).astype(BF16)
                e.dq[h, rows, :] += dot_nt(g_scores, keys)
                d_keys = d_keys + dot_nn(e.q_t[krows, rows], g_scores)
                d_values = d_values + dot_nn(e.gc_t[krows, rows], probs.astype(BF16))
                return d_keys, d_values

            zero = jnp.zeros((HS, S), F32)
            d_keys, d_values = lax.fori_loop(0, S // TQ, tile, (zero, zero))
            e.dkv[to, krows, :] = d_keys
            e.dkv[to, vrows, :] = d_values

    NB = dims.NB

    def dkv_right(b):
        return copy(
            e.kv.at[b], e.dkv_in.at[0, lax.rem(C - 1 - b, NB)], "dkv_right", b, right
        )

    def dkv_left(b):
        return copy(e.kv.at[b], e.dkv_in.at[1, lax.rem(b, NB)], "dkv_left", b, left)

    def dkv_send(way, b):
        order = C - 1 - b if way == 0 else b
        if C - 1 > NB:

            @pl.when(order >= NB)
            def _():
                pl.semaphore_wait(e.credits.at[way], 1)

        if way == 0:

            @pl.when(b < C - 1)
            def _():
                dkv_right(b + 1).wait_send()

            dkv_right(b).start()
        else:

            @pl.when(b > 0)
            def _():
                dkv_left(b - 1).wait_send()

            dkv_left(b).start()

    def dkv_take(way, b, to):
        order = C - 1 - b if way == 0 else b
        (dkv_right if way == 0 else dkv_left)(b).wait_recv()
        e.dkv[to] += e.dkv_in[way, lax.rem(order, NB)].astype(F32)
        if C - 1 > NB:
            sends = C - me_c if way == 0 else me_c + 1

            @pl.when(order + NB < sends)
            def _():
                pl.semaphore_signal(
                    e.credits.at[way],
                    inc=1,
                    device_id=left if way == 0 else right,
                    device_id_type=MESH,
                )

    inner_device = (me_c > 0) & (me_c < C - 1)

    @pl.when(inner_device)
    def _():
        attend_back(me_c, 2)

    def dkv_step(s, carry):
        from_left = C - 1 + me_c - s
        from_right = s - (C - 1 - me_c)

        @pl.when(s >= me_c)
        def _():
            attend_back(from_left, 0)

        @pl.when(from_right >= 0)
        def _():
            attend_back(from_right, 1)

        @pl.when(s >= me_c)
        def _():
            @pl.when(me_c > 0)
            def _():
                dkv_take(0, from_left, 0)

            e.kv[from_left] = e.dkv[0].astype(BF16)
            dkv_send(0, from_left)

        @pl.when(from_right >= 0)
        def _():
            @pl.when(me_c < C - 1)
            def _():
                dkv_take(1, from_right, 1)

            e.kv[from_right] = e.dkv[1].astype(BF16)
            dkv_send(1, from_right)

        return carry

    lax.fori_loop(0, C - 1, dkv_step, 0)

    @pl.when(jnp.logical_not(inner_device))
    def _():
        attend_back(me_c, 2)

    for h in range(NH):
        e.dqkv[h * HS : (h + 1) * HS, :] = (e.dq[h] * (HS ** (-0.5))).T.astype(BF16)

    def fill_query(rows):
        e.dw_s[rows, :F] = dot_nt(e.x_rows_t[rows, :], e.dqkv[:F, :])
        e.dw_s[rows, F:] = dot_nn(e.gr_t[rows, :], e.ctx[...])

    row_tiles(fill_query)
    weight_swap("dwqm", e.dw_s)
    weight_send("dwqm", e.dw_s)
    weight_collect("dw3")
    weight_collect("dw2")

    for i in range(1, C):
        gv_col(i).wait_recv()
    gsum = e.gall[2]
    for i in range(1, C):
        gsum = gsum + e.gcol[i]
    e.gsum[...] = gsum

    def gv_row(i):
        return copy(e.gsum.at[pl.ds(0, 8)], e.grow.at[i], "gv_row", i, to_row(i))

    for i in range(1, R):
        gv_row(i).start()

    @pl.when(me_c > 0)
    def _():
        dkv_take(0, me_c, 2)

    @pl.when(me_c < C - 1)
    def _():
        dkv_take(1, me_c, 2)

    e.dqkv[F : 3 * F, :] = e.dkv[2].astype(BF16)

    for i in list(range(1, R)) + [0]:
        rb = lax.rem(me_r + i, R)
        part = dot_nn(wqm[:, :F], e.dqkv[:F, blk_rows(rb)]) + dot_nn(
            wkv[...], e.dqkv[F:, blk_rows(rb)]
        )
        if i:
            e.dx_stage[i - 1] = part.astype(BF16)
            copy(e.dx_stage.at[i - 1], e.dx_land.at[i - 1], "dx", i, to_row(i)).start()
        else:
            e.dx_own[...] = part

    def fill_keys(rows):
        e.dw_s[rows, :] = dot_nt(e.x_rows_t[rows, :], e.dqkv[F:, :])

    row_tiles(fill_keys)
    weight_swap("dwkv", e.dw_s)
    e.ab[0] = dot_nt(jnp.ones((8, S), BF16), e.dqkv[...])

    def ab_dp():
        return copy(e.ab.at[0], e.ab.at[1], "ab_dp", 0, partner)

    def ab_col(i):
        return copy(e.ab.at[2], e.abcol.at[i], "ab_col", i, to_col(i))

    ab_dp().start()
    weight_send("dwkv", e.dw_s)
    ab_dp().wait_recv()
    e.ab[2] = e.ab[0] + e.ab[1]
    for i in range(1, C):
        ab_col(i).start()

    weight_collect("dwqm")

    total = e.dx_own[...] + e.g_first[...].T
    for i in range(1, R):
        copy(e.dx_stage.at[i - 1], e.dx_land.at[i - 1], "dx", i, to_row(i)).wait_recv()
        total = total + e.dx_land[i - 1].astype(F32)
    e.grad_input[...] = total

    vsum = e.gsum[0:8, :D]
    for i in range(1, R):
        gv_row(i).wait_recv()
        vsum = vsum + e.grow[i][:, :D]
    mine = vsum[:, :RB]
    for c in range(1, C):
        mine = jnp.where(me_c == c, vsum[:, c * RB : (c + 1) * RB], mine)
    e.g_vec[...] = mine
    e.g_unit[...] = e.gsum[8:9, :U]
    asum = e.ab[2]
    for i in range(1, C):
        ab_col(i).wait_recv()
        asum = asum + e.abcol[i]
    e.g_ab[0:1, :] = asum[0:1, :F]
    e.g_ab[1:2, :] = asum[0:1, 2 * F :]
    weight_collect("dwkv")
    if dims.flat:
        for name in ("dw3", "dw2", "dwqm", "dwkv"):
            result_copy(name).wait_recv()
    e.g_attn[0] = e.dwqm_sum[:, :F]
    e.g_mix[...] = e.dwqm_sum[:, F:]
    e.g_attn[1] = e.dwkv_sum[:, :F]
    e.g_attn[2] = e.dwkv_sum[:, F:]

    for name in ("wkv", "wqm", "w2", "w3"):
        weight_close(name)
    for i in range(1, R):
        x_copy(i).wait_send()
        copy(e.stage.at[0, i - 1], e.landing.at[0, i - 1], "mix", i, to_row(i)).wait_send()
        copy(e.stage.at[1, i - 1], e.landing.at[1, i - 1], "red", i, to_row(i)).wait_send()
        share(e.gr_g, "gr", i).wait_send()
        copy(e.stage.at[2, i - 1], e.landing.at[2, i - 1], "gh", i, to_row(i)).wait_send()
        share(e.hid_g, "gm", i).wait_send()
        copy(e.dx_stage.at[i - 1], e.dx_land.at[i - 1], "dx", i, to_row(i)).wait_send()
        gv_row(i).wait_send()
    gv_dp().wait_send()
    ab_dp().wait_send()
    for i in range(1, C):
        vec_copy(i).wait_send()
        gv_col(i).wait_send()
        ab_col(i).wait_send()
    for name in ("dw3", "dw2", "dwqm", "dwkv"):
        other_copy(name).wait_send()
        for i in range(1, C):
            d_copy(name, i).wait_send()
        if dims.flat:
            result_copy(name).wait_send()

    @pl.when(me_c < C - 1)
    def _():
        dkv_right(me_c + 1).wait_send()

    @pl.when(me_c > 0)
    def _():
        dkv_left(me_c - 1).wait_send()


def run_layer(x_t, length, w_attn, w_mixer, w2, w3, out_grad, b_attn, b_expand, **vectors):
    R = lax.axis_size("row")
    C = lax.axis_size("col")
    T = x_t.shape[1]
    S = T * R
    F = w_mixer.shape[1]
    U = w2.shape[1]
    RB = w_mixer.shape[0]
    flat = RB % 32 == 0
    HS = D // H
    dims = SimpleNamespace(
        R=R, C=C, T=T, S=S, F=F, U=U, RB=RB, HS=HS, NH=F // HS,
        flat=flat, HB=RB // 2 if flat else RB, TQ=min(256, S), TR=256, NB=min(C - 1, 3),
    )
    HB = dims.HB
    NH = dims.NH
    slots = slots_of(R, C)
    wide = max(D, U)
    w_shape = (lambda n: (C * RB, n)) if dims.flat else (lambda n: (C, RB, n))
    inputs = dict(
        x_t=x_t, length=length, w_attn=w_attn, w_mixer=w_mixer, w2=w2, w3=w3, out_grad=out_grad,
        b_attn=b_attn, b_expand=b_expand, **vectors,
    )
    outputs = dict(
        layer_out=((D, T), BF16),
        grad_input=((D, T), F32),
        g_attn=((3, RB, F), F32),
        g_mix=((RB, F), F32),
        dw2_sum=((RB, U), F32),
        dw3_sum=((RB, U), F32),
        g_vec=((8, RB), F32),
        g_unit=((1, U), F32),
        g_ab=((2, F), F32),
    )
    scratch = dict(
        xg=((R, T, D), BF16),
        wkv=((RB, 2 * F), BF16),
        wqm=((RB, 2 * F), BF16),
        wkv_g=(w_shape(2 * F), BF16),
        wqm_g=(w_shape(2 * F), BF16),
        w2_g=(w_shape(U), BF16),
        w3_g=(w_shape(U), BF16),
        mix=((D, F), BF16),
        vecr=((C, 8, F), F32),
        vecs=((8, D), F32),
        bias=((1, U), F32),
        kv=((C, 2 * F, S), BF16),
        q_t=((F, S), BF16),
        q_h=((NH, S, HS), BF16),
        x_rows_t=((D, S), BF16),
        top=((NH, S, 1), F32),
        total=((NH, S, 1), F32),
        acc=((NH, S, HS), F32),
        ctx=((S, F), BF16),
        stage=((3, R - 1, T, D), BF16),
        landing=((3, R - 1, T, D), BF16),
        own=((T, D), F32),
        n1=((T, D), F32),
        r1=((T, 1), F32),
        hidden=((T, D), F32),
        hid_g=((R, T, D), BF16),
        active=((S, U), BF16),
        slope=((S, U), F32),
        hid_t=((D, S), BF16),
        g_second=((T, D), F32),
        gr_g=((R, T, D), BF16),
        gr_t=((D, S), BF16),
        g_inner=((S, U), BF16),
        gv=((8, D), F32),
        gu=((8, U), F32),
        gall=((3, 16, wide), F32),
        gcol=((C, 16, wide), F32),
        gsum=((16, wide), F32),
        grow=((R, 8, wide), F32),
        dw_f=((D, U), F32),
        dw_s=((D, 2 * F), F32),
        dwqm_sum=((RB, 2 * F), F32),
        dwkv_sum=((RB, 2 * F), F32),
        g_first=((T, D), F32),
        gc_t=((F, S), BF16),
        gc_h=((NH, S, HS), BF16),
        inner_sum=((NH, S, 1), F32),
        dq=((NH, S, HS), F32),
        dkv=((3, 2 * F, S), F32),
        dkv_in=((2, dims.NB, 2 * F, S), BF16),
        dqkv=((3 * F, S), BF16),
        dx_stage=((R - 1, D, T), BF16),
        dx_land=((R - 1, D, T), BF16),
        dx_own=((D, T), F32),
        ab=((3, 8, 3 * F), F32),
        abcol=((C, 8, 3 * F), F32),
    )
    for name, width in (("wkv", 2 * F), ("wqm", 2 * F), ("w2", U), ("w3", U)):
        for part in ("out", "in", "land"):
            scratch["d" + name + "_" + part] = ((C, HB, width), BF16)
        if not dims.flat:
            scratch[name + "_f"] = ((C * RB, width), BF16)
    names = list(inputs) + list(outputs) + list(scratch) + ["send_sems", "recv_sems", "credits"]
    vmem = pl.BlockSpec(memory_space=pltpu.VMEM)
    in_specs = [
        pl.BlockSpec(memory_space=pltpu.SMEM) if name == "length" else vmem for name in inputs
    ]
    results = pl.pallas_call(
        functools.partial(layer_kernel, dims, names),
        out_shape=[jax.ShapeDtypeStruct(s, t) for s, t in outputs.values()],
        in_specs=in_specs,
        out_specs=[vmem] * len(outputs),
        scratch_shapes=[pltpu.VMEM(s, t) for s, t in scratch.values()]
        + [pltpu.SemaphoreType.DMA((slots.total,)), pltpu.SemaphoreType.DMA((slots.total,))]
        + [pltpu.SemaphoreType.REGULAR((2,))],
        compiler_params=pltpu.CompilerParams(
            collective_id=0, has_side_effects=True, vmem_limit_bytes=63 * 2**20
        ),
        name="layer",
    )(*inputs.values())
    return dict(zip(outputs, results))


def finish_kernel(*refs):
    big_in, rows, unit, big_out, vecs, unit_out = (
        refs[:7], refs[7], refs[8], refs[9:16], refs[16:22], refs[22],
    )
    for src, dst in zip(big_in, big_out):
        dst[...] = src[...]
    for k, ref in enumerate(vecs):
        ref[...] = rows[k : k + 1, :].reshape(ref.shape)
    unit_out[...] = unit[...].reshape(unit_out.shape)


def finish(out):
    big = [
        out[name]
        for name in ("layer_out", "grad_input", "g_attn", "g_mix", "dw2_sum", "dw3_sum", "g_ab")
    ]
    rows = out["g_vec"].shape[1]
    units = out["g_unit"].shape[1]
    vmem = pl.BlockSpec(memory_space=pltpu.VMEM)
    shapes = [jax.ShapeDtypeStruct(a.shape, a.dtype) for a in big]
    shapes += [jax.ShapeDtypeStruct((rows,), F32)] * 6 + [jax.ShapeDtypeStruct((units,), F32)]
    return pl.pallas_call(
        finish_kernel,
        out_shape=shapes,
        in_specs=[vmem] * 9,
        out_specs=[vmem] * 14,
        name="finish",
    )(*big, out["g_vec"], out["g_unit"])


def on_device(
    layer_in,
    lengths,
    w_attn,
    b_attn,
    w_mixer,
    b_mixer,
    gain_one,
    shift_one,
    w_expand,
    b_expand,
    w_reduce,
    b_reduce,
    gain_two,
    shift_two,
    out_grad,
):
    out = run_layer(
        layer_in,
        lengths,
        jnp.transpose(w_attn, (1, 0, 2)),
        w_mixer,
        w_expand,
        w_reduce,
        out_grad,
        b_attn,
        b_expand,
        b_mixer=b_mixer,
        gain_one=gain_one,
        shift_one=shift_one,
        b_reduce=b_reduce,
        gain_two=gain_two,
        shift_two=shift_two,
    )
    layer_out, grad_input, g_attn, g_mix, g_expand, g_reduce, g_ab, *vecs, g_unit = finish(out)
    return (
        layer_out,
        grad_input,
        jnp.transpose(g_attn, (1, 0, 2)),
        g_ab,
        g_mix,
        vecs[0],
        vecs[1],
        vecs[2],
        g_expand,
        g_unit,
        g_reduce,
        vecs[3],
        vecs[4],
        vecs[5],
    )


def solution(mesh):
    return jax.shard_map(
        on_device,
        mesh=mesh,
        in_specs=(
            P(None, ("dp", "row", "col")),
            P("dp"),
            P("col", None, "row"),
            P(None, "row"),
            P("col", "row"),
            P("col"),
            P("col"),
            P("col"),
            P("col", "row"),
            P("row"),
            P("col", "row"),
            P("col"),
            P("col"),
            P("col"),
            P(None, ("dp", "row", "col")),
        ),
        out_specs=(
            P(None, ("dp", "row", "col")),
            P(None, ("dp", "row", "col")),
            P("col", None, "row"),
            P(None, "row"),
            P("col", "row"),
            P("col"),
            P("col"),
            P("col"),
            P("col", "row"),
            P("row"),
            P("col", "row"),
            P("col"),
            P("col"),
            P("col"),
        ),
        check_vma=False,
    )
```

```python
import functools
from types import SimpleNamespace

import jax
import jax.numpy as jnp
from jax import lax
from jax.experimental import pallas as pl
from jax.experimental.pallas import tpu as pltpu
from jax.sharding import PartitionSpec as P

D = 768
H = 12
EPSILON = 1e-12
NEGATIVE = -1000000000.0
MESH = pl.DeviceIdType.MESH
F32 = jnp.float32
BF16 = jnp.bfloat16


def dot_nn(left_in, right_in):
    return lax.dot_general(
        left_in, right_in, (((1,), (0,)), ((), ())), preferred_element_type=F32
    )


def dot_nt(left_in, right_in):
    return lax.dot_general(
        left_in, right_in, (((1,), (1,)), ((), ())), preferred_element_type=F32
    )


def turned(values):
    return values.astype(F32).T


def normalize(values):
    row_mean = jnp.mean(values, 1, keepdims=True)
    centered = values - row_mean
    row_var = jnp.mean(centered * centered, 1, keepdims=True)
    row_scale = lax.rsqrt(row_var + EPSILON)
    return centered * row_scale, row_scale


def normalize_back(upstream, normed, row_scale, gain_vec):
    scaled = upstream * gain_vec
    mean_plain = jnp.mean(scaled, 1, keepdims=True)
    mean_cross = jnp.mean(scaled * normed, 1, keepdims=True)
    return row_scale * (scaled - mean_plain - normed * mean_cross)


def column_sum(values):
    return jnp.sum(values, 0, keepdims=True)


class Slots:
    def __init__(self):
        self.base = {}
        self.total = 0

    def add(self, name, count):
        self.base[name] = self.total
        self.total += count


def slots_of(R, C):
    slots = Slots()
    for name in ("x", "hid", "gr", "gm"):
        slots.add(name, 4)
    for name in ("mix", "red", "gh", "dx"):
        slots.add(name, 3)
    slots.add("gv_row", R)
    for name in ("vec", "gv_col", "ab_col", "kv_right", "kv_left", "dkv_right", "dkv_left"):
        slots.add(name, C)
    for name in ("wkv", "wqm", "w2", "w3"):
        slots.add(name, C)
        slots.add(name + "_dp", C)
        slots.add("d" + name, C)
        slots.add("d" + name + "_dp", 1)
        slots.add("d" + name + "_out", 1)
    for name in ("kv_pass", "dkv_pass"):
        slots.add(name, C)
    for name in ("gv_dp", "ab_dp", "len"):
        slots.add(name, 1)
    slots.add("swap", 4)
    return slots


def layer_kernel(dims, names, *refs):
    e = SimpleNamespace(**dict(zip(names, refs)))
    R, C, T, S, F, U, RB = dims.R, dims.C, dims.T, dims.S, dims.F, dims.U, dims.RB
    NH, HS, HB = dims.NH, dims.HS, dims.HB
    slots = slots_of(R, C)
    me_d = lax.axis_index("dp")
    me_r = lax.axis_index("row")
    me_c = lax.axis_index("col")

    def to_row(step):
        return {"row": lax.rem(me_r + step, R)}

    def to_col(step):
        return {"col": lax.rem(me_c + step, C)}

    partner = {"dp": 1 - me_d}

    HC = C // 2
    half, place = me_c // HC, lax.rem(me_c, HC)
    mine = me_d * HC + place
    swapped = me_d != half
    stays = me_d == half

    def swap_copy(src, dst, at):
        where = {"dp": 1 - me_d, "col": lax.rem(me_c + HC, C)}
        return copy(src, dst, "swap", at, where)

    def copy(src, dst, family, at, where):
        number = slots.base[family] + at
        return pltpu.make_async_remote_copy(
            src_ref=src,
            dst_ref=dst,
            send_sem=e.send_sems.at[number],
            recv_sem=e.recv_sems.at[number],
            device_id=where,
            device_id_type=MESH,
        )

    barrier = pltpu.get_barrier_semaphore()
    pl.semaphore_signal(barrier, inc=1, device_id=partner, device_id_type=MESH)
    for i in range(1, R):
        pl.semaphore_signal(barrier, inc=1, device_id=to_row(i), device_id_type=MESH)
    for i in range(1, C):
        pl.semaphore_signal(barrier, inc=1, device_id=to_col(i), device_id_type=MESH)
    pl.semaphore_signal(
        barrier,
        inc=1,
        device_id={"dp": 1 - me_d, "col": lax.rem(me_c + HC, C)},
        device_id_type=MESH,
    )
    e.wkv[:, :F] = e.w_attn[1]
    e.wkv[:, F:] = e.w_attn[2]
    e.wqm[:, :F] = e.w_attn[0]
    e.wqm[:, F:] = e.w_mixer[...]
    vectors = (e.b_mixer, e.gain_one, e.shift_one, e.b_reduce, e.gain_two, e.shift_two)
    for k, ref in enumerate(vectors):
        e.vecr[me_c, k : k + 1, :RB] = ref[...].astype(F32).reshape(1, RB)
    e.bias[...] = e.b_expand[...].astype(F32).reshape(1, U)
    e.lens[me_d] = jnp.full((8, 128), e.length[0].astype(F32), F32)
    pl.semaphore_wait(barrier, 2 + (R - 1) + (C - 1))

    @pl.when(swapped)
    def _():
        swap_copy(e.x_t, e.x_in, 0).start()

    @pl.when(stays)
    def _():
        e.x_in[...] = e.x_t[...]
        e.og_in[...] = e.out_grad[...]

    def len_copy():
        return copy(e.lens.at[me_d], e.lens.at[me_d], "len", 0, partner)

    len_copy().start()

    def w_rows(ref, c, d):
        if not dims.flat:
            return ref.at[c]
        return ref.at[pl.ds(pl.multiple_of(c * RB + d * HB, HB), HB)]

    def weight_copy(name, i):
        own = getattr(e, name)
        if dims.flat:
            own = own.at[pl.ds(pl.multiple_of(me_d * HB, HB), HB)]
        return copy(own, w_rows(getattr(e, name + "_g"), me_c, me_d), name, i, to_col(i))

    def weight_pass(name, i):
        there = w_rows(getattr(e, name + "_g"), lax.rem(me_c - i + C, C), me_d)
        return copy(there, there, name + "_dp", i, partner)

    def weight_start(name):
        for i in range(1, C):
            weight_copy(name, i).start()

    def weight_own(name):
        full = getattr(e, name + "_g")
        if dims.flat:
            full[pl.ds(pl.multiple_of(me_c * RB, RB), RB), :] = getattr(e, name)[...]
        else:
            full[me_c] = getattr(e, name)[...]

    def weight_share(name):
        for i in range(1, C):
            weight_copy(name, i).wait_recv()
            if dims.flat:
                weight_pass(name, i).start()

    def weight_end(name):
        if dims.flat:
            for i in range(1, C):
                weight_pass(name, i).wait_recv()
        else:
            full = getattr(e, name + "_g")
            flat = full[...].astype(F32).reshape(C * RB, full.shape[2])
            getattr(e, name + "_f")[...] = flat.astype(BF16)

    def weight_close(name):
        for i in range(1, C):
            weight_copy(name, i).wait_send()
            if dims.flat:
                weight_pass(name, i).wait_send()

    wkv, wqm, w2f, w3f = [
        getattr(e, name + ("_g" if dims.flat else "_f")) for name in ("wkv", "wqm", "w2", "w3")
    ]

    beside = {"row": me_r + 1 - 2 * lax.rem(me_r, 2)}
    across = {"row": lax.rem(me_r + 2, R)}
    near, over, far = beside["row"], across["row"], R - 1 - me_r
    low, high = pl.ds(0, T // 2), pl.ds(T // 2, T // 2)

    def gather_copy(ref, family, at):
        part, where = (
            (ref.at[me_r], beside),
            (ref.at[me_r], across),
            (ref.at[near, low], across),
            (ref.at[over, high], beside),
        )[at]
        return copy(part, part, family, at, where)

    def gather_start(ref, family):
        gather_copy(ref, family, 0).start()
        gather_copy(ref, family, 1).start()

    def gather_near(ref, family):
        gather_copy(ref, family, 0).wait_recv()
        gather_copy(ref, family, 2).start()

    def gather_over(ref, family):
        gather_copy(ref, family, 1).wait_recv()
        gather_copy(ref, family, 3).start()

    def gather_far(ref, family):
        gather_copy(ref, family, 2).wait_recv()
        gather_copy(ref, family, 3).wait_recv()

    def gather_close(ref, family):
        for at in range(4):
            gather_copy(ref, family, at).wait_send()

    def gathered(ref, family):
        yield "own", me_r
        gather_near(ref, family)
        gather_over(ref, family)
        yield "near", near
        yield "over", over
        gather_far(ref, family)
        yield "far", far

    def sum_copy(k, family, kind):
        at = ("near", "over", "far").index(kind)
        where = (beside, across, {"row": far})[at]
        out, land, _ = e.sums[k]
        return copy(out.at[at], land.at[at], family, at, where)

    def sum_add(k, family, kind, part):
        out, _, own = e.sums[k]
        if kind == "own":
            own[...] = part
        else:
            out[("near", "over", "far").index(kind)] = part.astype(BF16)
            sum_copy(k, family, kind).start()

    def sum_collect(k, family):
        _, land, own = e.sums[k]
        total = own[...]
        for at, kind in enumerate(("near", "over", "far")):
            sum_copy(k, family, kind).wait_recv()
            total = total + land[at].astype(F32)
        return total

    def sum_close(k, family):
        for kind in ("near", "over", "far"):
            sum_copy(k, family, kind).wait_send()

    e.sums = [
        (getattr(e, f"out_{k}"), getattr(e, f"land_{k}"), own)
        for k, own in ((0, e.own_0), (1, e.own_1), (0, e.own_0), (2, e.own_dx))
    ]

    def vec_copy(i):
        return copy(e.vecr.at[me_c], e.vecr.at[me_c], "vec", i, to_col(i))

    weight_start("wkv")
    for name in ("wkv", "wqm", "w2", "w3"):
        weight_own(name)

    @pl.when(swapped)
    def _():
        swap_copy(e.x_t, e.x_in, 0).wait_recv()

    e.xg[me_r] = turned(e.x_in[...]).astype(BF16)
    gather_start(e.xg, "x")
    weight_share("wkv")
    weight_start("wqm")

    @pl.when(swapped)
    def _():
        swap_copy(e.out_grad, e.og_in, 1).start()

    len_copy().wait_recv()
    length = e.lens[half][0:1, 0:1]
    for i in range(1, C):
        vec_copy(i).start()
    weight_end("wkv")

    for _, rb in gathered(e.xg, "x"):
        tokens = pl.ds(pl.multiple_of(rb * T, T), T)
        both = dot_nn(e.xg[rb], wkv[...])
        values = both[:, F:] + e.b_attn[1:2, :].astype(F32)
        e.kv[mine, pl.ds(0, F), tokens] = both[:, :F].T.astype(BF16)
        e.kv[mine, pl.ds(F, F), tokens] = values.T.astype(BF16)

    def make_queries():
        weight_share("wqm")
        weight_end("wqm")
        e.mix[...] = wqm[:, F:]
        for i in range(R):
            tokens = pl.ds(i * T, T)
            block = e.xg[i]
            q = dot_nn(block, wqm[:, :F]) + e.b_attn[0:1, :].astype(F32)
            q = q.astype(BF16).astype(F32) * (HS ** (-0.5))
            e.q_t[:, tokens] = q.T.astype(BF16)
            for h in range(NH):
                e.q_h[h, tokens, :] = q[:, h * HS : (h + 1) * HS].astype(BF16)
            e.x_rows_t[:, tokens] = turned(block).astype(BF16)

    right = {"col": lax.rem(me_c + 1, C)}
    left = {"col": lax.rem(me_c + C - 1, C)}

    def kv_right(b):
        return copy(e.kv.at[b], e.kv.at[b], "kv_right", b, right)

    def kv_left(b):
        return copy(e.kv.at[b], e.kv.at[b], "kv_left", b, left)

    def kv_pass(b):
        return copy(e.kv.at[b], e.kv.at[b], "kv_pass", b, partner)

    def key_valid(b):
        lane = lax.broadcasted_iota(jnp.int32, (1, S), 1)
        return (lane // T * (T * C) + b * T + lane % T).astype(F32) < length

    TQ = dims.TQ
    e.top[...] = jnp.full(e.top.shape, -3e38, F32)
    e.total[...] = jnp.zeros(e.total.shape, F32)
    e.acc[...] = jnp.zeros(e.acc.shape, F32)

    def attend(b):
        valid = key_valid(b)

        def tile(t, carry):
            rows = pl.ds(pl.multiple_of(t * TQ, TQ), TQ)
            for h in range(NH):
                keys = e.kv[b, h * HS : (h + 1) * HS, :]
                values = e.kv[b, F + h * HS : F + (h + 1) * HS, :]
                scores = dot_nn(e.q_h[h, rows, :], keys)
                scores = jnp.where(valid, scores, NEGATIVE)
                old = e.top[h, rows, :]
                new = jnp.maximum(old, jnp.max(scores, 1, keepdims=True))
                shrink = jnp.exp(old - new)
                probs = jnp.exp(scores - new)
                e.top[h, rows, :] = new
                e.total[h, rows, :] = shrink * e.total[h, rows, :] + jnp.sum(
                    probs, 1, keepdims=True
                )
                e.acc[h, rows, :] = shrink * e.acc[h, rows, :] + dot_nt(
                    probs.astype(BF16), values
                )
            return carry

        lax.fori_loop(0, S // TQ, tile, 0)

    @pl.when(place < HC - 1)
    def _():
        kv_right(mine).start()

    @pl.when(place > 0)
    def _():
        kv_left(mine).start()

    kv_pass(mine).start()
    make_queries()
    attend(mine)

    def of_core(d, at):
        return d * HC + at

    kv_pass(of_core(1 - me_d, place)).wait_recv()
    attend(of_core(1 - me_d, place))

    def kv_step(s, carry):
        from_left = place - s
        from_right = place + s

        @pl.when(from_left >= 0)
        def _():
            b = of_core(me_d, from_left)
            kv_right(b).wait_recv()
            kv_pass(b).start()

            @pl.when(place < HC - 1)
            def _():
                kv_right(b).start()

        @pl.when(from_right < HC)
        def _():
            b = of_core(me_d, from_right)
            kv_left(b).wait_recv()
            kv_pass(b).start()

            @pl.when(place > 0)
            def _():
                kv_left(b).start()

        @pl.when(s == HC - 1)
        def _():
            weight_start("w2")
            weight_start("w3")

        @pl.when(from_left >= 0)
        def _():
            attend(of_core(me_d, from_left))
            kv_pass(of_core(1 - me_d, from_left)).wait_recv()
            attend(of_core(1 - me_d, from_left))

        @pl.when(from_right < HC)
        def _():
            attend(of_core(me_d, from_right))
            kv_pass(of_core(1 - me_d, from_right)).wait_recv()
            attend(of_core(1 - me_d, from_right))

        return carry

    lax.fori_loop(1, HC, kv_step, 0)

    def kv_close(at, carry):
        b = of_core(me_d, at)
        kv_pass(b).wait_send()

        @pl.when((at <= place) & (place < HC - 1))
        def _():
            kv_right(b).wait_send()

        @pl.when((at >= place) & (place > 0))
        def _():
            kv_left(b).wait_send()

        return carry

    lax.fori_loop(0, HC, kv_close, 0)

    for h in range(NH):
        inverse = 1.0 / e.total[h]
        e.total[h] = inverse
        context = e.acc[h] * inverse
        e.acc[h] = context
        e.ctx[:, h * HS : (h + 1) * HS] = context.astype(BF16)

    for i in range(1, C):
        vec_copy(i).wait_recv()
    for c in range(C):
        e.vecs[:, c * RB : (c + 1) * RB] = e.vecr[c][:, :RB]

    def vector(at):
        return e.vecs[at : at + 1, :]

    def blk_rows(rb):
        return pl.ds(pl.multiple_of(rb * T, T), T)

    for kind, rb in (("far", far), ("near", near), ("over", over), ("own", me_r)):
        sum_add(0, "mix", kind, dot_nt(e.ctx[blk_rows(rb), :], e.mix[...]))

    first_sum = turned(e.x_in[...]) + sum_collect(0, "mix") + vector(0)
    normed, scale = normalize(first_sum)
    hidden = normed * vector(1) + vector(2)
    e.n1[...] = normed
    e.r1[...] = scale
    e.hidden[...] = hidden
    e.hid_g[me_r] = hidden.astype(BF16)

    gather_start(e.hid_g, "hid")
    weight_share("w2")
    weight_end("w2")

    for kind, rb in gathered(e.hid_g, "hid"):
        inner = dot_nn(e.hid_g[rb], w2f[...]) + e.bias[...]
        cdf = 0.5 * (1.0 + lax.erf(inner * (0.5**0.5)))
        active = (inner * cdf).astype(BF16)
        slope = cdf + inner * (jnp.exp(-0.5 * inner * inner) * 0.3989422804014327)
        e.active[blk_rows(rb), :] = active
        e.slope[blk_rows(rb), :] = slope
        if kind == "own":
            continue
        if kind == "near":
            weight_share("w3")
            weight_end("w3")
            sum_add(1, "red", "own", dot_nt(e.active[blk_rows(me_r), :], w3f[...]))
        sum_add(1, "red", kind, dot_nt(e.active[blk_rows(rb), :], w3f[...]))
    for i in range(R):
        e.hid_t[:, i * T : (i + 1) * T] = turned(e.hid_g[i]).astype(BF16)
    gather_close(e.hid_g, "hid")

    second_sum = e.hidden[...] + sum_collect(1, "red") + vector(3)
    normed, scale = normalize(second_sum)
    slot = lax.broadcasted_iota(jnp.int32, (T, 1), 0) + (me_r * (T * C) + mine * T)
    row_valid = (slot.astype(F32) < length).astype(F32)

    @pl.when(swapped)
    def _():
        swap_copy(e.out_grad, e.og_in, 1).wait_recv()

    upstream = turned(e.og_in[...]) * row_valid
    g_second = normalize_back(upstream, normed, scale, vector(4))
    g_reduced = g_second.astype(BF16)
    e.gr_g[me_r] = g_reduced
    gather_start(e.gr_g, "gr")
    e.lo_out[...] = ((normed * vector(4) + vector(5)) * row_valid).T.astype(BF16)

    @pl.when(swapped)
    def _():
        swap_copy(e.lo_out, e.layer_out, 2).start()

    @pl.when(stays)
    def _():
        e.layer_out[...] = e.lo_out[...]

    e.g_second[...] = g_second
    e.gv[4:5, :] = column_sum(upstream * normed)
    e.gv[5:6, :] = column_sum(upstream)
    e.gv[3:4, :] = column_sum(g_reduced.astype(F32))
    e.gv[7:8, :] = jnp.zeros((1, D), F32)

    unit_sum = jnp.zeros((1, U), F32)
    sum_close(0, "mix")
    for kind, rb in gathered(e.gr_g, "gr"):
        g_active = dot_nn(e.gr_g[rb], w3f[...]).astype(BF16).astype(F32)
        g_inner = (g_active * e.slope[blk_rows(rb), :]).astype(BF16)
        e.g_inner[blk_rows(rb), :] = g_inner
        unit_sum = unit_sum + column_sum(g_inner.astype(F32))
        sum_add(2, "gh", kind, dot_nt(e.g_inner[blk_rows(rb), :], w2f[...]))
    e.gu[0:1, :] = unit_sum
    for i in range(R):
        e.gr_t[:, i * T : (i + 1) * T] = turned(e.gr_g[i]).astype(BF16)

    TR = dims.TR

    def half_rows(c, d):
        if not dims.flat:
            return pl.ds(c * RB, RB)
        return pl.ds(pl.multiple_of(c * RB + d * HB, HB), HB)

    def other_copy(name):
        return copy(getattr(e, name + "_out"), getattr(e, name + "_in"), name + "_dp", 0, partner)

    def d_copy(name, i):
        stage = getattr(e, name + "_in").at[lax.rem(me_c + i, C)]
        return copy(stage, getattr(e, name + "_land").at[i], name, i, to_col(i))

    def row_tiles(fill):
        def tile(t, carry):
            fill(pl.ds(pl.multiple_of(t * TR, TR), TR))
            return carry

        lax.fori_loop(0, D // TR, tile, 0)

    def weight_swap(name, source):
        def block(c, carry):
            getattr(e, name + "_out")[c] = source[half_rows(c, 1 - me_d), :].astype(BF16)
            return carry

        lax.fori_loop(0, C, block, 0)
        other_copy(name).start()

    def weight_send(name, source):
        other_copy(name).wait_recv()

        def block(c, carry):
            total = source[half_rows(c, me_d), :] + getattr(e, name + "_in")[c].astype(F32)
            getattr(e, name + "_in")[c] = total.astype(BF16)
            return carry

        lax.fori_loop(0, C, block, 0)
        for i in range(1, C):
            d_copy(name, i).start()

    def result_part(name):
        full = getattr(e, name + "_sum")
        return full.at[pl.ds(pl.multiple_of(me_d * HB, HB), HB)] if dims.flat else full

    def result_copy(name):
        return copy(result_part(name), result_part(name), name + "_out", 0, partner)

    def weight_collect(name):
        total = getattr(e, name + "_in")[me_c].astype(F32)
        for i in range(1, C):
            d_copy(name, i).wait_recv()
            total = total + getattr(e, name + "_land")[i].astype(F32)
        result_part(name)[...] = total
        if dims.flat:
            result_copy(name).start()

    def fill_reduce(rows):
        e.dw_f[rows, :] = dot_nn(e.gr_t[rows, :], e.active[...])

    def fill_expand(rows):
        e.dw_f[rows, :] = dot_nn(e.hid_t[rows, :], e.g_inner[...])

    row_tiles(fill_reduce)
    weight_swap("dw3", e.dw_f)
    weight_send("dw3", e.dw_f)
    row_tiles(fill_expand)
    weight_swap("dw2", e.dw_f)
    weight_send("dw2", e.dw_f)

    g_hidden = sum_collect(2, "gh") + e.g_second[...]
    normed = e.n1[...]
    g_first = normalize_back(g_hidden, normed, e.r1[...], vector(1))
    g_mixed = g_first.astype(BF16)
    e.hid_g[me_r] = g_mixed
    gather_start(e.hid_g, "gm")
    e.g_first[...] = g_first
    e.gv[1:2, :] = column_sum(g_hidden * normed)
    e.gv[2:3, :] = column_sum(g_hidden)
    e.gv[0:1, :] = column_sum(g_mixed.astype(F32))
    e.gv[6:7, :] = jnp.zeros((1, D), F32)

    def gv_dp():
        return copy(e.gall.at[0], e.gall.at[1], "gv_dp", 0, partner)

    e.gall[0, 0:8, :D] = e.gv[...]
    e.gall[0, 8:16, :U] = jnp.broadcast_to(e.gu[0:1, :], (8, U))
    gv_dp().start()

    for _, rb in gathered(e.hid_g, "gm"):
        rows = blk_rows(rb)
        g_context = dot_nn(e.hid_g[rb], e.mix[...]).astype(BF16).astype(F32)
        e.gc_t[:, rows] = g_context.T.astype(BF16)
        for h in range(NH):
            part = g_context[:, h * HS : (h + 1) * HS]
            e.gc_h[h, rows, :] = part.astype(BF16)
            e.inner_sum[h, rows, :] = jnp.sum(part * e.acc[h, rows, :], 1, keepdims=True)
        e.gr_t[:, rows] = turned(e.hid_g[rb]).astype(BF16)

    def gv_col(i):
        return copy(e.gall.at[2], e.gcol.at[i], "gv_col", i, to_col(i))

    e.dq[...] = jnp.zeros(e.dq.shape, F32)

    def attend_back(b, to):
        valid = key_valid(b)
        for h in range(NH):
            krows = slice(h * HS, (h + 1) * HS)
            vrows = slice(F + h * HS, F + (h + 1) * HS)

            def tile(t, carry):
                d_keys, d_values = carry
                rows = pl.ds(pl.multiple_of(t * TQ, TQ), TQ)
                keys = e.kv[b, krows, :]
                values = e.kv[b, vrows, :]
                scores = dot_nn(e.q_h[h, rows, :], keys)
                scores = jnp.where(valid, scores, NEGATIVE)
                probs = jnp.exp(scores - e.top[h, rows, :]) * e.total[h, rows, :]
                g_weights = dot_nn(e.gc_h[h, rows, :], values)
                g_scores = (probs * (g_weights - e.inner_sum[h, rows, :])).astype(BF16)
                e.dq[h, rows, :] += dot_nt(g_scores, keys)
                d_keys = d_keys + dot_nn(e.q_t[krows, rows], g_scores)
                d_values = d_values + dot_nn(e.gc_t[krows, rows], probs.astype(BF16))
                return d_keys, d_values

            zero = jnp.zeros((HS, S), F32)
            d_keys, d_values = lax.fori_loop(0, S // TQ, tile, (zero, zero))
            e.dkv[to, krows, :] = d_keys
            e.dkv[to, vrows, :] = d_values

    NB = dims.NB

    def dkv_right(at):
        b = of_core(me_d, at)
        return copy(
            e.kv.at[b], e.dkv_in.at[0, lax.rem(HC - 1 - at, NB)], "dkv_right", at, right
        )

    def dkv_left(at):
        b = of_core(me_d, at)
        return copy(e.kv.at[b], e.dkv_in.at[1, lax.rem(at, NB)], "dkv_left", at, left)

    def dkv_send(way, at):
        order = HC - 1 - at if way == 0 else at
        if HC - 1 > NB:

            @pl.when(order >= NB)
            def _():
                pl.semaphore_wait(e.credits.at[way], 1)

        if way == 0:

            @pl.when(at < HC - 1)
            def _():
                dkv_right(at + 1).wait_send()

            dkv_right(at).start()
        else:

            @pl.when(at > 0)
            def _():
                dkv_left(at - 1).wait_send()

            dkv_left(at).start()

    def dkv_take(way, at, to):
        order = HC - 1 - at if way == 0 else at
        (dkv_right if way == 0 else dkv_left)(at).wait_recv()
        e.dkv[to] += e.dkv_in[way, lax.rem(order, NB)].astype(F32)
        if HC - 1 > NB:
            sends = HC - place if way == 0 else place + 1

            @pl.when(order + NB < sends)
            def _():
                pl.semaphore_signal(
                    e.credits.at[way],
                    inc=1,
                    device_id=left if way == 0 else right,
                    device_id_type=MESH,
                )

    def dkv_pass(at, to):
        b = of_core(1 - me_d, at)
        return copy(e.kv.at[b], e.dkv_par.at[to], "dkv_pass", at, partner)

    def both_cores(at, to):
        other = of_core(1 - me_d, at)
        attend_back(other, to)
        e.kv[other] = e.dkv[to].astype(BF16)
        again = at < HC - 1 if to == 0 else at > 0
        if HC > 2 and to < 2:

            @pl.when(again)
            def _():
                pl.semaphore_wait(e.pass_credits.at[to], 1)

        dkv_pass(at, to).start()
        attend_back(of_core(me_d, at), to)
        dkv_pass(at, to).wait_recv()
        e.dkv[to] += e.dkv_par[to].astype(F32)
        more = at > place + 1 if to == 0 else at < place - 1
        if HC > 2 and to < 2:

            @pl.when(more)
            def _():
                pl.semaphore_signal(
                    e.pass_credits.at[to], inc=1, device_id=partner, device_id_type=MESH
                )

    def dkv_step(s, carry):
        from_left = HC - 1 + place - s
        from_right = s - (HC - 1 - place)

        @pl.when(s >= place)
        def _():
            both_cores(from_left, 0)

            @pl.when(place > 0)
            def _():
                dkv_take(0, from_left, 0)

            e.kv[of_core(me_d, from_left)] = e.dkv[0].astype(BF16)
            dkv_send(0, from_left)

        @pl.when(from_right >= 0)
        def _():
            both_cores(from_right, 1)

            @pl.when(place < HC - 1)
            def _():
                dkv_take(1, from_right, 1)

            e.kv[of_core(me_d, from_right)] = e.dkv[1].astype(BF16)
            dkv_send(1, from_right)

        return carry

    lax.fori_loop(0, HC - 1, dkv_step, 0)
    both_cores(place, 2)

    for h in range(NH):
        e.dqkv[h * HS : (h + 1) * HS, :] = (e.dq[h] * (HS ** (-0.5))).T.astype(BF16)

    def fill_query(rows):
        e.dw_f[rows, :F] = dot_nt(e.x_rows_t[rows, :], e.dqkv[:F, :])
        e.dw_f[rows, F : 2 * F] = dot_nn(e.gr_t[rows, :], e.ctx[...])

    row_tiles(fill_query)
    query_grad = e.dw_f.at[:, pl.ds(0, 2 * F)]
    weight_swap("dwqm", query_grad)
    gv_dp().wait_recv()
    e.gall[2] = e.gall[0] + e.gall[1]
    for i in range(1, C):
        gv_col(i).start()
    weight_send("dwqm", query_grad)

    @pl.when(place > 0)
    def _():
        dkv_take(0, place, 2)

    @pl.when(place < HC - 1)
    def _():
        dkv_take(1, place, 2)

    e.dqkv[F : 3 * F, :] = e.dkv[2].astype(BF16)

    def fill_keys(rows):
        e.dw_f[rows, 2 * F :] = dot_nt(e.x_rows_t[rows, :], e.dqkv[F:, :])

    row_tiles(fill_keys)
    key_grad = e.dw_f.at[:, pl.ds(2 * F, 2 * F)]
    weight_swap("dwkv", key_grad)

    def input_part(kind, rb):
        part = dot_nn(wqm[:, :F], e.dqkv[:F, blk_rows(rb)])
        part = part + dot_nn(wkv[...], e.dqkv[F:, blk_rows(rb)])
        sum_add(3, "dx", kind, part)

    input_part("far", far)
    for i in range(1, C):
        gv_col(i).wait_recv()
    gsum = e.gall[2]
    for i in range(1, C):
        gsum = gsum + e.gcol[i]
    e.gsum[...] = gsum

    def gv_row(i):
        return copy(e.gsum.at[pl.ds(0, 8)], e.grow.at[i], "gv_row", i, to_row(i))

    for i in range(1, R):
        gv_row(i).start()

    e.ab[0] = dot_nt(jnp.ones((8, S), BF16), e.dqkv[...])

    def ab_dp():
        return copy(e.ab.at[0], e.ab.at[1], "ab_dp", 0, partner)

    def ab_col(i):
        return copy(e.ab.at[2], e.abcol.at[i], "ab_col", i, to_col(i))

    ab_dp().start()
    weight_send("dwkv", key_grad)
    ab_dp().wait_recv()
    e.ab[2] = e.ab[0] + e.ab[1]
    for i in range(1, C):
        ab_col(i).start()

    input_part("near", near)
    input_part("over", over)
    input_part("own", me_r)
    e.own_dx[...] = sum_collect(3, "dx") + e.g_first[...].T

    @pl.when(swapped)
    def _():
        swap_copy(e.lo_out, e.layer_out, 2).wait_send()
        swap_copy(e.lo_out, e.layer_out, 2).wait_recv()
        e.lo_out[...] = e.own_dx[...].astype(BF16)
        swap_copy(e.lo_out, e.og_in, 3).start()

    @pl.when(stays)
    def _():
        e.grad_input[...] = e.own_dx[...]

    weight_collect("dw3")
    weight_collect("dw2")
    weight_collect("dwqm")

    vsum = e.gsum[0:8, :D]
    for i in range(1, R):
        gv_row(i).wait_recv()
        vsum = vsum + e.grow[i][:, :D]
    picked = vsum[:, :RB]
    for c in range(1, C):
        picked = jnp.where(me_c == c, vsum[:, c * RB : (c + 1) * RB], picked)
    e.g_vec[...] = picked
    e.g_unit[...] = e.gsum[8:9, :U]
    asum = e.ab[2]
    for i in range(1, C):
        ab_col(i).wait_recv()
        asum = asum + e.abcol[i]
    e.g_ab[0:1, :] = asum[0:1, :F]
    e.g_ab[1:2, :] = asum[0:1, 2 * F :]
    weight_collect("dwkv")
    if dims.flat:
        for name in ("dw3", "dw2", "dwqm", "dwkv"):
            result_copy(name).wait_recv()
    e.g_attn[0] = e.dwqm_sum[:, :F]
    e.g_mix[...] = e.dwqm_sum[:, F:]
    e.g_attn[1] = e.dwkv_sum[:, :F]
    e.g_attn[2] = e.dwkv_sum[:, F:]

    @pl.when(swapped)
    def _():
        swap_copy(e.lo_out, e.og_in, 3).wait_recv()
        e.grad_input[...] = e.og_in[...].astype(F32)

    @pl.when(swapped)
    def _():
        swap_copy(e.x_t, e.x_in, 0).wait_send()
        swap_copy(e.out_grad, e.og_in, 1).wait_send()
        swap_copy(e.lo_out, e.og_in, 3).wait_send()

    len_copy().wait_send()
    for name in ("wkv", "wqm", "w2", "w3"):
        weight_close(name)
    gather_close(e.xg, "x")
    gather_close(e.gr_g, "gr")
    gather_close(e.hid_g, "gm")
    for k, family in ((1, "red"), (2, "gh"), (3, "dx")):
        sum_close(k, family)
    for i in range(1, R):
        gv_row(i).wait_send()
    gv_dp().wait_send()
    ab_dp().wait_send()
    for i in range(1, C):
        vec_copy(i).wait_send()
        gv_col(i).wait_send()
        ab_col(i).wait_send()
    for name in ("dw3", "dw2", "dwqm", "dwkv"):
        other_copy(name).wait_send()
        for i in range(1, C):
            d_copy(name, i).wait_send()
        if dims.flat:
            result_copy(name).wait_send()

    for at in range(HC):
        dkv_pass(at, 2).wait_send()

    @pl.when(place < HC - 1)
    def _():
        dkv_right(place + 1).wait_send()

    @pl.when(place > 0)
    def _():
        dkv_left(place - 1).wait_send()


def run_layer(x_t, length, w_attn, w_mixer, w2, w3, out_grad, b_attn, b_expand, **vectors):
    R = lax.axis_size("row")
    C = lax.axis_size("col")
    T = x_t.shape[1]
    S = T * R
    F = w_mixer.shape[1]
    U = w2.shape[1]
    RB = w_mixer.shape[0]
    flat = RB % 32 == 0
    HS = D // H
    dims = SimpleNamespace(
        R=R, C=C, T=T, S=S, F=F, U=U, RB=RB, HS=HS, NH=F // HS,
        flat=flat, HB=RB // 2 if flat else RB, TQ=min(256, S), TR=256, NB=max(1, min(C // 2 - 1, 3)),
    )
    HB = dims.HB
    NH = dims.NH
    slots = slots_of(R, C)
    wide = max(D, U)
    w_shape = (lambda n: (C * RB, n)) if dims.flat else (lambda n: (C, RB, n))
    inputs = dict(
        x_t=x_t, length=length, w_attn=w_attn, w_mixer=w_mixer, w2=w2, w3=w3, out_grad=out_grad,
        b_attn=b_attn, b_expand=b_expand, **vectors,
    )
    outputs = dict(
        layer_out=((D, T), BF16),
        grad_input=((D, T), F32),
        g_attn=((3, RB, F), F32),
        g_mix=((RB, F), F32),
        dw2_sum=((RB, U), F32),
        dw3_sum=((RB, U), F32),
        g_vec=((8, RB), F32),
        g_unit=((1, U), F32),
        g_ab=((2, F), F32),
    )
    scratch = dict(
        xg=((R, T, D), BF16),
        wkv=((RB, 2 * F), BF16),
        wqm=((RB, 2 * F), BF16),
        wkv_g=(w_shape(2 * F), BF16),
        wqm_g=(w_shape(2 * F), BF16),
        w2_g=(w_shape(U), BF16),
        w3_g=(w_shape(U), BF16),
        mix=((D, F), BF16),
        vecr=((C, 8, F), F32),
        vecs=((8, D), F32),
        bias=((1, U), F32),
        kv=((C, 2 * F, S), BF16),
        q_t=((F, S), BF16),
        q_h=((NH, S, HS), BF16),
        x_rows_t=((D, S), BF16),
        top=((NH, S, 1), F32),
        total=((NH, S, 1), F32),
        acc=((NH, S, HS), F32),
        ctx=((S, F), BF16),
        own_0=((T, D), F32),
        own_1=((T, D), F32),
        own_dx=((D, T), F32),
        n1=((T, D), F32),
        r1=((T, 1), F32),
        hidden=((T, D), F32),
        hid_g=((R, T, D), BF16),
        active=((S, U), BF16),
        slope=((S, U), F32),
        hid_t=((D, S), BF16),
        g_second=((T, D), F32),
        gr_g=((R, T, D), BF16),
        gr_t=((D, S), BF16),
        g_inner=((S, U), BF16),
        gv=((8, D), F32),
        gu=((8, U), F32),
        gall=((3, 16, wide), F32),
        gcol=((C, 16, wide), F32),
        gsum=((16, wide), F32),
        grow=((R, 8, wide), F32),
        dw_f=((D, U), F32),
        dwqm_sum=((RB, 2 * F), F32),
        dwkv_sum=((RB, 2 * F), F32),
        g_first=((T, D), F32),
        gc_t=((F, S), BF16),
        gc_h=((NH, S, HS), BF16),
        inner_sum=((NH, S, 1), F32),
        dq=((NH, S, HS), F32),
        dkv=((3, 2 * F, S), F32),
        dkv_par=((3, 2 * F, S), BF16),
        lens=((2, 8, 128), F32),
        x_in=((D, T), BF16),
        og_in=((D, T), BF16),
        lo_out=((D, T), BF16),
        dkv_in=((2, dims.NB, 2 * F, S), BF16),
        dqkv=((3 * F, S), BF16),
        ab=((3, 8, 3 * F), F32),
        abcol=((C, 8, 3 * F), F32),
    )
    for k, (rows, width) in enumerate(((T, D), (T, D), (D, T))):
        scratch[f"out_{k}"] = ((3, rows, width), BF16)
        scratch[f"land_{k}"] = ((3, rows, width), BF16)
    for name, width in (("wkv", 2 * F), ("wqm", 2 * F), ("w2", U), ("w3", U)):
        for part in ("out", "in", "land"):
            scratch["d" + name + "_" + part] = ((C, HB, width), BF16)
        if not dims.flat:
            scratch[name + "_f"] = ((C * RB, width), BF16)
    names = list(inputs) + list(outputs) + list(scratch) + ["send_sems", "recv_sems", "credits", "pass_credits"]
    vmem = pl.BlockSpec(memory_space=pltpu.VMEM)
    in_specs = [
        pl.BlockSpec(memory_space=pltpu.SMEM) if name == "length" else vmem for name in inputs
    ]
    results = pl.pallas_call(
        functools.partial(layer_kernel, dims, names),
        out_shape=[jax.ShapeDtypeStruct(s, t) for s, t in outputs.values()],
        in_specs=in_specs,
        out_specs=[vmem] * len(outputs),
        scratch_shapes=[pltpu.VMEM(s, t) for s, t in scratch.values()]
        + [pltpu.SemaphoreType.DMA((slots.total,)), pltpu.SemaphoreType.DMA((slots.total,))]
        + [pltpu.SemaphoreType.REGULAR((2,)), pltpu.SemaphoreType.REGULAR((2,))],
        compiler_params=pltpu.CompilerParams(
            collective_id=0, has_side_effects=True, vmem_limit_bytes=63 * 2**20
        ),
        name="layer",
    )(*inputs.values())
    return dict(zip(outputs, results))


def finish_kernel(*refs):
    big_in, rows, unit, big_out, vecs, unit_out = (
        refs[:7], refs[7], refs[8], refs[9:16], refs[16:22], refs[22],
    )
    for src, dst in zip(big_in, big_out):
        dst[...] = src[...]
    for k, ref in enumerate(vecs):
        ref[...] = rows[k : k + 1, :].reshape(ref.shape)
    unit_out[...] = unit[...].reshape(unit_out.shape)


def finish(out):
    big = [
        out[name]
        for name in ("layer_out", "grad_input", "g_attn", "g_mix", "dw2_sum", "dw3_sum", "g_ab")
    ]
    rows = out["g_vec"].shape[1]
    units = out["g_unit"].shape[1]
    vmem = pl.BlockSpec(memory_space=pltpu.VMEM)
    shapes = [jax.ShapeDtypeStruct(a.shape, a.dtype) for a in big]
    shapes += [jax.ShapeDtypeStruct((rows,), F32)] * 6 + [jax.ShapeDtypeStruct((units,), F32)]
    return pl.pallas_call(
        finish_kernel,
        out_shape=shapes,
        in_specs=[vmem] * 9,
        out_specs=[vmem] * 14,
        name="finish",
    )(*big, out["g_vec"], out["g_unit"])


def on_device(
    layer_in,
    lengths,
    w_attn,
    b_attn,
    w_mixer,
    b_mixer,
    gain_one,
    shift_one,
    w_expand,
    b_expand,
    w_reduce,
    b_reduce,
    gain_two,
    shift_two,
    out_grad,
):
    out = run_layer(
        layer_in,
        lengths,
        jnp.transpose(w_attn, (1, 0, 2)),
        w_mixer,
        w_expand,
        w_reduce,
        out_grad,
        b_attn,
        b_expand,
        b_mixer=b_mixer,
        gain_one=gain_one,
        shift_one=shift_one,
        b_reduce=b_reduce,
        gain_two=gain_two,
        shift_two=shift_two,
    )
    layer_out, grad_input, g_attn, g_mix, g_expand, g_reduce, g_ab, *vecs, g_unit = finish(out)
    return (
        layer_out,
        grad_input,
        jnp.transpose(g_attn, (1, 0, 2)),
        g_ab,
        g_mix,
        vecs[0],
        vecs[1],
        vecs[2],
        g_expand,
        g_unit,
        g_reduce,
        vecs[3],
        vecs[4],
        vecs[5],
    )


def solution(mesh):
    return jax.shard_map(
        on_device,
        mesh=mesh,
        in_specs=(
            P(None, ("dp", "row", "col")),
            P("dp"),
            P("col", None, "row"),
            P(None, "row"),
            P("col", "row"),
            P("col"),
            P("col"),
            P("col"),
            P("col", "row"),
            P("row"),
            P("col", "row"),
            P("col"),
            P("col"),
            P("col"),
            P(None, ("dp", "row", "col")),
        ),
        out_specs=(
            P(None, ("dp", "row", "col")),
            P(None, ("dp", "row", "col")),
            P("col", None, "row"),
            P(None, "row"),
            P("col", "row"),
            P("col"),
            P("col"),
            P("col"),
            P("col", "row"),
            P("row"),
            P("col", "row"),
            P("col"),
            P("col"),
            P("col"),
        ),
        check_vma=False,
    )
```

```python
import functools
from types import SimpleNamespace

import jax
import jax.numpy as jnp
from jax import lax
from jax.experimental import pallas as pl
from jax.experimental.pallas import tpu as pltpu
from jax.sharding import PartitionSpec as P

D = 768
H = 12
EPSILON = 1e-12
NEGATIVE = -1000000000.0
MESH = pl.DeviceIdType.MESH
F32 = jnp.float32
BF16 = jnp.bfloat16


def dot_nn(left_in, right_in):
    return lax.dot_general(
        left_in, right_in, (((1,), (0,)), ((), ())), preferred_element_type=F32
    )


def dot_nt(left_in, right_in):
    return lax.dot_general(
        left_in, right_in, (((1,), (1,)), ((), ())), preferred_element_type=F32
    )


def turned(values):
    return values.astype(F32).T


def normalize(values):
    row_mean = jnp.mean(values, 1, keepdims=True)
    centered = values - row_mean
    row_var = jnp.mean(centered * centered, 1, keepdims=True)
    row_scale = lax.rsqrt(row_var + EPSILON)
    return centered * row_scale, row_scale


def normalize_back(upstream, normed, row_scale, gain_vec):
    scaled = upstream * gain_vec
    mean_plain = jnp.mean(scaled, 1, keepdims=True)
    mean_cross = jnp.mean(scaled * normed, 1, keepdims=True)
    return row_scale * (scaled - mean_plain - normed * mean_cross)


def column_sum(values):
    return jnp.sum(values, 0, keepdims=True)


class Slots:
    def __init__(self):
        self.base = {}
        self.total = 0

    def add(self, name, count):
        self.base[name] = self.total
        self.total += count


def slots_of(R, C):
    slots = Slots()
    for name in ("x", "hid", "gr", "gm"):
        slots.add(name, 4)
    for name in ("mix", "red", "gh", "dx"):
        slots.add(name, 3)
    slots.add("gv_row", R)
    for name in ("vec", "gv_col", "ab_col", "dkv_right", "dkv_left"):
        slots.add(name, C)
    for name in ("wkv", "wqm", "w2", "w3"):
        slots.add(name + "_right", C)
        slots.add(name + "_left", C)
        slots.add(name + "_dp", C)
        slots.add("d" + name, C)
        slots.add("d" + name + "_dp", 1)
        slots.add("d" + name + "_out", 1)
    slots.add("dkv_pass", C)
    for name in ("kv_pass", "kv_right", "kv_left"):
        slots.add(name, C * R)
    for name in ("gv_dp", "ab_dp", "len"):
        slots.add(name, 1)
    slots.add("swap", 4)
    return slots


def layer_kernel(dims, names, *refs):
    e = SimpleNamespace(**dict(zip(names, refs)))
    R, C, T, S, F, U, RB = dims.R, dims.C, dims.T, dims.S, dims.F, dims.U, dims.RB
    NH, HS, HB = dims.NH, dims.HS, dims.HB
    slots = slots_of(R, C)
    me_d = lax.axis_index("dp")
    me_r = lax.axis_index("row")
    me_c = lax.axis_index("col")

    def to_row(step):
        return {"row": lax.rem(me_r + step, R)}

    def to_col(step):
        return {"col": lax.rem(me_c + step, C)}

    partner = {"dp": 1 - me_d}

    HC = C // 2
    half, place = me_c // HC, lax.rem(me_c, HC)
    mine = me_d * HC + place
    swapped = me_d != half
    stays = me_d == half

    def swap_copy(src, dst, at):
        where = {"dp": 1 - me_d, "col": lax.rem(me_c + HC, C)}
        return copy(src, dst, "swap", at, where)

    def copy(src, dst, family, at, where):
        number = slots.base[family] + at
        return pltpu.make_async_remote_copy(
            src_ref=src,
            dst_ref=dst,
            send_sem=e.send_sems.at[number],
            recv_sem=e.recv_sems.at[number],
            device_id=where,
            device_id_type=MESH,
        )

    barrier = pltpu.get_barrier_semaphore()
    pl.semaphore_signal(barrier, inc=1, device_id=partner, device_id_type=MESH)
    for i in range(1, R):
        pl.semaphore_signal(barrier, inc=1, device_id=to_row(i), device_id_type=MESH)
    for i in range(1, C):
        pl.semaphore_signal(barrier, inc=1, device_id=to_col(i), device_id_type=MESH)
    pl.semaphore_signal(
        barrier,
        inc=1,
        device_id={"dp": 1 - me_d, "col": lax.rem(me_c + HC, C)},
        device_id_type=MESH,
    )
    e.wkv[:, :F] = e.w_attn[1]
    e.wkv[:, F:] = e.w_attn[2]
    e.wqm[:, :F] = e.w_attn[0]
    e.wqm[:, F:] = e.w_mixer[...]
    vectors = (e.b_mixer, e.gain_one, e.shift_one, e.b_reduce, e.gain_two, e.shift_two)
    for k, ref in enumerate(vectors):
        e.vecr[me_c, k : k + 1, :RB] = ref[...].astype(F32).reshape(1, RB)
    e.bias[...] = e.b_expand[...].astype(F32).reshape(1, U)
    e.lens[me_d] = jnp.full((8, 128), e.length[0].astype(F32), F32)
    pl.semaphore_wait(barrier, 2 + (R - 1) + (C - 1))

    @pl.when(swapped)
    def _():
        swap_copy(e.x_t, e.x_in, 0).start()

    @pl.when(stays)
    def _():
        e.x_in[...] = e.x_t[...]
        e.og_in[...] = e.out_grad[...]

    def len_copy():
        return copy(e.lens.at[me_d], e.lens.at[me_d], "len", 0, partner)

    len_copy().start()

    def w_rows(ref, c, d):
        if not dims.flat:
            return ref.at[c]
        return ref.at[pl.ds(pl.multiple_of(c * RB + d * HB, HB), HB)]

    def weight_own(name):
        full = getattr(e, name + "_g")
        if dims.flat:
            full[pl.ds(pl.multiple_of(me_c * RB, RB), RB), :] = getattr(e, name)[...]
        else:
            full[me_c] = getattr(e, name)[...]

    right = {"col": lax.rem(me_c + 1, C)}
    left = {"col": lax.rem(me_c + C - 1, C)}

    def line_copy(name, way, b):
        there = w_rows(getattr(e, name + "_g"), b, me_d)
        return copy(there, there, name + way, b, right if way == "_right" else left)

    def line_pass(name, b):
        there = w_rows(getattr(e, name + "_g"), b, me_d)
        return copy(there, there, name + "_dp", b, partner)

    def line_on(name, way, b):
        pl.when(me_c < C - 1 if way == "_right" else me_c > 0)(line_copy(name, way, b).start)

    def line_start(name):
        line_on(name, "_right", me_c)
        line_on(name, "_left", me_c)

    def line_step(name, step):
        for way, b, there in (
            ("_right", me_c - step, me_c >= step),
            ("_left", me_c + step, me_c + step < C),
        ):

            @pl.when(there)
            def _(way=way, b=b):
                line_copy(name, way, b).wait_recv()
                line_on(name, way, b)
                if dims.flat:
                    line_pass(name, b).start()

    def line_end(name, first=3):
        def step(i, carry):
            line_step(name, i)
            return carry

        lax.fori_loop(min(first, C), C, step, 0)
        if dims.flat:
            for i in range(1, C):
                line_pass(name, lax.rem(me_c + i, C)).wait_recv()
        else:
            full = getattr(e, name + "_g")
            flat = full[...].astype(F32).reshape(C * RB, full.shape[2])
            getattr(e, name + "_f")[...] = flat.astype(BF16)

    def line_close(name):
        def step(b, carry):
            @pl.when((b <= me_c) & (me_c < C - 1))
            def _():
                line_copy(name, "_right", b).wait_send()

            @pl.when((b >= me_c) & (me_c > 0))
            def _():
                line_copy(name, "_left", b).wait_send()

            if dims.flat:

                @pl.when(b != me_c)
                def _():
                    line_pass(name, b).wait_send()

            return carry

        lax.fori_loop(0, C, step, 0)

    wkv, wqm, w2f, w3f = [
        getattr(e, name + ("_g" if dims.flat else "_f")) for name in ("wkv", "wqm", "w2", "w3")
    ]

    beside = {"row": me_r + 1 - 2 * lax.rem(me_r, 2)}
    across = {"row": lax.rem(me_r + 2, R)}
    near, over, far = beside["row"], across["row"], R - 1 - me_r
    low, high = pl.ds(0, T // 2), pl.ds(T // 2, T // 2)

    def gather_copy(ref, family, at):
        part, where = (
            (ref.at[me_r], beside),
            (ref.at[me_r], across),
            (ref.at[near, low], across),
            (ref.at[over, high], beside),
        )[at]
        return copy(part, part, family, at, where)

    def gather_start(ref, family):
        gather_copy(ref, family, 0).start()
        gather_copy(ref, family, 1).start()

    def gather_near(ref, family):
        gather_copy(ref, family, 0).wait_recv()
        gather_copy(ref, family, 2).start()

    def gather_over(ref, family):
        gather_copy(ref, family, 1).wait_recv()
        gather_copy(ref, family, 3).start()

    def gather_far(ref, family):
        gather_copy(ref, family, 2).wait_recv()
        gather_copy(ref, family, 3).wait_recv()

    def gather_close(ref, family):
        for at in range(4):
            gather_copy(ref, family, at).wait_send()

    def each(count, body):
        def step(j, carry):
            body(j)
            return carry

        lax.fori_loop(0, count, step, 0)

    def gathered(ref, family):
        yield "own", me_r
        gather_near(ref, family)
        gather_over(ref, family)
        yield "near", near
        yield "over", over
        gather_far(ref, family)
        yield "far", far

    def sum_copy(k, family, kind):
        at = ("near", "over", "far").index(kind)
        where = (beside, across, {"row": far})[at]
        out, land, _ = e.sums[k]
        return copy(out.at[at], land.at[at], family, at, where)

    def sum_add(k, family, kind, part):
        out, _, own = e.sums[k]
        if kind == "own":
            own[...] = part
        else:
            out[("near", "over", "far").index(kind)] = part.astype(BF16)
            sum_copy(k, family, kind).start()

    def sum_collect(k, family):
        _, land, own = e.sums[k]
        total = own[...]
        for at, kind in enumerate(("near", "over", "far")):
            sum_copy(k, family, kind).wait_recv()
            total = total + land[at].astype(F32)
        return total

    def sum_close(k, family):
        for kind in ("near", "over", "far"):
            sum_copy(k, family, kind).wait_send()

    e.sums = [
        (getattr(e, f"out_{k}"), getattr(e, f"land_{k}"), own)
        for k, own in ((0, e.own), (1, e.own), (0, e.own), (2, e.own_dx))
    ]

    def vec_copy(i):
        return copy(e.vecr.at[me_c], e.vecr.at[me_c], "vec", i, to_col(i))

    for name in ("wkv", "wqm", "w2", "w3"):
        weight_own(name)
    line_start("wkv")
    line_start("wqm")

    @pl.when(swapped)
    def _():
        swap_copy(e.x_t, e.x_in, 0).wait_recv()

    e.xg[me_r] = turned(e.x_in[...]).astype(BF16)
    gather_start(e.xg, "x")
    for step in range(1, min(3, C)):
        line_step("wkv", step)
        line_step("wqm", step)

    len_copy().wait_recv()
    length = e.lens[half][0:1, 0:1]
    for i in range(1, C):
        vec_copy(i).start()
    gather_near(e.xg, "x")
    gather_over(e.xg, "x")
    line_end("wkv")

    def of_core(d, at):
        return d * HC + at

    def kv_copy(b, i, family, where):
        part = e.kv.at[b, :, pl.ds(pl.multiple_of(i * T, T), T)]
        return copy(part, part, family, b * R + i, where)

    def kv_right(b, i):
        return kv_copy(b, i, "kv_right", right)

    def kv_left(b, i):
        return kv_copy(b, i, "kv_left", left)

    def kv_pass(b, i):
        return kv_copy(b, i, "kv_pass", partner)

    def kv_on(b, i):
        pl.when(place < HC - 1)(kv_right(b, i).start)
        pl.when(place > 0)(kv_left(b, i).start)
        kv_pass(b, i).start()

    for kind, rb in (("own", me_r), ("near", near), ("over", over), ("far", far)):
        if kind == "far":
            gather_far(e.xg, "x")
        tokens = pl.ds(pl.multiple_of(rb * T, T), T)
        both = dot_nn(e.xg[rb], wkv[...])
        values = both[:, F:] + e.b_attn[1:2, :].astype(F32)
        e.kv[mine, pl.ds(0, F), tokens] = both[:, :F].T.astype(BF16)
        e.kv[mine, pl.ds(F, F), tokens] = values.T.astype(BF16)
        kv_on(mine, rb)

    def make_queries():
        line_end("wqm")
        e.mix[...] = wqm[:, F:]
        for i in range(R):
            tokens = pl.ds(i * T, T)
            block = e.xg[i]
            q = dot_nn(block, wqm[:, :F]) + e.b_attn[0:1, :].astype(F32)
            q = q.astype(BF16).astype(F32) * (HS ** (-0.5))
            e.q_t[:, tokens] = q.T.astype(BF16)
            for h in range(NH):
                e.q_h[h, tokens, :] = q[:, h * HS : (h + 1) * HS].astype(BF16)
            e.x_rows_t[:, tokens] = turned(block).astype(BF16)

    def key_valid(b):
        lane = lax.broadcasted_iota(jnp.int32, (1, S), 1)
        return (lane // T * (T * C) + b * T + lane % T).astype(F32) < length

    TQ = dims.TQ
    e.top[...] = jnp.full(e.top.shape, -3e38, F32)
    e.acc[...] = jnp.zeros(e.acc.shape, F32)
    ones = jnp.ones((16, S), BF16)

    def tiles(body):
        if TQ == S:
            body(0, 0)
        else:
            lax.fori_loop(0, S // TQ, body, 0)

    def attend(at):
        blocks = (of_core(0, at), of_core(1, at))
        valid = [key_valid(b) for b in blocks]

        def tile(t, carry):
            rows = pl.ds(pl.multiple_of(t * TQ, TQ), TQ)
            for h in range(NH):
                scores = [
                    jnp.where(
                        ok,
                        dot_nn(e.q_h[h, rows, :], e.kv[b, h * HS : (h + 1) * HS, :]),
                        NEGATIVE,
                    )
                    for b, ok in zip(blocks, valid)
                ]
                old = e.top[h, rows, :]
                new = jnp.maximum(
                    old, jnp.max(jnp.maximum(*scores), 1, keepdims=True)
                )
                e.top[h, rows, :] = new
                part = jnp.exp(old - new) * e.acc[h, rows, :]
                for b, score in zip(blocks, scores):
                    values = e.kv[b, F + h * HS : F + (h + 1) * HS, :]
                    part = part + dot_nt(
                        jnp.exp(score - new).astype(BF16), jnp.concatenate([values, ones], 0)
                    )
                e.acc[h, rows, :] = part
            return carry

        tiles(tile)

    make_queries()

    def kv_step(s, carry):
        from_left = place - s
        from_right = place + s

        @pl.when((s > 0) & (from_left >= 0))
        def _():
            b = of_core(me_d, from_left)

            @functools.partial(each, R)
            def _(i):
                kv_right(b, i).wait_recv()
                kv_pass(b, i).start()
                pl.when(place < HC - 1)(kv_right(b, i).start)

        @pl.when((s > 0) & (from_right < HC))
        def _():
            b = of_core(me_d, from_right)

            @functools.partial(each, R)
            def _(i):
                kv_left(b, i).wait_recv()
                kv_pass(b, i).start()
                pl.when(place > 0)(kv_left(b, i).start)

        @pl.when(s == HC - 1)
        def _():
            line_start("w2")
            line_start("w3")

        @functools.partial(each, 2)
        def _(k):
            at = jnp.where(k == 0, from_left, from_right)

            @pl.when((at >= 0) & (at < HC) & ((s > 0) | (k == 0)))
            def _():
                each(R, lambda i: kv_pass(of_core(1 - me_d, at), i).wait_recv())
                attend(at)

        return carry

    lax.fori_loop(0, HC, kv_step, 0)

    def kv_close(at, carry):
        b = of_core(me_d, at)

        @functools.partial(each, R)
        def _(i):
            kv_pass(b, i).wait_send()

            @pl.when((at <= place) & (place < HC - 1))
            def _():
                kv_right(b, i).wait_send()

            @pl.when((at >= place) & (place > 0))
            def _():
                kv_left(b, i).wait_send()

        return carry

    lax.fori_loop(0, HC, kv_close, 0)

    for h in range(NH):
        inverse = 1.0 / e.acc[h, :, HS : HS + 1]
        e.total[h] = inverse
        context = e.acc[h, :, :HS] * inverse
        e.acc[h, :, :HS] = context
        e.ctx[:, h * HS : (h + 1) * HS] = context.astype(BF16)

    for i in range(1, C):
        vec_copy(i).wait_recv()
    for c in range(C):
        e.vecs[:, c * RB : (c + 1) * RB] = e.vecr[c][:, :RB]

    def vector(at):
        return e.vecs[at : at + 1, :]

    def blk_rows(rb):
        return pl.ds(pl.multiple_of(rb * T, T), T)

    for kind, rb in (("far", far), ("near", near), ("over", over), ("own", me_r)):
        sum_add(0, "mix", kind, dot_nt(e.ctx[blk_rows(rb), :], e.mix[...]))

    line_step("w2", 1)
    line_step("w3", 1)
    first_sum = turned(e.x_in[...]) + sum_collect(0, "mix") + vector(0)
    normed, scale = normalize(first_sum)
    hidden = normed * vector(1) + vector(2)
    e.n1[...] = normed
    e.r1[...] = scale
    e.hidden[...] = hidden
    e.hid_g[me_r] = hidden.astype(BF16)

    gather_start(e.hid_g, "hid")

    @pl.when(swapped)
    def _():
        swap_copy(e.out_grad, e.og_in, 1).start()

    if C > 2:
        line_step("w2", 2)
        line_step("w3", 2)
    line_end("w2")

    for kind, rb in gathered(e.hid_g, "hid"):
        inner = dot_nn(e.hid_g[rb], w2f[...]) + e.bias[...]
        cdf = 0.5 * (1.0 + lax.erf(inner * (0.5**0.5)))
        active = (inner * cdf).astype(BF16)
        slope = cdf + inner * (jnp.exp(-0.5 * inner * inner) * 0.3989422804014327)
        e.active[blk_rows(rb), :] = active
        e.slope[blk_rows(rb), :] = slope
        if kind == "own":
            continue
        if kind == "near":
            line_end("w3")
            sum_add(1, "red", "own", dot_nt(e.active[blk_rows(me_r), :], w3f[...]))
        sum_add(1, "red", kind, dot_nt(e.active[blk_rows(rb), :], w3f[...]))
    for i in range(R):
        e.hid_t[:, i * T : (i + 1) * T] = turned(e.hid_g[i]).astype(BF16)
    gather_close(e.hid_g, "hid")

    second_sum = e.hidden[...] + sum_collect(1, "red") + vector(3)
    normed, scale = normalize(second_sum)
    slot = lax.broadcasted_iota(jnp.int32, (T, 1), 0) + (me_r * (T * C) + mine * T)
    row_valid = (slot.astype(F32) < length).astype(F32)

    @pl.when(swapped)
    def _():
        swap_copy(e.out_grad, e.og_in, 1).wait_recv()

    upstream = turned(e.og_in[...]) * row_valid
    g_second = normalize_back(upstream, normed, scale, vector(4))
    g_reduced = g_second.astype(BF16)
    e.gr_g[me_r] = g_reduced
    gather_start(e.gr_g, "gr")
    e.lo_out[...] = ((normed * vector(4) + vector(5)) * row_valid).T.astype(BF16)

    @pl.when(swapped)
    def _():
        swap_copy(e.lo_out, e.layer_out, 2).start()

    @pl.when(stays)
    def _():
        e.layer_out[...] = e.lo_out[...]

    e.g_second[...] = g_second
    e.gv[4:5, :] = column_sum(upstream * normed)
    e.gv[5:6, :] = column_sum(upstream)
    e.gv[3:4, :] = column_sum(g_reduced.astype(F32))
    e.gv[7:8, :] = jnp.zeros((1, D), F32)

    unit_sum = jnp.zeros((1, U), F32)
    sum_close(0, "mix")
    for kind, rb in gathered(e.gr_g, "gr"):
        g_active = dot_nn(e.gr_g[rb], w3f[...]).astype(BF16).astype(F32)
        g_inner = (g_active * e.slope[blk_rows(rb), :]).astype(BF16)
        e.g_inner[blk_rows(rb), :] = g_inner
        unit_sum = unit_sum + column_sum(g_inner.astype(F32))
        sum_add(2, "gh", kind, dot_nt(e.g_inner[blk_rows(rb), :], w2f[...]))
    e.gu[0:1, :] = unit_sum
    for i in range(R):
        e.gr_t[:, i * T : (i + 1) * T] = turned(e.gr_g[i]).astype(BF16)

    TR = dims.TR

    def half_rows(c, d):
        if not dims.flat:
            return pl.ds(c * RB, RB)
        return pl.ds(pl.multiple_of(c * RB + d * HB, HB), HB)

    def other_copy(name):
        return copy(getattr(e, name + "_out"), getattr(e, name + "_in"), name + "_dp", 0, partner)

    def d_copy(name, i):
        stage = getattr(e, name + "_in").at[lax.rem(me_c + i, C)]
        return copy(stage, getattr(e, name + "_land").at[i], name, i, to_col(i))

    def row_tiles(fill):
        def tile(t, carry):
            fill(pl.ds(pl.multiple_of(t * TR, TR), TR))
            return carry

        lax.fori_loop(0, D // TR, tile, 0)

    def weight_swap(name, source):
        def block(c, carry):
            getattr(e, name + "_out")[c] = source[half_rows(c, 1 - me_d), :].astype(BF16)
            return carry

        lax.fori_loop(0, C, block, 0)
        other_copy(name).start()

    def weight_send(name, source):
        other_copy(name).wait_recv()

        def block(c, carry):
            total = source[half_rows(c, me_d), :] + getattr(e, name + "_in")[c].astype(F32)
            getattr(e, name + "_in")[c] = total.astype(BF16)
            return carry

        lax.fori_loop(0, C, block, 0)
        for i in range(1, C):
            d_copy(name, i).start()

    def result_part(name):
        full = getattr(e, name + "_sum")
        return full.at[pl.ds(pl.multiple_of(me_d * HB, HB), HB)] if dims.flat else full

    def result_copy(name):
        return copy(result_part(name), result_part(name), name + "_out", 0, partner)

    def weight_collect(name):
        total = getattr(e, name + "_in")[me_c].astype(F32)
        for i in range(1, C):
            d_copy(name, i).wait_recv()
            total = total + getattr(e, name + "_land")[i].astype(F32)
        result_part(name)[...] = total
        if dims.flat:
            result_copy(name).start()

    def fill_reduce(rows):
        e.dw_f[rows, :] = dot_nn(e.gr_t[rows, :], e.active[...])

    def fill_expand(rows):
        e.dw_f[rows, :] = dot_nn(e.hid_t[rows, :], e.g_inner[...])

    row_tiles(fill_reduce)
    weight_swap("dw3", e.dw_f)
    weight_send("dw3", e.dw_f)
    row_tiles(fill_expand)
    weight_swap("dw2", e.dw_f)
    weight_send("dw2", e.dw_f)

    g_hidden = sum_collect(2, "gh") + e.g_second[...]
    normed = e.n1[...]
    g_first = normalize_back(g_hidden, normed, e.r1[...], vector(1))
    g_mixed = g_first.astype(BF16)
    e.hid_g[me_r] = g_mixed
    gather_start(e.hid_g, "gm")
    e.g_first[...] = g_first
    e.gv[1:2, :] = column_sum(g_hidden * normed)
    e.gv[2:3, :] = column_sum(g_hidden)
    e.gv[0:1, :] = column_sum(g_mixed.astype(F32))
    e.gv[6:7, :] = jnp.zeros((1, D), F32)

    def gv_dp():
        return copy(e.gall.at[0], e.gall.at[1], "gv_dp", 0, partner)

    e.gall[0, :, :D] = e.gv[...]
    e.gall[0, 6:7, :U] = e.gu[0:1, :]
    gv_dp().start()

    for _, rb in gathered(e.hid_g, "gm"):
        rows = blk_rows(rb)
        g_context = dot_nn(e.hid_g[rb], e.mix[...]).astype(BF16).astype(F32)
        e.gc_t[:, rows] = g_context.T.astype(BF16)
        for h in range(NH):
            part = g_context[:, h * HS : (h + 1) * HS]
            e.gc_h[h, rows, :] = part.astype(BF16)
            e.inner_sum[h, rows, :] = jnp.sum(part * e.acc[h, rows, :HS], 1, keepdims=True)
        e.gr_t[:, rows] = turned(e.hid_g[rb]).astype(BF16)

    def gv_col(i):
        return copy(e.gall.at[2], e.gcol.at[i], "gv_col", i, to_col(i))

    e.dq[...] = jnp.zeros(e.dq.shape, F32)

    def attend_back(b, to):
        valid = key_valid(b)
        for h in range(NH):
            krows = slice(h * HS, (h + 1) * HS)
            vrows = slice(F + h * HS, F + (h + 1) * HS)

            def tile(t, carry):
                d_keys, d_values = carry
                rows = pl.ds(pl.multiple_of(t * TQ, TQ), TQ)
                keys = e.kv[b, krows, :]
                values = e.kv[b, vrows, :]
                scores = dot_nn(e.q_h[h, rows, :], keys)
                scores = jnp.where(valid, scores, NEGATIVE)
                probs = jnp.exp(scores - e.top[h, rows, :]) * e.total[h, rows, :]
                g_weights = dot_nn(e.gc_h[h, rows, :], values)
                g_scores = (probs * (g_weights - e.inner_sum[h, rows, :])).astype(BF16)
                e.dq[h, rows, :] += dot_nt(g_scores, keys)
                d_keys = d_keys + dot_nn(e.q_t[krows, rows], g_scores)
                d_values = d_values + dot_nn(e.gc_t[krows, rows], probs.astype(BF16))
                return d_keys, d_values

            zero = jnp.zeros((HS, S), F32)
            if TQ == S:
                d_keys, d_values = tile(0, (zero, zero))
            else:
                d_keys, d_values = lax.fori_loop(0, S // TQ, tile, (zero, zero))
            e.dkv[to, krows, :] = d_keys
            e.dkv[to, vrows, :] = d_values

    NB = dims.NB

    def dkv_right(at):
        b = of_core(me_d, at)
        return copy(
            e.kv.at[b], e.dkv_in.at[0, lax.rem(HC - 1 - at, NB)], "dkv_right", at, right
        )

    def dkv_left(at):
        b = of_core(me_d, at)
        return copy(e.kv.at[b], e.dkv_in.at[1, lax.rem(at, NB)], "dkv_left", at, left)

    def dkv_send(way, at):
        order = HC - 1 - at if way == 0 else at
        if HC - 1 > NB:

            @pl.when(order >= NB)
            def _():
                pl.semaphore_wait(e.credits.at[way], 1)

        if way == 0:

            @pl.when(at < HC - 1)
            def _():
                dkv_right(at + 1).wait_send()

            dkv_right(at).start()
        else:

            @pl.when(at > 0)
            def _():
                dkv_left(at - 1).wait_send()

            dkv_left(at).start()

    def dkv_take(way, at, to):
        order = HC - 1 - at if way == 0 else at
        (dkv_right if way == 0 else dkv_left)(at).wait_recv()
        e.dkv[to] += e.dkv_in[way, lax.rem(order, NB)].astype(F32)
        if HC - 1 > NB:
            sends = HC - place if way == 0 else place + 1

            @pl.when(order + NB < sends)
            def _():
                pl.semaphore_signal(
                    e.credits.at[way],
                    inc=1,
                    device_id=left if way == 0 else right,
                    device_id_type=MESH,
                )

    def dkv_pass(at, to):
        b = of_core(1 - me_d, at)
        return copy(e.kv.at[b], e.dkv_par.at[to], "dkv_pass", at, partner)

    def both_cores(at, to):
        first = jnp.where(to == 0, at == HC - 1, at == 0)
        last = jnp.where(to == 0, at == place + 1, at == place - 1)

        @functools.partial(each, 2)
        def _(k):
            b = of_core(jnp.where(k == 0, 1 - me_d, me_d), at)
            attend_back(b, to)

            @pl.when(k == 0)
            def _():
                e.kv[b] = e.dkv[to].astype(BF16)
                if HC > 2:

                    @pl.when((to < 2) & jnp.logical_not(first))
                    def _():
                        pl.semaphore_wait(e.pass_credits.at[to], 1)

                dkv_pass(at, to).start()

        dkv_pass(at, to).wait_recv()
        e.dkv[to] += e.dkv_par[to].astype(F32)
        if HC > 2:

            @pl.when((to < 2) & jnp.logical_not(last))
            def _():
                pl.semaphore_signal(
                    e.pass_credits.at[to], inc=1, device_id=partner, device_id_type=MESH
                )

    def dkv_step(n, carry):
        s, way = n // 2, lax.rem(n, 2)
        own = s == HC - 1
        at = jnp.where(way == 0, HC - 1 + place - s, s - (HC - 1 - place))
        there = jnp.where(own, way == 0, jnp.where(way == 0, s >= place, at >= 0))

        @pl.when(there)
        def _():
            both_cores(at, jnp.where(own, 2, way))

            @pl.when(jnp.logical_not(own) & (way == 0))
            def _():
                @pl.when(place > 0)
                def _():
                    dkv_take(0, at, 0)

                e.kv[of_core(me_d, at)] = e.dkv[0].astype(BF16)
                dkv_send(0, at)

            @pl.when(jnp.logical_not(own) & (way == 1))
            def _():
                @pl.when(place < HC - 1)
                def _():
                    dkv_take(1, at, 1)

                e.kv[of_core(me_d, at)] = e.dkv[1].astype(BF16)
                dkv_send(1, at)

        return carry

    lax.fori_loop(0, 2 * HC, dkv_step, 0)

    for h in range(NH):
        e.dqkv[h * HS : (h + 1) * HS, :] = (e.dq[h] * (HS ** (-0.5))).T.astype(BF16)

    def fill_query(rows):
        e.dw_f[rows, :F] = dot_nt(e.x_rows_t[rows, :], e.dqkv[:F, :])
        e.dw_f[rows, F : 2 * F] = dot_nn(e.gr_t[rows, :], e.ctx[...])

    row_tiles(fill_query)
    query_grad = e.dw_f.at[:, pl.ds(0, 2 * F)]
    weight_swap("dwqm", query_grad)
    gv_dp().wait_recv()
    e.gall[2] = e.gall[0] + e.gall[1]
    for i in range(1, C):
        gv_col(i).start()
    weight_send("dwqm", query_grad)

    @pl.when(place > 0)
    def _():
        dkv_take(0, place, 2)

    @pl.when(place < HC - 1)
    def _():
        dkv_take(1, place, 2)

    e.dqkv[F : 3 * F, :] = e.dkv[2].astype(BF16)

    def fill_keys(rows):
        e.dw_f[rows, 2 * F :] = dot_nt(e.x_rows_t[rows, :], e.dqkv[F:, :])

    row_tiles(fill_keys)
    key_grad = e.dw_f.at[:, pl.ds(2 * F, 2 * F)]
    weight_swap("dwkv", key_grad)

    def input_part(kind, rb):
        part = dot_nn(wqm[:, :F], e.dqkv[:F, blk_rows(rb)])
        part = part + dot_nn(wkv[...], e.dqkv[F:, blk_rows(rb)])
        sum_add(3, "dx", kind, part)

    input_part("far", far)
    for i in range(1, C):
        gv_col(i).wait_recv()
    gsum = e.gall[2]
    for i in range(1, C):
        gsum = gsum + e.gcol[i]
    e.gsum[...] = gsum

    def gv_row(i):
        return copy(e.gsum, e.grow.at[i], "gv_row", i, to_row(i))

    for i in range(1, R):
        gv_row(i).start()

    e.ab[0] = dot_nt(jnp.ones((8, S), BF16), e.dqkv[...])

    def ab_dp():
        return copy(e.ab.at[0], e.ab.at[1], "ab_dp", 0, partner)

    def ab_col(i):
        return copy(e.ab.at[2], e.abcol.at[i], "ab_col", i, to_col(i))

    ab_dp().start()
    weight_send("dwkv", key_grad)
    ab_dp().wait_recv()
    e.ab[2] = e.ab[0] + e.ab[1]
    for i in range(1, C):
        ab_col(i).start()

    input_part("near", near)
    input_part("over", over)
    input_part("own", me_r)
    e.own_dx[...] = sum_collect(3, "dx") + e.g_first[...].T

    @pl.when(swapped)
    def _():
        swap_copy(e.lo_out, e.layer_out, 2).wait_send()
        swap_copy(e.lo_out, e.layer_out, 2).wait_recv()
        e.lo_out[...] = e.own_dx[...].astype(BF16)
        swap_copy(e.lo_out, e.og_in, 3).start()

    @pl.when(stays)
    def _():
        e.grad_input[...] = e.own_dx[...]

    weight_collect("dw3")
    weight_collect("dw2")
    weight_collect("dwqm")

    vsum = e.gsum[0:8, :D]
    for i in range(1, R):
        gv_row(i).wait_recv()
        vsum = vsum + e.grow[i][:, :D]
    picked = vsum[:, :RB]
    for c in range(1, C):
        picked = jnp.where(me_c == c, vsum[:, c * RB : (c + 1) * RB], picked)
    e.g_vec[...] = picked
    e.g_unit[...] = e.gsum[6:7, :U]
    asum = e.ab[2]
    for i in range(1, C):
        ab_col(i).wait_recv()
        asum = asum + e.abcol[i]
    e.g_ab[0:1, :] = asum[0:1, :F]
    e.g_ab[1:2, :] = asum[0:1, 2 * F :]
    weight_collect("dwkv")
    if dims.flat:
        for name in ("dw3", "dw2", "dwqm", "dwkv"):
            result_copy(name).wait_recv()
    e.g_attn[0] = e.dwqm_sum[:, :F]
    e.g_mix[...] = e.dwqm_sum[:, F:]
    e.g_attn[1] = e.dwkv_sum[:, :F]
    e.g_attn[2] = e.dwkv_sum[:, F:]

    @pl.when(swapped)
    def _():
        swap_copy(e.lo_out, e.og_in, 3).wait_recv()
        e.grad_input[...] = e.og_in[...].astype(F32)

    @pl.when(swapped)
    def _():
        swap_copy(e.x_t, e.x_in, 0).wait_send()
        swap_copy(e.out_grad, e.og_in, 1).wait_send()
        swap_copy(e.lo_out, e.og_in, 3).wait_send()

    len_copy().wait_send()
    for name in ("wkv", "wqm", "w2", "w3"):
        line_close(name)
    gather_close(e.xg, "x")
    gather_close(e.gr_g, "gr")
    gather_close(e.hid_g, "gm")
    for k, family in ((1, "red"), (2, "gh"), (3, "dx")):
        sum_close(k, family)
    for i in range(1, R):
        gv_row(i).wait_send()
    gv_dp().wait_send()
    ab_dp().wait_send()
    for i in range(1, C):
        vec_copy(i).wait_send()
        gv_col(i).wait_send()
        ab_col(i).wait_send()
    for name in ("dw3", "dw2", "dwqm", "dwkv"):
        other_copy(name).wait_send()
        for i in range(1, C):
            d_copy(name, i).wait_send()
        if dims.flat:
            result_copy(name).wait_send()

    for at in range(HC):
        dkv_pass(at, 2).wait_send()

    @pl.when(place < HC - 1)
    def _():
        dkv_right(place + 1).wait_send()

    @pl.when(place > 0)
    def _():
        dkv_left(place - 1).wait_send()


def run_layer(x_t, length, w_attn, w_mixer, w2, w3, out_grad, b_attn, b_expand, **vectors):
    R = lax.axis_size("row")
    C = lax.axis_size("col")
    T = x_t.shape[1]
    S = T * R
    F = w_mixer.shape[1]
    U = w2.shape[1]
    RB = w_mixer.shape[0]
    flat = RB % 32 == 0
    HS = D // H
    dims = SimpleNamespace(
        R=R, C=C, T=T, S=S, F=F, U=U, RB=RB, HS=HS, NH=F // HS,
        flat=flat, HB=RB // 2 if flat else RB, TQ=min(256, S), TR=256, NB=max(1, min(C // 2 - 1, 3)),
    )
    HB = dims.HB
    NH = dims.NH
    slots = slots_of(R, C)
    wide = max(D, U)
    w_shape = (lambda n: (C * RB, n)) if dims.flat else (lambda n: (C, RB, n))
    inputs = dict(
        x_t=x_t, length=length, w_attn=w_attn, w_mixer=w_mixer, w2=w2, w3=w3, out_grad=out_grad,
        b_attn=b_attn, b_expand=b_expand, **vectors,
    )
    outputs = dict(
        layer_out=((D, T), BF16),
        grad_input=((D, T), F32),
        g_attn=((3, RB, F), F32),
        g_mix=((RB, F), F32),
        dw2_sum=((RB, U), F32),
        dw3_sum=((RB, U), F32),
        g_vec=((8, RB), F32),
        g_unit=((1, U), F32),
        g_ab=((2, F), F32),
    )
    scratch = dict(
        xg=((R, T, D), BF16),
        wkv=((RB, 2 * F), BF16),
        wqm=((RB, 2 * F), BF16),
        wkv_g=(w_shape(2 * F), BF16),
        wqm_g=(w_shape(2 * F), BF16),
        w2_g=(w_shape(U), BF16),
        w3_g=(w_shape(U), BF16),
        mix=((D, F), BF16),
        vecr=((C, 8, F), F32),
        vecs=((8, D), F32),
        bias=((1, U), F32),
        kv=((C, 2 * F, S), BF16),
        q_t=((F, S), BF16),
        q_h=((NH, S, HS), BF16),
        x_rows_t=((D, S), BF16),
        top=((NH, S, 1), F32),
        total=((NH, S, 1), F32),
        acc=((NH, S, HS + 16), F32),
        ctx=((S, F), BF16),
        own=((T, D), F32),
        own_dx=((D, T), F32),
        n1=((T, D), F32),
        r1=((T, 1), F32),
        hidden=((T, D), F32),
        hid_g=((R, T, D), BF16),
        active=((S, U), BF16),
        slope=((S, U), F32),
        hid_t=((D, S), BF16),
        g_second=((T, D), F32),
        gr_g=((R, T, D), BF16),
        gr_t=((D, S), BF16),
        g_inner=((S, U), BF16),
        gv=((8, D), F32),
        gu=((8, U), F32),
        gall=((3, 8, wide), F32),
        gcol=((C, 8, wide), F32),
        gsum=((8, wide), F32),
        grow=((R, 8, wide), F32),
        dw_f=((D, U), F32),
        dwqm_sum=((RB, 2 * F), F32),
        dwkv_sum=((RB, 2 * F), F32),
        g_first=((T, D), F32),
        gc_t=((F, S), BF16),
        gc_h=((NH, S, HS), BF16),
        inner_sum=((NH, S, 1), F32),
        dq=((NH, S, HS), F32),
        dkv=((3, 2 * F, S), F32),
        dkv_par=((3, 2 * F, S), BF16),
        lens=((2, 8, 128), F32),
        x_in=((D, T), BF16),
        og_in=((D, T), BF16),
        lo_out=((D, T), BF16),
        dkv_in=((2, dims.NB, 2 * F, S), BF16),
        dqkv=((3 * F, S), BF16),
        ab=((3, 8, 3 * F), F32),
        abcol=((C, 8, 3 * F), F32),
    )
    for k, (rows, width) in enumerate(((T, D), (T, D), (D, T))):
        scratch[f"out_{k}"] = ((3, rows, width), BF16)
        scratch[f"land_{k}"] = ((3, rows, width), BF16)
    for name, width in (("wkv", 2 * F), ("wqm", 2 * F), ("w2", U), ("w3", U)):
        for part in ("out", "in", "land"):
            scratch["d" + name + "_" + part] = ((C, HB, width), BF16)
        if not dims.flat:
            scratch[name + "_f"] = ((C * RB, width), BF16)
    names = list(inputs) + list(outputs) + list(scratch) + ["send_sems", "recv_sems", "credits", "pass_credits"]
    vmem = pl.BlockSpec(memory_space=pltpu.VMEM)
    in_specs = [
        pl.BlockSpec(memory_space=pltpu.SMEM) if name == "length" else vmem for name in inputs
    ]
    results = pl.pallas_call(
        functools.partial(layer_kernel, dims, names),
        out_shape=[jax.ShapeDtypeStruct(s, t) for s, t in outputs.values()],
        in_specs=in_specs,
        out_specs=[vmem] * len(outputs),
        scratch_shapes=[pltpu.VMEM(s, t) for s, t in scratch.values()]
        + [pltpu.SemaphoreType.DMA((slots.total,)), pltpu.SemaphoreType.DMA((slots.total,))]
        + [pltpu.SemaphoreType.REGULAR((2,)), pltpu.SemaphoreType.REGULAR((2,))],
        compiler_params=pltpu.CompilerParams(
            collective_id=0, has_side_effects=True, vmem_limit_bytes=639 * 2**20 // 10
        ),
        name="layer",
    )(*inputs.values())
    return dict(zip(outputs, results))


def finish_kernel(*refs):
    big_in, rows, unit, big_out, vecs, unit_out = (
        refs[:7], refs[7], refs[8], refs[9:16], refs[16:22], refs[22],
    )
    for src, dst in zip(big_in, big_out):
        dst[...] = src[...]
    for k, ref in enumerate(vecs):
        ref[...] = rows[k : k + 1, :].reshape(ref.shape)
    unit_out[...] = unit[...].reshape(unit_out.shape)


def finish(out):
    big = [
        out[name]
        for name in ("layer_out", "grad_input", "g_attn", "g_mix", "dw2_sum", "dw3_sum", "g_ab")
    ]
    rows = out["g_vec"].shape[1]
    units = out["g_unit"].shape[1]
    vmem = pl.BlockSpec(memory_space=pltpu.VMEM)
    shapes = [jax.ShapeDtypeStruct(a.shape, a.dtype) for a in big]
    shapes += [jax.ShapeDtypeStruct((rows,), F32)] * 6 + [jax.ShapeDtypeStruct((units,), F32)]
    return pl.pallas_call(
        finish_kernel,
        out_shape=shapes,
        in_specs=[vmem] * 9,
        out_specs=[vmem] * 14,
        name="finish",
    )(*big, out["g_vec"], out["g_unit"])


def on_device(
    layer_in,
    lengths,
    w_attn,
    b_attn,
    w_mixer,
    b_mixer,
    gain_one,
    shift_one,
    w_expand,
    b_expand,
    w_reduce,
    b_reduce,
    gain_two,
    shift_two,
    out_grad,
):
    out = run_layer(
        layer_in,
        lengths,
        jnp.transpose(w_attn, (1, 0, 2)),
        w_mixer,
        w_expand,
        w_reduce,
        out_grad,
        b_attn,
        b_expand,
        b_mixer=b_mixer,
        gain_one=gain_one,
        shift_one=shift_one,
        b_reduce=b_reduce,
        gain_two=gain_two,
        shift_two=shift_two,
    )
    layer_out, grad_input, g_attn, g_mix, g_expand, g_reduce, g_ab, *vecs, g_unit = finish(out)
    return (
        layer_out,
        grad_input,
        jnp.transpose(g_attn, (1, 0, 2)),
        g_ab,
        g_mix,
        vecs[0],
        vecs[1],
        vecs[2],
        g_expand,
        g_unit,
        g_reduce,
        vecs[3],
        vecs[4],
        vecs[5],
    )


def solution(mesh):
    return jax.shard_map(
        on_device,
        mesh=mesh,
        in_specs=(
            P(None, ("dp", "row", "col")),
            P("dp"),
            P("col", None, "row"),
            P(None, "row"),
            P("col", "row"),
            P("col"),
            P("col"),
            P("col"),
            P("col", "row"),
            P("row"),
            P("col", "row"),
            P("col"),
            P("col"),
            P("col"),
            P(None, ("dp", "row", "col")),
        ),
        out_specs=(
            P(None, ("dp", "row", "col")),
            P(None, ("dp", "row", "col")),
            P("col", None, "row"),
            P(None, "row"),
            P("col", "row"),
            P("col"),
            P("col"),
            P("col"),
            P("col", "row"),
            P("row"),
            P("col", "row"),
            P("col"),
            P("col"),
            P("col"),
        ),
        check_vma=False,
    )
```

```python
import functools
from types import SimpleNamespace

import jax
import jax.numpy as jnp
from jax import lax
from jax.experimental import pallas as pl
from jax.experimental.pallas import tpu as pltpu
from jax.sharding import PartitionSpec as P

D = 768
H = 12
EPSILON = 1e-12
NEGATIVE = -1000000000.0
MESH = pl.DeviceIdType.MESH
F32 = jnp.float32
BF16 = jnp.bfloat16


def dot_nn(left_in, right_in):
    return lax.dot_general(
        left_in, right_in, (((1,), (0,)), ((), ())), preferred_element_type=F32
    )


def dot_nt(left_in, right_in):
    return lax.dot_general(
        left_in, right_in, (((1,), (1,)), ((), ())), preferred_element_type=F32
    )


def turned(values):
    return values.astype(F32).T


def normalize(values):
    row_mean = jnp.mean(values, 1, keepdims=True)
    centered = values - row_mean
    row_var = jnp.mean(centered * centered, 1, keepdims=True)
    row_scale = lax.rsqrt(row_var + EPSILON)
    return centered * row_scale, row_scale


def normalize_back(upstream, normed, row_scale, gain_vec):
    scaled = upstream * gain_vec
    mean_plain = jnp.mean(scaled, 1, keepdims=True)
    mean_cross = jnp.mean(scaled * normed, 1, keepdims=True)
    return row_scale * (scaled - mean_plain - normed * mean_cross)


def column_sum(values):
    return jnp.sum(values, 0, keepdims=True)


class Slots:
    def __init__(self):
        self.base = {}
        self.total = 0

    def add(self, name, count):
        self.base[name] = self.total
        self.total += count


def slots_of(R, C):
    slots = Slots()
    for name in ("x", "hid", "gr", "gm"):
        slots.add(name, 4)
    for name in ("mix", "red", "gh", "dx"):
        slots.add(name, 3)
    slots.add("gv_row", R)
    for name in ("vec", "gv_col", "ab_col", "dkv_right", "dkv_left"):
        slots.add(name, C)
    for name in ("wkv", "wqm", "w2", "w3"):
        slots.add(name + "_right", C)
        slots.add(name + "_left", C)
        slots.add(name + "_dp", C)
        slots.add("d" + name, C)
        slots.add("d" + name + "_dp", 1)
        slots.add("d" + name + "_out", 1)
    slots.add("dkv_pass", C)
    for name in ("kv_pass", "kv_right", "kv_left"):
        slots.add(name, C * R)
    for name in ("gv_dp", "ab_dp", "len"):
        slots.add(name, 1)
    slots.add("swap", 4)
    return slots


def layer_kernel(dims, names, *refs):
    e = SimpleNamespace(**dict(zip(names, refs)))
    R, C, T, S, F, U, RB = dims.R, dims.C, dims.T, dims.S, dims.F, dims.U, dims.RB
    NH, HS, HB = dims.NH, dims.HS, dims.HB
    slots = slots_of(R, C)
    me_d = lax.axis_index("dp")
    me_r = lax.axis_index("row")
    me_c = lax.axis_index("col")

    def to_row(step):
        return {"row": lax.rem(me_r + step, R)}

    def to_col(step):
        return {"col": lax.rem(me_c + step, C)}

    partner = {"dp": 1 - me_d}

    HC = C // 2
    half, place = me_c // HC, lax.rem(me_c, HC)
    mine = me_d * HC + place
    swapped = me_d != half
    stays = me_d == half

    def swap_copy(src, dst, at):
        where = {"dp": 1 - me_d, "col": lax.rem(me_c + HC, C)}
        return copy(src, dst, "swap", at, where)

    def copy(src, dst, family, at, where):
        number = slots.base[family] + at
        return pltpu.make_async_remote_copy(
            src_ref=src,
            dst_ref=dst,
            send_sem=e.send_sems.at[number],
            recv_sem=e.recv_sems.at[number],
            device_id=where,
            device_id_type=MESH,
        )

    barrier = pltpu.get_barrier_semaphore()
    pl.semaphore_signal(barrier, inc=1, device_id=partner, device_id_type=MESH)
    for i in range(1, R):
        pl.semaphore_signal(barrier, inc=1, device_id=to_row(i), device_id_type=MESH)
    for i in range(1, C):
        pl.semaphore_signal(barrier, inc=1, device_id=to_col(i), device_id_type=MESH)
    pl.semaphore_signal(
        barrier,
        inc=1,
        device_id={"dp": 1 - me_d, "col": lax.rem(me_c + HC, C)},
        device_id_type=MESH,
    )
    e.wkv[:, :F] = e.w_attn[1]
    e.wkv[:, F:] = e.w_attn[2]
    e.wqm[:, :F] = e.w_attn[0]
    e.wqm[:, F:] = e.w_mixer[...]
    vectors = (e.b_mixer, e.gain_one, e.shift_one, e.b_reduce, e.gain_two, e.shift_two)
    for k, ref in enumerate(vectors):
        e.vecr[me_c, k : k + 1, :RB] = ref[...].astype(F32).reshape(1, RB)
    e.bias[...] = e.b_expand[...].astype(F32).reshape(1, U)
    e.lens[me_d] = jnp.full((8, 128), e.length[0].astype(F32), F32)
    pl.semaphore_wait(barrier, 2 + (R - 1) + (C - 1))

    @pl.when(swapped)
    def _():
        swap_copy(e.x_t, e.x_in, 0).start()

    @pl.when(stays)
    def _():
        e.x_in[...] = e.x_t[...]
        e.og_in[...] = e.out_grad[...]

    def len_copy():
        return copy(e.lens.at[me_d], e.lens.at[me_d], "len", 0, partner)

    len_copy().start()

    def w_rows(ref, c, d):
        if not dims.flat:
            return ref.at[c]
        return ref.at[pl.ds(pl.multiple_of(c * RB + d * HB, HB), HB)]

    def weight_own(name):
        full = getattr(e, name + "_g")
        if dims.flat:
            full[pl.ds(pl.multiple_of(me_c * RB, RB), RB), :] = getattr(e, name)[...]
        else:
            full[me_c] = getattr(e, name)[...]

    right = {"col": lax.rem(me_c + 1, C)}
    left = {"col": lax.rem(me_c + C - 1, C)}

    def line_copy(name, way, b):
        there = w_rows(getattr(e, name + "_g"), b, me_d)
        return copy(there, there, name + way, b, right if way == "_right" else left)

    def line_pass(name, b):
        there = w_rows(getattr(e, name + "_g"), b, me_d)
        return copy(there, there, name + "_dp", b, partner)

    def line_on(name, way, b):
        pl.when(me_c < C - 1 if way == "_right" else me_c > 0)(line_copy(name, way, b).start)

    def line_start(name):
        line_on(name, "_right", me_c)
        line_on(name, "_left", me_c)

    def line_step(name, step):
        for way, b, there in (
            ("_right", me_c - step, me_c >= step),
            ("_left", me_c + step, me_c + step < C),
        ):

            @pl.when(there)
            def _(way=way, b=b):
                line_copy(name, way, b).wait_recv()
                line_on(name, way, b)
                if dims.flat:
                    line_pass(name, b).start()

    def line_end(name, first=3):
        def step(i, carry):
            line_step(name, i)
            return carry

        lax.fori_loop(min(first, C), C, step, 0)
        if dims.flat:
            for i in range(1, C):
                line_pass(name, lax.rem(me_c + i, C)).wait_recv()
        else:
            full = getattr(e, name + "_g")
            flat = full[...].astype(F32).reshape(C * RB, full.shape[2])
            getattr(e, name + "_f")[...] = flat.astype(BF16)

    def line_close(name):
        def step(b, carry):
            @pl.when((b <= me_c) & (me_c < C - 1))
            def _():
                line_copy(name, "_right", b).wait_send()

            @pl.when((b >= me_c) & (me_c > 0))
            def _():
                line_copy(name, "_left", b).wait_send()

            if dims.flat:

                @pl.when(b != me_c)
                def _():
                    line_pass(name, b).wait_send()

            return carry

        lax.fori_loop(0, C, step, 0)

    wkv, wqm, w2f, w3f = [
        getattr(e, name + ("_g" if dims.flat else "_f")) for name in ("wkv", "wqm", "w2", "w3")
    ]

    beside = {"row": me_r + 1 - 2 * lax.rem(me_r, 2)}
    across = {"row": lax.rem(me_r + 2, R)}
    near, over, far = beside["row"], across["row"], R - 1 - me_r
    low, high = pl.ds(0, T // 2), pl.ds(T // 2, T // 2)

    def gather_copy(ref, family, at):
        part, where = (
            (ref.at[me_r], beside),
            (ref.at[me_r], across),
            (ref.at[near, low], across),
            (ref.at[over, high], beside),
        )[at]
        return copy(part, part, family, at, where)

    def gather_start(ref, family):
        gather_copy(ref, family, 0).start()
        gather_copy(ref, family, 1).start()

    def gather_near(ref, family):
        gather_copy(ref, family, 0).wait_recv()
        gather_copy(ref, family, 2).start()

    def gather_over(ref, family):
        gather_copy(ref, family, 1).wait_recv()
        gather_copy(ref, family, 3).start()

    def gather_far(ref, family):
        gather_copy(ref, family, 2).wait_recv()
        gather_copy(ref, family, 3).wait_recv()

    def gather_close(ref, family):
        for at in range(4):
            gather_copy(ref, family, at).wait_send()

    def each(count, body):
        def step(j, carry):
            body(j)
            return carry

        lax.fori_loop(0, count, step, 0)

    def gathered(ref, family):
        yield "own", me_r
        gather_near(ref, family)
        gather_over(ref, family)
        yield "near", near
        yield "over", over
        gather_far(ref, family)
        yield "far", far

    def sum_copy(k, family, kind):
        at = ("near", "over", "far").index(kind)
        where = (beside, across, {"row": far})[at]
        out, land, _ = e.sums[k]
        return copy(out.at[at], land.at[at], family, at, where)

    def sum_add(k, family, kind, part):
        out, _, own = e.sums[k]
        if kind == "own":
            own[...] = part
        else:
            out[("near", "over", "far").index(kind)] = part.astype(BF16)
            sum_copy(k, family, kind).start()

    def sum_collect(k, family):
        _, land, own = e.sums[k]
        total = own[...]
        for at, kind in enumerate(("near", "over", "far")):
            sum_copy(k, family, kind).wait_recv()
            total = total + land[at].astype(F32)
        return total

    def sum_close(k, family):
        for kind in ("near", "over", "far"):
            sum_copy(k, family, kind).wait_send()

    e.sums = [
        (getattr(e, f"out_{k}"), getattr(e, f"land_{k}"), own)
        for k, own in ((0, e.own), (1, e.own), (0, e.own), (2, e.own_dx))
    ]

    def vec_copy(i):
        return copy(e.vecr.at[me_c], e.vecr.at[me_c], "vec", i, to_col(i))

    for name in ("wkv", "wqm", "w2", "w3"):
        weight_own(name)
    line_start("wkv")
    line_start("wqm")

    @pl.when(swapped)
    def _():
        swap_copy(e.x_t, e.x_in, 0).wait_recv()

    e.xg[me_r] = turned(e.x_in[...]).astype(BF16)
    gather_start(e.xg, "x")
    for step in range(1, min(3, C)):
        line_step("wkv", step)
        line_step("wqm", step)

    len_copy().wait_recv()
    length = e.lens[half][0:1, 0:1]
    for i in range(1, C):
        vec_copy(i).start()
    gather_near(e.xg, "x")
    gather_over(e.xg, "x")
    line_end("wkv")

    def of_core(d, at):
        return d * HC + at

    def kv_copy(b, i, family, where):
        part = e.kv.at[b, :, pl.ds(pl.multiple_of(i * T, T), T)]
        return copy(part, part, family, b * R + i, where)

    def kv_right(b, i):
        return kv_copy(b, i, "kv_right", right)

    def kv_left(b, i):
        return kv_copy(b, i, "kv_left", left)

    def kv_pass(b, i):
        return kv_copy(b, i, "kv_pass", partner)

    def kv_on(b, i):
        pl.when(place < HC - 1)(kv_right(b, i).start)
        pl.when(place > 0)(kv_left(b, i).start)
        kv_pass(b, i).start()

    for kind, rb in (("own", me_r), ("near", near), ("over", over), ("far", far)):
        if kind == "far":
            gather_far(e.xg, "x")
        tokens = pl.ds(pl.multiple_of(rb * T, T), T)
        both = dot_nn(e.xg[rb], wkv[...])
        values = both[:, F:] + e.b_attn[1:2, :].astype(F32)
        e.kv[mine, pl.ds(0, F), tokens] = both[:, :F].T.astype(BF16)
        e.kv[mine, pl.ds(F, F), tokens] = values.T.astype(BF16)
        kv_on(mine, rb)

    def make_queries():
        line_end("wqm")
        e.mix[...] = wqm[:, F:]
        for i in range(R):
            tokens = pl.ds(i * T, T)
            block = e.xg[i]
            q = dot_nn(block, wqm[:, :F]) + e.b_attn[0:1, :].astype(F32)
            q = q.astype(BF16).astype(F32) * (HS ** (-0.5))
            e.q_t[:, tokens] = q.T.astype(BF16)
            for h in range(NH):
                e.q_h[h, tokens, :] = q[:, h * HS : (h + 1) * HS].astype(BF16)
            e.x_rows_t[:, tokens] = turned(block).astype(BF16)

    def key_valid(b):
        lane = lax.broadcasted_iota(jnp.int32, (1, S), 1)
        return (lane // T * (T * C) + b * T + lane % T).astype(F32) < length

    TQ = dims.TQ
    e.top[...] = jnp.full(e.top.shape, -3e38, F32)
    e.acc[...] = jnp.zeros(e.acc.shape, F32)
    ones = jnp.ones((16, S), BF16)

    def tiles(body):
        if TQ == S:
            body(0, 0)
        else:
            lax.fori_loop(0, S // TQ, body, 0)

    def attend(at):
        blocks = (of_core(0, at), of_core(1, at))
        valid = [key_valid(b) for b in blocks]

        def tile(t, carry):
            rows = pl.ds(pl.multiple_of(t * TQ, TQ), TQ)
            for h in range(NH):
                scores = [
                    jnp.where(
                        ok,
                        dot_nn(e.q_h[h, rows, :], e.kv[b, h * HS : (h + 1) * HS, :]),
                        NEGATIVE,
                    )
                    for b, ok in zip(blocks, valid)
                ]
                old = e.top[h, rows, :]
                new = jnp.maximum(
                    old, jnp.max(jnp.maximum(*scores), 1, keepdims=True)
                )
                e.top[h, rows, :] = new
                part = jnp.exp(old - new) * e.acc[h, rows, :]
                for b, score in zip(blocks, scores):
                    values = e.kv[b, F + h * HS : F + (h + 1) * HS, :]
                    part = part + dot_nt(
                        jnp.exp(score - new).astype(BF16), jnp.concatenate([values, ones], 0)
                    )
                e.acc[h, rows, :] = part
            return carry

        tiles(tile)

    make_queries()

    def kv_step(s, carry):
        from_left = place - s
        from_right = place + s

        @pl.when((s > 0) & (from_left >= 0))
        def _():
            b = of_core(me_d, from_left)

            @functools.partial(each, R)
            def _(i):
                kv_right(b, i).wait_recv()
                kv_pass(b, i).start()
                pl.when(place < HC - 1)(kv_right(b, i).start)

        @pl.when((s > 0) & (from_right < HC))
        def _():
            b = of_core(me_d, from_right)

            @functools.partial(each, R)
            def _(i):
                kv_left(b, i).wait_recv()
                kv_pass(b, i).start()
                pl.when(place > 0)(kv_left(b, i).start)

        @pl.when(s == HC - 1)
        def _():
            line_start("w2")
            line_start("w3")

        @functools.partial(each, 2)
        def _(k):
            at = jnp.where(k == 0, from_left, from_right)

            @pl.when((at >= 0) & (at < HC) & ((s > 0) | (k == 0)))
            def _():
                each(R, lambda i: kv_pass(of_core(1 - me_d, at), i).wait_recv())
                attend(at)

        return carry

    lax.fori_loop(0, HC, kv_step, 0)

    def kv_close(at, carry):
        b = of_core(me_d, at)

        @functools.partial(each, R)
        def _(i):
            kv_pass(b, i).wait_send()

            @pl.when((at <= place) & (place < HC - 1))
            def _():
                kv_right(b, i).wait_send()

            @pl.when((at >= place) & (place > 0))
            def _():
                kv_left(b, i).wait_send()

        return carry

    lax.fori_loop(0, HC, kv_close, 0)

    for h in range(NH):
        inverse = 1.0 / e.acc[h, :, HS : HS + 1]
        e.total[h] = inverse
        context = e.acc[h, :, :HS] * inverse
        e.acc[h, :, :HS] = context
        e.ctx[:, h * HS : (h + 1) * HS] = context.astype(BF16)

    for i in range(1, C):
        vec_copy(i).wait_recv()
    for c in range(C):
        e.vecs[:, c * RB : (c + 1) * RB] = e.vecr[c][:, :RB]

    def vector(at):
        return e.vecs[at : at + 1, :]

    def blk_rows(rb):
        return pl.ds(pl.multiple_of(rb * T, T), T)

    for kind, rb in (("far", far), ("near", near), ("over", over), ("own", me_r)):
        sum_add(0, "mix", kind, dot_nt(e.ctx[blk_rows(rb), :], e.mix[...]))

    line_step("w2", 1)
    line_step("w3", 1)
    first_sum = turned(e.x_in[...]) + sum_collect(0, "mix") + vector(0)
    normed, scale = normalize(first_sum)
    hidden = normed * vector(1) + vector(2)
    e.n1[...] = normed
    e.r1[...] = scale
    e.hidden[...] = hidden
    e.hid_g[me_r] = hidden.astype(BF16)

    gather_start(e.hid_g, "hid")

    @pl.when(swapped)
    def _():
        swap_copy(e.out_grad, e.og_in, 1).start()

    if C > 2:
        line_step("w2", 2)
        line_step("w3", 2)
    line_end("w2")

    for kind, rb in gathered(e.hid_g, "hid"):
        inner = dot_nn(e.hid_g[rb], w2f[...]) + e.bias[...]
        cdf = 0.5 * (1.0 + lax.erf(inner * (0.5**0.5)))
        active = (inner * cdf).astype(BF16)
        slope = cdf + inner * (jnp.exp(-0.5 * inner * inner) * 0.3989422804014327)
        e.active[blk_rows(rb), :] = active
        e.slope[blk_rows(rb), :] = slope
        if kind == "own":
            continue
        if kind == "near":
            line_end("w3")
            sum_add(1, "red", "own", dot_nt(e.active[blk_rows(me_r), :], w3f[...]))
        sum_add(1, "red", kind, dot_nt(e.active[blk_rows(rb), :], w3f[...]))
    for i in range(R):
        e.hid_t[:, i * T : (i + 1) * T] = turned(e.hid_g[i]).astype(BF16)
    gather_close(e.hid_g, "hid")

    second_sum = e.hidden[...] + sum_collect(1, "red") + vector(3)
    normed, scale = normalize(second_sum)
    slot = lax.broadcasted_iota(jnp.int32, (T, 1), 0) + (me_r * (T * C) + mine * T)
    row_valid = (slot.astype(F32) < length).astype(F32)

    @pl.when(swapped)
    def _():
        swap_copy(e.out_grad, e.og_in, 1).wait_recv()

    upstream = turned(e.og_in[...]) * row_valid
    g_second = normalize_back(upstream, normed, scale, vector(4))
    g_reduced = g_second.astype(BF16)
    e.gr_g[me_r] = g_reduced
    gather_start(e.gr_g, "gr")
    e.lo_out[...] = ((normed * vector(4) + vector(5)) * row_valid).T.astype(BF16)

    @pl.when(swapped)
    def _():
        swap_copy(e.lo_out, e.layer_out, 2).start()

    @pl.when(stays)
    def _():
        e.layer_out[...] = e.lo_out[...]

    e.g_second[...] = g_second
    e.gv[4:5, :] = column_sum(upstream * normed)
    e.gv[5:6, :] = column_sum(upstream)
    e.gv[3:4, :] = column_sum(g_reduced.astype(F32))
    e.gv[7:8, :] = jnp.zeros((1, D), F32)

    unit_sum = jnp.zeros((1, U), F32)
    sum_close(0, "mix")
    for kind, rb in gathered(e.gr_g, "gr"):
        g_active = dot_nn(e.gr_g[rb], w3f[...]).astype(BF16).astype(F32)
        g_inner = (g_active * e.slope[blk_rows(rb), :]).astype(BF16)
        e.g_inner[blk_rows(rb), :] = g_inner
        unit_sum = unit_sum + column_sum(g_inner.astype(F32))
        sum_add(2, "gh", kind, dot_nt(e.g_inner[blk_rows(rb), :], w2f[...]))
    e.gu[0:1, :] = unit_sum
    for i in range(R):
        e.gr_t[:, i * T : (i + 1) * T] = turned(e.gr_g[i]).astype(BF16)

    TR = dims.TR

    def half_rows(c, d):
        if not dims.flat:
            return pl.ds(c * RB, RB)
        return pl.ds(pl.multiple_of(c * RB + d * HB, HB), HB)

    def other_copy(name):
        return copy(getattr(e, name + "_out"), getattr(e, name + "_in"), name + "_dp", 0, partner)

    def d_copy(name, i):
        stage = getattr(e, name + "_in").at[lax.rem(me_c + i, C)]
        return copy(stage, getattr(e, name + "_land").at[i], name, i, to_col(i))

    def row_tiles(fill):
        def tile(t, carry):
            fill(pl.ds(pl.multiple_of(t * TR, TR), TR))
            return carry

        lax.fori_loop(0, D // TR, tile, 0)

    def weight_swap(name, source):
        def block(c, carry):
            getattr(e, name + "_out")[c] = source[half_rows(c, 1 - me_d), :].astype(BF16)
            return carry

        lax.fori_loop(0, C, block, 0)
        other_copy(name).start()

    def weight_send(name, source):
        other_copy(name).wait_recv()

        def block(c, carry):
            total = source[half_rows(c, me_d), :] + getattr(e, name + "_in")[c].astype(F32)
            getattr(e, name + "_in")[c] = total.astype(BF16)
            return carry

        lax.fori_loop(0, C, block, 0)
        for i in range(1, C):
            d_copy(name, i).start()

    def result_part(name):
        full = getattr(e, name + "_sum")
        return full.at[pl.ds(pl.multiple_of(me_d * HB, HB), HB)] if dims.flat else full

    def result_copy(name):
        return copy(result_part(name), result_part(name), name + "_out", 0, partner)

    def weight_collect(name):
        total = getattr(e, name + "_in")[me_c].astype(F32)
        for i in range(1, C):
            d_copy(name, i).wait_recv()
            total = total + getattr(e, name + "_land")[i].astype(F32)
        result_part(name)[...] = total
        if dims.flat:
            result_copy(name).start()

    def fill_reduce(rows):
        e.dw_f[rows, :] = dot_nn(e.gr_t[rows, :], e.active[...])

    def fill_expand(rows):
        e.dw_f[rows, :] = dot_nn(e.hid_t[rows, :], e.g_inner[...])

    row_tiles(fill_reduce)
    weight_swap("dw3", e.dw_f)
    weight_send("dw3", e.dw_f)
    row_tiles(fill_expand)
    weight_swap("dw2", e.dw_f)
    weight_send("dw2", e.dw_f)

    g_hidden = sum_collect(2, "gh") + e.g_second[...]
    normed = e.n1[...]
    g_first = normalize_back(g_hidden, normed, e.r1[...], vector(1))
    g_mixed = g_first.astype(BF16)
    e.hid_g[me_r] = g_mixed
    gather_start(e.hid_g, "gm")
    e.g_first[...] = g_first
    e.gv[1:2, :] = column_sum(g_hidden * normed)
    e.gv[2:3, :] = column_sum(g_hidden)
    e.gv[0:1, :] = column_sum(g_mixed.astype(F32))
    e.gv[6:7, :] = jnp.zeros((1, D), F32)

    def gv_dp():
        return copy(e.gall.at[0], e.gall.at[1], "gv_dp", 0, partner)

    e.gall[0, :, :D] = e.gv[...]
    e.gall[0, 6:7, :U] = e.gu[0:1, :]
    gv_dp().start()

    for _, rb in gathered(e.hid_g, "gm"):
        rows = blk_rows(rb)
        g_context = dot_nn(e.hid_g[rb], e.mix[...]).astype(BF16).astype(F32)
        e.gc_t[:, rows] = g_context.T.astype(BF16)
        for h in range(NH):
            part = g_context[:, h * HS : (h + 1) * HS]
            e.gc_h[h, rows, :] = part.astype(BF16)
            e.inner_sum[h, rows, :] = jnp.sum(part * e.acc[h, rows, :HS], 1, keepdims=True)
        e.gr_t[:, rows] = turned(e.hid_g[rb]).astype(BF16)

    def gv_col(i):
        return copy(e.gall.at[2], e.gcol.at[i], "gv_col", i, to_col(i))

    e.dq[...] = jnp.zeros(e.dq.shape, F32)

    def attend_back(b, to):
        valid = key_valid(b)
        for h in range(NH):
            krows = slice(h * HS, (h + 1) * HS)
            vrows = slice(F + h * HS, F + (h + 1) * HS)

            def tile(t, carry):
                d_keys, d_values = carry
                rows = pl.ds(pl.multiple_of(t * TQ, TQ), TQ)
                keys = e.kv[b, krows, :]
                values = e.kv[b, vrows, :]
                scores = dot_nn(e.q_h[h, rows, :], keys)
                scores = jnp.where(valid, scores, NEGATIVE)
                probs = jnp.exp(scores - e.top[h, rows, :]) * e.total[h, rows, :]
                g_weights = dot_nn(e.gc_h[h, rows, :], values)
                g_scores = (probs * (g_weights - e.inner_sum[h, rows, :])).astype(BF16)
                e.dq[h, rows, :] += dot_nt(g_scores, keys)
                d_keys = d_keys + dot_nn(e.q_t[krows, rows], g_scores)
                d_values = d_values + dot_nn(e.gc_t[krows, rows], probs.astype(BF16))
                return d_keys, d_values

            zero = jnp.zeros((HS, S), F32)
            if TQ == S:
                d_keys, d_values = tile(0, (zero, zero))
            else:
                d_keys, d_values = lax.fori_loop(0, S // TQ, tile, (zero, zero))
            e.dkv[to, krows, :] = d_keys
            e.dkv[to, vrows, :] = d_values

    NB = dims.NB

    def dkv_right(at):
        b = of_core(me_d, at)
        return copy(
            e.kv.at[b], e.dkv_in.at[0, lax.rem(HC - 1 - at, NB)], "dkv_right", at, right
        )

    def dkv_left(at):
        b = of_core(me_d, at)
        return copy(e.kv.at[b], e.dkv_in.at[1, lax.rem(at, NB)], "dkv_left", at, left)

    def dkv_send(way, at):
        order = HC - 1 - at if way == 0 else at
        if HC - 1 > NB:

            @pl.when(order >= NB)
            def _():
                pl.semaphore_wait(e.credits.at[way], 1)

        if way == 0:

            @pl.when(at < HC - 1)
            def _():
                dkv_right(at + 1).wait_send()

            dkv_right(at).start()
        else:

            @pl.when(at > 0)
            def _():
                dkv_left(at - 1).wait_send()

            dkv_left(at).start()

    def dkv_take(way, at, to):
        order = HC - 1 - at if way == 0 else at
        (dkv_right if way == 0 else dkv_left)(at).wait_recv()
        e.dkv[to] += e.dkv_in[way, lax.rem(order, NB)].astype(F32)
        if HC - 1 > NB:
            sends = HC - place if way == 0 else place + 1

            @pl.when(order + NB < sends)
            def _():
                pl.semaphore_signal(
                    e.credits.at[way],
                    inc=1,
                    device_id=left if way == 0 else right,
                    device_id_type=MESH,
                )

    def dkv_pass(at, to):
        b = of_core(1 - me_d, at)
        return copy(e.kv.at[b], e.dkv_par.at[to], "dkv_pass", at, partner)

    def both_cores(at, to):
        first = jnp.where(to == 0, at == HC - 1, at == 0)
        last = jnp.where(to == 0, at == place + 1, at == place - 1)

        @functools.partial(each, 2)
        def _(k):
            b = of_core(jnp.where(k == 0, 1 - me_d, me_d), at)
            attend_back(b, to)

            @pl.when(k == 0)
            def _():
                e.kv[b] = e.dkv[to].astype(BF16)
                if HC > 2:

                    @pl.when((to < 2) & jnp.logical_not(first))
                    def _():
                        pl.semaphore_wait(e.pass_credits.at[to], 1)

                dkv_pass(at, to).start()

        dkv_pass(at, to).wait_recv()
        e.dkv[to] += e.dkv_par[to].astype(F32)
        if HC > 2:

            @pl.when((to < 2) & jnp.logical_not(last))
            def _():
                pl.semaphore_signal(
                    e.pass_credits.at[to], inc=1, device_id=partner, device_id_type=MESH
                )

    def dkv_step(n, carry):
        s, way = n // 2, lax.rem(n, 2)
        own = s == HC - 1
        at = jnp.where(way == 0, HC - 1 + place - s, s - (HC - 1 - place))
        there = jnp.where(own, way == 0, jnp.where(way == 0, s >= place, at >= 0))

        @pl.when(there)
        def _():
            both_cores(at, jnp.where(own, 2, way))

            @pl.when(jnp.logical_not(own) & (way == 0))
            def _():
                @pl.when(place > 0)
                def _():
                    dkv_take(0, at, 0)

                e.kv[of_core(me_d, at)] = e.dkv[0].astype(BF16)
                dkv_send(0, at)

            @pl.when(jnp.logical_not(own) & (way == 1))
            def _():
                @pl.when(place < HC - 1)
                def _():
                    dkv_take(1, at, 1)

                e.kv[of_core(me_d, at)] = e.dkv[1].astype(BF16)
                dkv_send(1, at)

        return carry

    lax.fori_loop(0, 2 * HC, dkv_step, 0)

    for h in range(NH):
        e.dqkv[h * HS : (h + 1) * HS, :] = (e.dq[h] * (HS ** (-0.5))).T.astype(BF16)

    def fill_query(rows):
        e.dw_f[rows, :F] = dot_nt(e.x_rows_t[rows, :], e.dqkv[:F, :])
        e.dw_f[rows, F : 2 * F] = dot_nn(e.gr_t[rows, :], e.ctx[...])

    row_tiles(fill_query)
    query_grad = e.dw_f.at[:, pl.ds(0, 2 * F)]
    weight_swap("dwqm", query_grad)
    gv_dp().wait_recv()
    e.gall[2] = e.gall[0] + e.gall[1]
    for i in range(1, C):
        gv_col(i).start()
    weight_send("dwqm", query_grad)
    weight_collect("dw3")
    weight_collect("dw2")

    @pl.when(place > 0)
    def _():
        dkv_take(0, place, 2)

    @pl.when(place < HC - 1)
    def _():
        dkv_take(1, place, 2)

    e.dqkv[F : 3 * F, :] = e.dkv[2].astype(BF16)

    def fill_keys(rows):
        e.dw_f[rows, 2 * F :] = dot_nt(e.x_rows_t[rows, :], e.dqkv[F:, :])

    row_tiles(fill_keys)
    key_grad = e.dw_f.at[:, pl.ds(2 * F, 2 * F)]
    weight_swap("dwkv", key_grad)

    def input_part(kind, rb):
        part = dot_nn(wqm[:, :F], e.dqkv[:F, blk_rows(rb)])
        part = part + dot_nn(wkv[...], e.dqkv[F:, blk_rows(rb)])
        sum_add(3, "dx", kind, part)

    input_part("far", far)
    for i in range(1, C):
        gv_col(i).wait_recv()
    gsum = e.gall[2]
    for i in range(1, C):
        gsum = gsum + e.gcol[i]
    e.gsum[...] = gsum

    def gv_row(i):
        return copy(e.gsum, e.grow.at[i], "gv_row", i, to_row(i))

    for i in range(1, R):
        gv_row(i).start()

    e.ab[0] = dot_nt(jnp.ones((8, S), BF16), e.dqkv[...])

    def ab_dp():
        return copy(e.ab.at[0], e.ab.at[1], "ab_dp", 0, partner)

    def ab_col(i):
        return copy(e.ab.at[2], e.abcol.at[i], "ab_col", i, to_col(i))

    ab_dp().start()
    weight_send("dwkv", key_grad)
    ab_dp().wait_recv()
    e.ab[2] = e.ab[0] + e.ab[1]
    for i in range(1, C):
        ab_col(i).start()

    input_part("near", near)
    input_part("over", over)
    input_part("own", me_r)
    e.own_dx[...] = sum_collect(3, "dx") + e.g_first[...].T

    @pl.when(swapped)
    def _():
        swap_copy(e.lo_out, e.layer_out, 2).wait_send()
        swap_copy(e.lo_out, e.layer_out, 2).wait_recv()
        e.lo_out[...] = e.own_dx[...].astype(BF16)
        swap_copy(e.lo_out, e.og_in, 3).start()

    @pl.when(stays)
    def _():
        e.grad_input[...] = e.own_dx[...]

    weight_collect("dwqm")

    vsum = e.gsum[0:8, :D]
    for i in range(1, R):
        gv_row(i).wait_recv()
        vsum = vsum + e.grow[i][:, :D]
    picked = vsum[:, :RB]
    for c in range(1, C):
        picked = jnp.where(me_c == c, vsum[:, c * RB : (c + 1) * RB], picked)
    e.g_vec[...] = picked
    e.g_unit[...] = e.gsum[6:7, :U]
    asum = e.ab[2]
    for i in range(1, C):
        ab_col(i).wait_recv()
        asum = asum + e.abcol[i]
    e.g_ab[0:1, :] = asum[0:1, :F]
    e.g_ab[1:2, :] = asum[0:1, 2 * F :]
    weight_collect("dwkv")
    if dims.flat:
        for name in ("dw3", "dw2", "dwqm", "dwkv"):
            result_copy(name).wait_recv()
    e.g_attn[0] = e.dwqm_sum[:, :F]
    e.g_mix[...] = e.dwqm_sum[:, F:]
    e.g_attn[1] = e.dwkv_sum[:, :F]
    e.g_attn[2] = e.dwkv_sum[:, F:]

    @pl.when(swapped)
    def _():
        swap_copy(e.lo_out, e.og_in, 3).wait_recv()
        e.grad_input[...] = e.og_in[...].astype(F32)

    @pl.when(swapped)
    def _():
        swap_copy(e.x_t, e.x_in, 0).wait_send()
        swap_copy(e.out_grad, e.og_in, 1).wait_send()
        swap_copy(e.lo_out, e.og_in, 3).wait_send()

    len_copy().wait_send()
    for name in ("wkv", "wqm", "w2", "w3"):
        line_close(name)
    gather_close(e.xg, "x")
    gather_close(e.gr_g, "gr")
    gather_close(e.hid_g, "gm")
    for k, family in ((1, "red"), (2, "gh"), (3, "dx")):
        sum_close(k, family)
    for i in range(1, R):
        gv_row(i).wait_send()
    gv_dp().wait_send()
    ab_dp().wait_send()
    for i in range(1, C):
        vec_copy(i).wait_send()
        gv_col(i).wait_send()
        ab_col(i).wait_send()
    for name in ("dw3", "dw2", "dwqm", "dwkv"):
        other_copy(name).wait_send()
        for i in range(1, C):
            d_copy(name, i).wait_send()
        if dims.flat:
            result_copy(name).wait_send()

    for at in range(HC):
        dkv_pass(at, 2).wait_send()

    @pl.when(place < HC - 1)
    def _():
        dkv_right(place + 1).wait_send()

    @pl.when(place > 0)
    def _():
        dkv_left(place - 1).wait_send()


def run_layer(x_t, length, w_attn, w_mixer, w2, w3, out_grad, b_attn, b_expand, **vectors):
    R = lax.axis_size("row")
    C = lax.axis_size("col")
    T = x_t.shape[1]
    S = T * R
    F = w_mixer.shape[1]
    U = w2.shape[1]
    RB = w_mixer.shape[0]
    flat = RB % 32 == 0
    HS = D // H
    dims = SimpleNamespace(
        R=R, C=C, T=T, S=S, F=F, U=U, RB=RB, HS=HS, NH=F // HS,
        flat=flat, HB=RB // 2 if flat else RB, TQ=min(256, S), TR=256, NB=max(1, min(C // 2 - 1, 3)),
    )
    HB = dims.HB
    NH = dims.NH
    slots = slots_of(R, C)
    wide = max(D, U)
    w_shape = (lambda n: (C * RB, n)) if dims.flat else (lambda n: (C, RB, n))
    inputs = dict(
        x_t=x_t, length=length, w_attn=w_attn, w_mixer=w_mixer, w2=w2, w3=w3, out_grad=out_grad,
        b_attn=b_attn, b_expand=b_expand, **vectors,
    )
    outputs = dict(
        layer_out=((D, T), BF16),
        grad_input=((D, T), F32),
        g_attn=((3, RB, F), F32),
        g_mix=((RB, F), F32),
        dw2_sum=((RB, U), F32),
        dw3_sum=((RB, U), F32),
        g_vec=((8, RB), F32),
        g_unit=((1, U), F32),
        g_ab=((2, F), F32),
    )
    scratch = dict(
        xg=((R, T, D), BF16),
        wkv=((RB, 2 * F), BF16),
        wqm=((RB, 2 * F), BF16),
        wkv_g=(w_shape(2 * F), BF16),
        wqm_g=(w_shape(2 * F), BF16),
        w2_g=(w_shape(U), BF16),
        w3_g=(w_shape(U), BF16),
        mix=((D, F), BF16),
        vecr=((C, 8, F), F32),
        vecs=((8, D), F32),
        bias=((1, U), F32),
        kv=((C, 2 * F, S), BF16),
        q_t=((F, S), BF16),
        q_h=((NH, S, HS), BF16),
        x_rows_t=((D, S), BF16),
        top=((NH, S, 1), F32),
        total=((NH, S, 1), F32),
        acc=((NH, S, HS + 16), F32),
        ctx=((S, F), BF16),
        own=((T, D), F32),
        own_dx=((D, T), F32),
        n1=((T, D), F32),
        r1=((T, 1), F32),
        hidden=((T, D), F32),
        hid_g=((R, T, D), BF16),
        active=((S, U), BF16),
        slope=((S, U), F32),
        hid_t=((D, S), BF16),
        g_second=((T, D), F32),
        gr_g=((R, T, D), BF16),
        gr_t=((D, S), BF16),
        g_inner=((S, U), BF16),
        gv=((8, D), F32),
        gu=((8, U), F32),
        gall=((3, 8, wide), F32),
        gcol=((C, 8, wide), F32),
        gsum=((8, wide), F32),
        grow=((R, 8, wide), F32),
        dw_f=((D, U), F32),
        dwqm_sum=((RB, 2 * F), F32),
        dwkv_sum=((RB, 2 * F), F32),
        g_first=((T, D), F32),
        gc_t=((F, S), BF16),
        gc_h=((NH, S, HS), BF16),
        inner_sum=((NH, S, 1), F32),
        dq=((NH, S, HS), F32),
        dkv=((3, 2 * F, S), F32),
        dkv_par=((3, 2 * F, S), BF16),
        lens=((2, 8, 128), F32),
        x_in=((D, T), BF16),
        og_in=((D, T), BF16),
        lo_out=((D, T), BF16),
        dkv_in=((2, dims.NB, 2 * F, S), BF16),
        dqkv=((3 * F, S), BF16),
        ab=((3, 8, 3 * F), F32),
        abcol=((C, 8, 3 * F), F32),
    )
    for k, (rows, width) in enumerate(((T, D), (T, D), (D, T))):
        scratch[f"out_{k}"] = ((3, rows, width), BF16)
        scratch[f"land_{k}"] = ((3, rows, width), BF16)
    for name, width in (("wkv", 2 * F), ("wqm", 2 * F), ("w2", U), ("w3", U)):
        for part in ("out", "in", "land"):
            scratch["d" + name + "_" + part] = ((C, HB, width), BF16)
        if not dims.flat:
            scratch[name + "_f"] = ((C * RB, width), BF16)
    names = list(inputs) + list(outputs) + list(scratch) + ["send_sems", "recv_sems", "credits", "pass_credits"]
    vmem = pl.BlockSpec(memory_space=pltpu.VMEM)
    in_specs = [
        pl.BlockSpec(memory_space=pltpu.SMEM) if name == "length" else vmem for name in inputs
    ]
    results = pl.pallas_call(
        functools.partial(layer_kernel, dims, names),
        out_shape=[jax.ShapeDtypeStruct(s, t) for s, t in outputs.values()],
        in_specs=in_specs,
        out_specs=[vmem] * len(outputs),
        scratch_shapes=[pltpu.VMEM(s, t) for s, t in scratch.values()]
        + [pltpu.SemaphoreType.DMA((slots.total,)), pltpu.SemaphoreType.DMA((slots.total,))]
        + [pltpu.SemaphoreType.REGULAR((2,)), pltpu.SemaphoreType.REGULAR((2,))],
        compiler_params=pltpu.CompilerParams(
            collective_id=0, has_side_effects=True, vmem_limit_bytes=639 * 2**20 // 10
        ),
        name="layer",
    )(*inputs.values())
    return dict(zip(outputs, results))


def finish_kernel(*refs):
    big_in, rows, unit, big_out, vecs, unit_out = (
        refs[:7], refs[7], refs[8], refs[9:16], refs[16:22], refs[22],
    )
    for src, dst in zip(big_in, big_out):
        dst[...] = src[...]
    for k, ref in enumerate(vecs):
        ref[...] = rows[k : k + 1, :].reshape(ref.shape)
    unit_out[...] = unit[...].reshape(unit_out.shape)


def finish(out):
    big = [
        out[name]
        for name in ("layer_out", "grad_input", "g_attn", "g_mix", "dw2_sum", "dw3_sum", "g_ab")
    ]
    rows = out["g_vec"].shape[1]
    units = out["g_unit"].shape[1]
    vmem = pl.BlockSpec(memory_space=pltpu.VMEM)
    shapes = [jax.ShapeDtypeStruct(a.shape, a.dtype) for a in big]
    shapes += [jax.ShapeDtypeStruct((rows,), F32)] * 6 + [jax.ShapeDtypeStruct((units,), F32)]
    return pl.pallas_call(
        finish_kernel,
        out_shape=shapes,
        in_specs=[vmem] * 9,
        out_specs=[vmem] * 14,
        name="finish",
    )(*big, out["g_vec"], out["g_unit"])


def on_device(
    layer_in,
    lengths,
    w_attn,
    b_attn,
    w_mixer,
    b_mixer,
    gain_one,
    shift_one,
    w_expand,
    b_expand,
    w_reduce,
    b_reduce,
    gain_two,
    shift_two,
    out_grad,
):
    out = run_layer(
        layer_in,
        lengths,
        jnp.transpose(w_attn, (1, 0, 2)),
        w_mixer,
        w_expand,
        w_reduce,
        out_grad,
        b_attn,
        b_expand,
        b_mixer=b_mixer,
        gain_one=gain_one,
        shift_one=shift_one,
        b_reduce=b_reduce,
        gain_two=gain_two,
        shift_two=shift_two,
    )
    layer_out, grad_input, g_attn, g_mix, g_expand, g_reduce, g_ab, *vecs, g_unit = finish(out)
    return (
        layer_out,
        grad_input,
        jnp.transpose(g_attn, (1, 0, 2)),
        g_ab,
        g_mix,
        vecs[0],
        vecs[1],
        vecs[2],
        g_expand,
        g_unit,
        g_reduce,
        vecs[3],
        vecs[4],
        vecs[5],
    )


def solution(mesh):
    return jax.shard_map(
        on_device,
        mesh=mesh,
        in_specs=(
            P(None, ("dp", "row", "col")),
            P("dp"),
            P("col", None, "row"),
            P(None, "row"),
            P("col", "row"),
            P("col"),
            P("col"),
            P("col"),
            P("col", "row"),
            P("row"),
            P("col", "row"),
            P("col"),
            P("col"),
            P("col"),
            P(None, ("dp", "row", "col")),
        ),
        out_specs=(
            P(None, ("dp", "row", "col")),
            P(None, ("dp", "row", "col")),
            P("col", None, "row"),
            P(None, "row"),
            P("col", "row"),
            P("col"),
            P("col"),
            P("col"),
            P("col", "row"),
            P("row"),
            P("col", "row"),
            P("col"),
            P("col"),
            P("col"),
        ),
        check_vma=False,
    )
```
